512 devices in a mesh: blk: 32 (over x, z_lo), grp: 16 (over y, z_hi, core).
Axes of the slice: x: 4, y: 4, z: 16 (z_hi: 2, z_lo: 8; z = z_hi * 8 + z_lo), core: 2. Of those that a mesh axis runs over, the one named last changes fastest.
Arguments:
- fluid_vel: float32 [3, 1024, 16, 256], P(None, ('blk', 'grp')), may hold values from -6 to 6
- pressure: float32 [1024, 16, 256], P(('blk', 'grp')), may hold values from -6 to 6
- parcel_vel: float32 [3, 4194304], P(None, ('blk', 'grp')), may hold values from -6 to 6
- parcel_vol: float32 [4194304], P(('blk', 'grp')), may hold values from 0.02 to 0.2
- parcel_rate: float32 [4194304], P(('blk', 'grp')), may hold values from 0.2 to 5
- cell_local: int32 [4194304], P(('blk', 'grp')), may hold values from 0 to 2047
- tile_block: int32 [16384], P(('blk', 'grp')), may hold values from 0 to 63
- parcel_count: int32 [512], P(('blk', 'grp')), may hold values from 2048 to 8192, as said below
- leave_lists: int32 [2, 131072], P(None, ('blk', 'grp')), may hold values from 0 to 8191, as said below
- mig_counts: int32 [2, 512], P(None, ('blk', 'grp')), may hold values from 1 to 256, as said below
Outputs:
- fluid_next: float32 [3, 1024, 16, 256], P(None, ('blk', 'grp'))
- pressure_next: float32 [1024, 16, 256], P(('blk', 'grp'))
- parcel_next: float32 [3, 4194304], P(None, ('blk', 'grp'))
- arrivals: float32 [2, 5, 131072], P(None, None, ('blk', 'grp'))
The draws below stay inside these ranges and needn't reach their ends.
Inputs may be any that keep to these rules, and one draw needn't show every extreme that they name: `parcel_count`: one device, drawn from the seed, holds 8192 live parcels. `leave_lists`: every listed slot is live on its device, and the 512 slots of one device are distinct; entries past the count are ignored. `mig_counts`: in each list, some device drawn from the seed uses all 256 entries.
All inputs are finite; a program needn't handle non-finite values.
Results may differ from the reference program's by a relative error of at most 0.0013.
Values may be sent and summed in bfloat16 or wider, within the bound.
No kernel may reach another device: no remote copies, remote signals or barrier semaphores. Data moves between devices by JAX's collectives and lax.ppermute only.
A program may use at most 64 MiB of HBM per device.

```python
import math
import jax
import jax.numpy as jnp
from jax import lax

PCAP = 8192
TP = 256
BLOCK = 2048
RADIAL = 16
LINE = 256
SWEEPS = 2
MIG = 256
SLAB_PLANES = 32
NBLOCKS = 64
PLANES = 1024
PARCELS = 4194304
TILES_ALL = 16384
N_BLK = 32
N_GRP = 16
DEVICES = 512


def shared_counts(key):
    low_counts = jax.random.randint(jax.random.fold_in(key, 11), (DEVICES,), PCAP // 4, PCAP + 1)
    full_device = jax.random.randint(jax.random.fold_in(key, 12), (), 0, DEVICES)
    return jnp.where(jnp.arange(DEVICES) == full_device, PCAP, low_counts).astype(jnp.int32)


def draw_parcel_count(key, part):
    counts = shared_counts(key)
    return counts


def draw_leave_lists(key, part):
    counts = shared_counts(key)
    key = jax.random.fold_in(key, 2)
    device_keys = jax.random.split(key, DEVICES)

    def one_device(device_key, count):
        order = jax.random.permutation(device_key, PCAP).astype(jnp.int32)
        scores = (order >= count).astype(jnp.int32) * PCAP + jnp.arange(PCAP, dtype=jnp.int32)
        picked = jnp.argsort(scores)
        return order[picked[:2 * MIG]]
    chosen = jax.vmap(one_device)(device_keys, counts)
    return chosen.reshape(DEVICES, 2, MIG).transpose(1, 0, 2).reshape(2, DEVICES * MIG).astype(jnp.int32)


def draw_mig_counts(key, part):
    key = jax.random.fold_in(key, 3)
    drawn = jax.random.randint(jax.random.fold_in(key, 1), (2, DEVICES), 1, MIG + 1)
    full_device = jax.random.randint(jax.random.fold_in(key, 2), (2,), 0, DEVICES)
    return jnp.where(jnp.arange(DEVICES)[None, :] == full_device[:, None], MIG, drawn).astype(jnp.int32)


def plant(array, key, low, high):
    extent = array.shape
    spot = [jax.random.randint(jax.random.fold_in(key, axis), (), 0, extent[axis]) for axis in range(len(extent))]
    array = array.at[tuple(spot)].set(low)
    longest = extent.index(max(extent))
    spot[longest] = (spot[longest] + 1) % extent[longest]
    return array.at[tuple(spot)].set(high)


def steps_of(rng, shape, shards, least, top_value):
    loudness, own = 1.0, jax.random.fold_in(rng, 6)
    for position, blocks in shards:
        steps = jnp.exp(jax.random.uniform(jax.random.fold_in(own, position), (blocks,), jnp.float32, least / len(shards), top_value / len(shards)))
        loudness = loudness * jnp.repeat(steps, shape[position] // blocks).reshape([-1 if axis == position else 1 for axis in range(len(shape))])
    return loudness


def bell_draw(key, extent, deviation, most, cuts=(), held_as=jnp.bfloat16):
    values = jax.random.normal(key, extent, jnp.float32) * deviation
    if len(cuts) > 0:
        values = steps_of(key, extent, cuts, -0.22, 0.18) * values
    return jnp.clip(values, min=-most, max=most).astype(held_as)


def setup_inputs(seed: int = 0) -> dict:
    splits = jax.random.split(jax.random.key(seed), 11)
    fluid_vel = bell_draw(splits[0], (3, PLANES, RADIAL, LINE), 1.0, 6.0, ((1, 512),), jnp.float32)
    pressure = bell_draw(splits[1], (PLANES, RADIAL, LINE), 1.0, 6.0, ((0, 512),), jnp.float32)
    parcel_vel = bell_draw(splits[2], (3, PARCELS), 1.0, 6.0, ((1, 512),), jnp.float32)
    parcel_vol = jnp.clip(jnp.exp(math.log(0.2) - 2.3025851 * jax.random.uniform(splits[3], (PARCELS,), jnp.float32) ** steps_of(splits[3], (PARCELS,), ((0, 512),), -0.2, 0.2)), 0.02, 0.2)
    parcel_rate = jnp.clip(jnp.exp(math.log(5.0) - 3.218876 * jax.random.uniform(splits[4], (PARCELS,), jnp.float32) ** steps_of(splits[4], (PARCELS,), ((0, 512),), -0.2, 0.2)), 0.2, 5.0)
    cell_local = plant(jax.random.randint(splits[5], (PARCELS,), 0, BLOCK), jax.random.fold_in(splits[5], 1), 0, BLOCK - 1).astype(jnp.int32)
    tile_block = plant(jax.random.randint(splits[6], (TILES_ALL,), 0, NBLOCKS), jax.random.fold_in(splits[6], 1), 0, NBLOCKS - 1).astype(jnp.int32)
    parcel_count = draw_parcel_count(jax.random.fold_in(splits[10], 71), 0)
    leave_lists = draw_leave_lists(jax.random.fold_in(splits[10], 71), 0)
    mig_counts = draw_mig_counts(jax.random.fold_in(splits[10], 71), 0)
    return {"fluid_vel": fluid_vel, "pressure": pressure, "parcel_vel": parcel_vel, "parcel_vol": parcel_vol, "parcel_rate": parcel_rate, "cell_local": cell_local, "tile_block": tile_block, "parcel_count": parcel_count, "leave_lists": leave_lists, "mig_counts": mig_counts}


DT = 0.2
NU = 0.5


def rad_up(values):
    return jnp.concatenate([values[..., 1:, :], jnp.zeros_like(values[..., :1, :])], axis=-2)


def rad_down(values):
    return jnp.concatenate([jnp.zeros_like(values[..., :1, :]), values[..., :-1, :]], axis=-2)


def axial_up(values):
    return jnp.concatenate([values[..., 1:], jnp.zeros_like(values[..., :1])], axis=-1)


def axial_down(values):
    return jnp.concatenate([jnp.zeros_like(values[..., :1]), values[..., :-1]], axis=-1)


def laplace(extended):
    center = extended[..., 1:-1, :, :]
    return (extended[..., 2:, :, :] + extended[..., :-2, :, :] + rad_up(center) + rad_down(center)
            + axial_up(center) + axial_down(center) - 6.0 * center)


def gradient(extended):
    center = extended[..., 1:-1, :, :]
    return jnp.stack([0.5 * (extended[..., 2:, :, :] - extended[..., :-2, :, :]),
                      0.5 * (rad_up(center) - rad_down(center)),
                      0.5 * (axial_up(center) - axial_down(center))])


def divergence(extended):
    center = extended[:, 1:-1]
    return 0.5 * (extended[0, 2:] - extended[0, :-2] + rad_up(center[1]) - rad_down(center[1])
                  + axial_up(center[2]) - axial_down(center[2]))


def jacobi(extended, source):
    center = extended[1:-1]
    return (extended[2:] + extended[:-2] + rad_up(center) + rad_down(center)
            + axial_up(center) + axial_down(center) - source / DT) / 6.0


def predict(extended, deposits):
    porosity = 1.0 / (1.0 + deposits[0])
    velocity = extended[:3, 1:-1]
    momentum_rhs = NU * laplace(extended[:3]) - gradient(extended[3])
    u_star = (velocity + DT * momentum_rhs + DT * deposits[2:5] / porosity) / (1.0 + DT * deposits[1] / porosity)
    return u_star, porosity


def cycle_ext(values, width):
    return jnp.concatenate([values[..., -width:, :, :], values, values[..., :width, :, :]], axis=-3)


def reference(fluid_vel, pressure, parcel_vel, parcel_vol, parcel_rate, cell_local, tile_block, parcel_count, leave_lists, mig_counts):
    slab_cells = SLAB_PLANES * RADIAL * LINE
    slot_ids = jnp.arange(PCAP, dtype=jnp.int32)
    active = (slot_ids[None, :] < parcel_count[:, None]).astype(jnp.float32)
    blocks = jnp.repeat(tile_block.reshape(DEVICES, PCAP // TP), TP, axis=1)
    slab_index = (jnp.arange(DEVICES, dtype=jnp.int32) // N_GRP)[:, None]
    cell_ids = (slab_index * slab_cells + blocks * BLOCK + cell_local.reshape(DEVICES, PCAP)).reshape(-1).astype(jnp.int32)
    volume = parcel_vol.reshape(DEVICES, PCAP)
    drag_rate = parcel_rate.reshape(DEVICES, PCAP)
    velocity = parcel_vel.reshape(3, DEVICES, PCAP)
    drag_coeff = volume * drag_rate
    quantity = jnp.concatenate([volume[None], drag_coeff[None], drag_coeff[None] * velocity]) * active[None]
    quantity = lax.optimization_barrier(quantity.astype(jnp.bfloat16)).astype(jnp.float32)
    total_cells = PLANES * RADIAL * LINE

    def cell_sum(column):
        return jax.ops.segment_sum(column, cell_ids, num_segments=total_cells)

    deposits = jax.vmap(cell_sum)(quantity.reshape(5, -1)).reshape(5, PLANES, RADIAL, LINE)
    extended = cycle_ext(jnp.concatenate([fluid_vel, pressure[None]]), 1)
    u_star, porosity = predict(extended, deposits)
    eps_flux = porosity * u_star
    source = divergence(cycle_ext(eps_flux, 1))
    pressure_now = pressure
    for sweep_index in range(SWEEPS):
        pressure_now = jacobi(cycle_ext(pressure_now, 1), source)
    fluid_new = u_star - DT * gradient(cycle_ext(pressure_now, 1))
    line_fields = lax.optimization_barrier(jnp.concatenate([fluid_new, porosity[None]]).astype(jnp.bfloat16))
    line_fields = line_fields.astype(jnp.float32).reshape(4, -1)
    sampled = line_fields[:, cell_ids].reshape(4, DEVICES, PCAP)
    coupling = drag_rate / (sampled[3] * sampled[3])
    moved_vel = (velocity + DT * coupling[None] * sampled[:3]) / (1.0 + DT * coupling[None])
    parcel_state = jnp.concatenate([moved_vel, volume[None], drag_rate[None]]) * active[None]
    leave_ids = leave_lists.reshape(2, DEVICES, MIG)
    list_valid = (jnp.arange(MIG, dtype=jnp.int32)[None, None, :] < mig_counts[:, :, None]).astype(jnp.float32)
    outgoing = jnp.stack([jnp.take_along_axis(parcel_state, jnp.broadcast_to(leave_ids[which][None], (5, DEVICES, MIG)), axis=2)
                          for which in range(2)]) * list_valid[:, None]
    row_ids = jnp.broadcast_to(jnp.arange(DEVICES, dtype=jnp.int32)[None, :, None], leave_ids.shape)
    leaving = jnp.zeros((DEVICES, PCAP), jnp.float32).at[row_ids, leave_ids].max(list_valid)
    parcel_next = (moved_vel * active[None] * (1.0 - leaving)[None]).reshape(3, DEVICES * PCAP)
    outgoing = outgoing.reshape(2, 5, N_BLK, N_GRP, MIG)
    from_above = jnp.roll(outgoing[0], -1, axis=1)
    from_below = jnp.roll(outgoing[1], 1, axis=1)
    arrivals = jnp.stack([from_above, from_below]).reshape(2, 5, DEVICES * MIG)
    return fluid_new, pressure_now, parcel_next, arrivals
```

```python
import jax
import jax.numpy as jnp
from jax import lax
from jax.experimental import pallas as pl
from jax.experimental.pallas import tpu as pltpu
from jax.sharding import Mesh, PartitionSpec as P

PCAP = 8192
TP = 256
TILES = PCAP // TP
ROWS = PCAP // 128
BLOCK = 2048
RADIAL = 16
LINE = 256
MIG = 256
N_BLK, N_Y, N_Z, N_C = 32, 4, 2, 2
Z_LO = 8
ALL = ("blk", "y", "z", "c")

DT = 0.2
NU = 0.5

PAY_ROWS = 6 * ROWS + 16
SCR_ROWS = 7 * ROWS
SOURCES = N_Y * N_Z * N_C
OWN_BLOCKS = 8
UNROLL = 4
LIST_CAP = SOURCES * TILES + UNROLL

F32 = jnp.float32
BF16 = jnp.bfloat16
I32 = jnp.int32


def flat(blk, y, z, c):
    return ((blk * N_Y + y) * N_Z + z) * N_C + c


def every_place():
    for blk in range(N_BLK):
        for y in range(N_Y):
            for z in range(N_Z):
                for c in range(N_C):
                    yield blk, y, z, c


def halo_route():
    pairs = []
    for blk, y, z, c in every_place():
        if c == 1:
            here = flat(blk, y, z, 1)
            if y < N_Y - 1:
                there = flat(blk, y + 1, z, 0)
            else:
                crossing = blk % Z_LO == Z_LO - 1
                there = flat((blk + 1) % N_BLK, 0, 1 - z if crossing else z, 0)
            pairs += [(here, there), (there, here)]
    return pairs


def leave_route(step):
    edge = 0 if step < 0 else Z_LO - 1
    pairs = []
    for blk, y, z, c in every_place():
        sender = flat(blk, y, 1 - z if blk % Z_LO == edge else z, c)
        pairs.append((sender, flat((blk + step) % N_BLK, y, z, c)))
    return pairs


def swap(values, axis):
    return lax.ppermute(values, axis, [(0, 1), (1, 0)])


def call(kernel, outs, ins, scratch=(), smem=(), limit=16 << 20):
    specs = [
        pl.BlockSpec(memory_space=pltpu.SMEM if i in smem else pltpu.VMEM) for i in range(len(ins))
    ]
    return pl.pallas_call(
        kernel,
        out_shape=[jax.ShapeDtypeStruct(shape, dtype) for shape, dtype in outs],
        in_specs=specs,
        out_specs=[pl.BlockSpec(memory_space=pltpu.VMEM) for _ in outs],
        scratch_shapes=list(scratch),
        compiler_params=pltpu.CompilerParams(vmem_limit_bytes=limit),
    )(*ins)


def rows_iota(rows, lanes):
    return lax.broadcasted_iota(I32, (rows, lanes), 0)


def dot_nt(a, b):
    return lax.dot_general(a, b, (((1,), (1,)), ((), ())), preferred_element_type=F32)


def dot_nn(a, b):
    return lax.dot_general(a, b, (((1,), (0,)), ((), ())), preferred_element_type=F32)


def hi_of(cell):
    return ((cell >> 7) & 1) * 8 + (cell >> 8)


def pack_kernel(
    vel, vol, rate, cell, tiles, count, lists, mig, fluid, press, pay, fpay, keep, vsc, tsc
):
    for r in range(ROWS):
        for k in range(3):
            vsc[k, r : r + 1, :] = vel[k : k + 1, r * 128 : (r + 1) * 128]
    slot = rows_iota(ROWS, 128) * 128 + lax.broadcasted_iota(I32, (ROWS, 128), 1)
    active = (slot < count[0]).astype(F32)
    drag = vol[...] * rate[...]
    pay[0:ROWS, :] = (vol[...] * active).astype(BF16)
    pay[ROWS : 2 * ROWS, :] = (drag * active).astype(BF16)
    for k in range(3):
        pay[(2 + k) * ROWS : (3 + k) * ROWS, :] = (drag * vsc[k] * active).astype(BF16)
    cells = cell[...]
    hi = hi_of(cells)
    code = ((cells & 127) + 128).astype(F32)
    for bit in range(4):
        code = code * jnp.where((hi >> bit) & 1 == 1, F32(2.0 ** (1 << bit)), F32(1.0))
    pay[5 * ROWS : 6 * ROWS, :] = code.astype(BF16)
    lane = lax.broadcasted_iota(I32, (1, TILES), 1)
    tsc[...] = jnp.zeros((16, 128), F32)
    tsc[0:1, 0:TILES] = tiles[...].astype(F32)
    raw_tiles = tsc[...].astype(BF16)
    tsc[0:1, 0:TILES] = jnp.where(lane * TP < count[0], tiles[...].astype(F32), 255.0)
    pay[6 * ROWS : 6 * ROWS + 16, :] = tsc[...].astype(BF16)
    for k in range(3):
        fpay[2 * k : 2 * k + 2] = fluid[k]
    fpay[6:8] = press[...]
    slots = jnp.concatenate([lists[0:1, :], lists[1:2, :]], axis=1)
    lane512 = lax.broadcasted_iota(I32, (1, 2 * MIG), 1)
    ends = jnp.where(lane512 < MIG, mig[0, 0], mig[1, 0] + MIG)
    valid = jnp.where(lane512 < ends, F32(1.0), F32(0.0))
    low = (rows_iota(128, 2 * MIG) == (slots & 127)).astype(F32).astype(BF16)
    row_mask = rows_iota(ROWS, 2 * MIG) == (slots >> 7)
    counts = dot_nt(jnp.where(row_mask, valid, 0.0).astype(BF16), low)
    keep[...] = active * jnp.where(counts > 0.5, 0.0, 1.0)

    def picked(values, parts):
        total = None
        for _ in range(parts):
            piece = values.astype(BF16)
            values = values - piece.astype(F32)
            term = dot_nn(piece, low)
            total = term if total is None else total + term
        return jnp.sum(jnp.where(row_mask, total, 0.0), axis=0, keepdims=True)

    def put(row, values):
        fpay[8, row : row + 1, :] = values[:, :MIG]
        fpay[8, 8 + row : 9 + row, :] = values[:, MIG:]

    for k in range(3):
        put(k, picked(vsc[k], 3))
    put(3, picked(vol[...], 3))
    put(4, picked(rate[...], 3))
    tile_hot = (rows_iota(128, 2 * MIG) == (slots >> 8)).astype(F32).astype(BF16)
    block = dot_nn(raw_tiles, tile_hot)[0:1, :]
    cell_hi = picked((cells >> 7).astype(F32), 1)
    cell_lo = picked((cells & 127).astype(F32), 1)
    put(5, block * BLOCK + cell_hi * 128.0 + cell_lo)
    put(6, valid)
    put(7, jnp.zeros_like(valid))


def planes_kernel(own, far, side, side_far, planes, send):
    z = lax.axis_index("z")
    c = lax.axis_index("c")
    for k in range(4):
        for i in range(2):
            planes[k, z * 4 + c * 2 + i] = own[2 * k + i]
            planes[k, (1 - z) * 4 + c * 2 + i] = far[2 * k + i]
            planes[k, z * 4 + (1 - c) * 2 + i] = side[2 * k + i]
            planes[k, (1 - z) * 4 + (1 - c) * 2 + i] = side_far[2 * k + i]
    for k in range(3):
        send[k] = planes[k, 7 * c]
        send[3 + k] = planes[3, 5 * c + k]


def at(values, axis, step):
    size = values.shape[axis]
    moved = pltpu.roll(values, (-step) % size, axis)
    place = lax.broadcasted_iota(I32, values.shape, axis)
    return jnp.where(place == (size - 1 if step > 0 else 0), 0.0, moved)


def rad_up(values):
    return at(values, values.ndim - 2, 1)


def rad_down(values):
    return at(values, values.ndim - 2, -1)


def axial_up(values):
    return at(values, values.ndim - 1, 1)


def axial_down(values):
    return at(values, values.ndim - 1, -1)


def deposit_kernel(
    pays, planes, halo, u_out, por_out, flux_y, flux_c, scr, acc, tile_v, tile_s, picks, wide, flux, sem
):
    y = lax.axis_index("y")
    c = lax.axis_index("c")
    first = y * 16 + c * OWN_BLOCKS
    for s in range(SOURCES):
        tile_v[s : s + 1, :] = pays[s, 6 * ROWS : 6 * ROWS + 16, :].astype(F32)[0:1, :].astype(I32)
    copy = pltpu.make_async_copy(tile_v, tile_s, sem)
    copy.start()

    def widen(s, carry):
        base = pl.multiple_of(s * SCR_ROWS, 8)
        scr[pl.ds(base, 5 * ROWS), :] = pays[s, 0 : 5 * ROWS, :].astype(F32)
        code = pays[s, 5 * ROWS : 6 * ROWS, :].astype(F32)
        hi = jnp.zeros_like(code)
        for step in (8, 4, 2, 1):
            large = code >= 2.0 ** (7 + step)
            code = jnp.where(large, code * 2.0**-step, code)
            hi = hi + jnp.where(large, F32(step), 0.0)
        scr[pl.ds(base + 5 * ROWS, ROWS), :] = hi
        scr[pl.ds(base + 6 * ROWS, ROWS), :] = code - 128.0
        return carry

    lax.fori_loop(0, SOURCES, widen, 0)
    acc[...] = jnp.zeros_like(acc)
    copy.wait()

    def choose(s, found):
        for t in range(TILES):
            block = tile_s[s, t] - first
            picks[found] = (s * SCR_ROWS + 2 * t) * 16 + block
            mine = jnp.logical_and(block >= 0, block < OWN_BLOCKS)
            found = found + mine.astype(I32)
        return found

    found = lax.fori_loop(0, SOURCES, choose, jnp.int32(0))
    for i in range(UNROLL):
        picks[found + i] = OWN_BLOCKS
    iota16 = lax.broadcasted_iota(I32, (16, 128), 0).astype(F32)
    iota128 = lax.broadcasted_iota(I32, (128, 128), 0).astype(F32)

    def one_tile(code):
        block = code & 15
        base = code >> 4
        left, right = [], []
        for h in range(2):
            hi = scr[pl.ds(base + 5 * ROWS + h, 1), :]
            lo = scr[pl.ds(base + 6 * ROWS + h, 1), :]
            mask = iota16 == hi
            parts = [
                jnp.where(mask, scr[pl.ds(base + k * ROWS + h, 1), :], 0.0).astype(BF16)
                for k in range(5)
            ]
            left.append(jnp.concatenate(parts, axis=0))
            right.append(jnp.where(iota128 == lo, F32(1.0), F32(0.0)).astype(BF16))
        sums = dot_nt(jnp.concatenate(left, axis=1), jnp.concatenate(right, axis=1))
        return block, sums

    def deposit(i, carry):
        done = [one_tile(picks[i * UNROLL + u]) for u in range(UNROLL)]
        for block, sums in done:
            acc[block] = acc[block] + sums
        return carry

    lax.fori_loop(0, (found + UNROLL - 1) // UNROLL, deposit, 0)

    def amount(k):
        halves = []
        for b in range(OWN_BLOCKS):
            halves.append(
                jnp.concatenate([acc[b, k * 16 : k * 16 + 8, :], acc[b, k * 16 + 8 : k * 16 + 16, :]], axis=1)
            )
        return jnp.stack(
            [jnp.concatenate([halves[2 * i], halves[2 * i + 1]], axis=0) for i in range(4)]
        )

    for k in range(4):
        wide[k, 1:5] = planes[k, pl.ds(c * 4, 4)]
        wide[k, 5 * (1 - c)] = planes[k, 4 - c]
        if k < 3:
            wide[k, 5 * c] = halo[k]
    wide[3, 5 * c] = halo[3 + 2 * (1 - c)]
    porosity = 1.0 / (1.0 + amount(0))
    por_out[...] = porosity
    below = 1.0 + DT * amount(1) / porosity
    centre = wide[3, 1:5]
    slopes = [
        0.5 * (wide[3, 2:6] - wide[3, 0:4]),
        0.5 * (rad_up(centre) - rad_down(centre)),
        0.5 * (axial_up(centre) - axial_down(centre)),
    ]
    for k in range(3):
        v = wide[k, 1:5]
        lap = (
            wide[k, 2:6] + wide[k, 0:4] + rad_up(v) + rad_down(v) + axial_up(v) + axial_down(v) - 6.0 * v
        )
        u = (v + DT * (NU * lap - slopes[k]) + DT * amount(2 + k) / porosity) / below
        u_out[k] = u
        flux[k] = porosity * u
    for k in range(3):
        for i in range(3):
            flux_y[3 * k + i] = flux[k, c + i]
            flux_c[3 * k + i] = flux[k, 1 - c + i]


def fluid_kernel(u_in, por_in, planes, halo, from_y, from_c, fields, kept, sent, flux, pres, out):
    c = lax.axis_index("c")
    for k in range(3):
        flux[k, 3:7] = por_in[...] * u_in[k]
        for i in range(3):
            flux[k, 7 * c + i] = from_y[3 * k + i]
            flux[k, 7 * (1 - c) + i] = from_c[3 * k + i]
    for i in range(3):
        pres[7 * c + i] = halo[3 + i]
    for j in range(7):
        pres[3 * (1 - c) + j] = planes[3, c + j]
    f1 = flux[1, 1:9]
    f2 = flux[2, 1:9]
    source = 0.5 * (
        flux[0, 2:10] - flux[0, 0:8] + rad_up(f1) - rad_down(f1) + axial_up(f2) - axial_down(f2)
    )

    def sweep(p, s):
        centre = p[1:-1]
        return (
            p[2:]
            + p[:-2]
            + rad_up(centre)
            + rad_down(centre)
            + axial_up(centre)
            + axial_down(centre)
            - s / DT
        ) / 6.0

    p1 = sweep(pres[...], source)
    p2 = sweep(p1, source[1:-1])
    centre = p2[1:-1]
    slopes = [
        0.5 * (p2[2:] - p2[:-2]),
        0.5 * (rad_up(centre) - rad_down(centre)),
        0.5 * (axial_up(centre) - axial_down(centre)),
    ]
    for k in range(3):
        out[k] = u_in[k] - DT * slopes[k]
    out[3] = centre
    for k in range(4):
        for i in range(4):
            plane = out[k, i] if k < 3 else por_in[i]
            for h in range(2):
                half = plane[8 * h : 8 * h + 8]
                both = jnp.concatenate([half[:, :128], half[:, 128:]], axis=0)
                fields[2 * i + h, 16 * k : 16 * k + 16, :] = both.astype(BF16)
    for k in range(4):
        for i in range(2):
            kept[k, i] = out[k, 2 * c + i]
            sent[k, i] = out[k, 2 * (1 - c) + i]


def step_parcel(vel, rate, sampled):
    coupling = rate / (sampled[3] * sampled[3])
    pull = DT * coupling
    below = 1.0 + pull
    return [(vel[k] + pull * sampled[k]) / below for k in range(3)]


def leave_kernel(fields, own, far, out0, out1):
    z_lo = lax.rem(lax.axis_index("blk"), Z_LO)
    list0 = jnp.where(z_lo == 0, far[8, 0:8, :], own[8, 0:8, :])
    list1 = jnp.where(z_lo == Z_LO - 1, far[8, 8:16, :], own[8, 8:16, :])
    both = jnp.concatenate([list0, list1], axis=1)
    place = both[5:6, :].astype(I32)
    block = place >> 11
    hi = hi_of(place & (BLOCK - 1))
    low = (rows_iota(128, 2 * MIG) == (place & 127)).astype(F32).astype(BF16)
    mask = rows_iota(16, 2 * MIG) == hi

    def gather(i, total):
        for u in range(8):
            picked = dot_nn(fields[i // 4, i % 4, u], low)
            wanted = (i % 4) * 16 + (i // 4) * OWN_BLOCKS + u
            total = total + jnp.where(block == wanted, picked, 0.0)
        return total

    total = lax.fori_loop(0, 8, gather, jnp.zeros((64, 2 * MIG), F32))
    sampled = [
        jnp.sum(jnp.where(mask, total[16 * k : 16 * k + 16], 0.0), axis=0, keepdims=True)
        for k in range(4)
    ]
    sampled[3] = jnp.where(both[6:7, :] > 0.5, sampled[3], 1.0)
    vol, rate, valid = both[3:4, :], both[4:5, :], both[6:7, :]
    moved = step_parcel([both[k : k + 1, :] for k in range(3)], rate, sampled)
    for k, values in enumerate(moved + [vol, rate]):
        values = values * valid
        out0[k : k + 1, :] = values[:, :MIG]
        out1[k : k + 1, :] = values[:, MIG:]


def move_kernel(fields, tiles, cell, keep, vel, rate, out):
    iota16 = rows_iota(16, TP)
    iota128 = rows_iota(128, TP)

    def pair(ref, t):
        return jnp.concatenate([ref[pl.ds(2 * t, 1), :], ref[pl.ds(2 * t + 1, 1), :]], axis=1)

    def one_tile(t):
        block = tiles[t]
        here = fields[(block >> 3) & 1, block >> 4, block & 7]
        cells = pair(cell, t)
        low = jnp.where(iota128 == (cells & 127), F32(1.0), F32(0.0)).astype(BF16)
        picked = dot_nn(here, low)
        mask = iota16 == hi_of(cells)
        sampled = [
            jnp.sum(jnp.where(mask, picked[16 * k : 16 * k + 16], 0.0), axis=0, keepdims=True)
            for k in range(4)
        ]
        lanes = pl.ds(pl.multiple_of(t * TP, TP), TP)
        moved = step_parcel([vel[k : k + 1, lanes] for k in range(3)], pair(rate, t), sampled)
        stays = pair(keep, t)
        for k in range(3):
            out[k : k + 1, lanes] = moved[k] * stays

    def some(i, carry):
        for u in range(4):
            one_tile(i * 4 + u)
        return carry

    lax.fori_loop(0, TILES // 4, some, 0)


def over_y(values):
    copies = jnp.broadcast_to(values[None], (N_Y,) + values.shape)
    return lax.all_to_all(copies, "y", 0, 0, tiled=False)


def per_device(
    fluid_vel,
    pressure,
    parcel_vel,
    parcel_vol,
    parcel_rate,
    cell_local,
    tile_block,
    parcel_count,
    leave_lists,
    mig_counts,
):
    vol = parcel_vol.reshape(ROWS, 128)
    rate = parcel_rate.reshape(ROWS, 128)
    cell = cell_local.reshape(ROWS, 128)
    tiles = tile_block.reshape(1, TILES)
    pay, fpay, keep = call(
        pack_kernel,
        [((PAY_ROWS, 128), BF16), ((9, RADIAL, LINE), F32), ((ROWS, 128), F32)],
        [parcel_vel, vol, rate, cell, tiles, parcel_count, leave_lists, mig_counts, fluid_vel, pressure],
        scratch=[pltpu.VMEM((3, ROWS, 128), F32), pltpu.VMEM((16, 128), F32)],
        smem=(5, 7),
    )
    fpay_far = swap(fpay, "z")
    pay_far = swap(pay, "z")
    fpay_side = swap(fpay, "c")
    fpay_side_far = swap(fpay_far, "c")
    planes, send = call(
        planes_kernel,
        [((4, 8, RADIAL, LINE), F32), ((6, RADIAL, LINE), F32)],
        [fpay, fpay_far, fpay_side, fpay_side_far],
    )
    route = halo_route()
    halo = lax.ppermute(send, ALL, route)
    pays = over_y(jnp.concatenate([pay, pay_far]))
    pays = lax.all_gather(pays, "c", axis=0).reshape(SOURCES, PAY_ROWS, 128)
    u_star, porosity, flux_y, flux_c = call(
        deposit_kernel,
        [
            ((3, 4, RADIAL, LINE), F32),
            ((4, RADIAL, LINE), F32),
            ((9, RADIAL, LINE), F32),
            ((9, RADIAL, LINE), F32),
        ],
        [pays, planes, halo],
        scratch=[
            pltpu.VMEM((SOURCES * SCR_ROWS, 128), F32),
            pltpu.VMEM((OWN_BLOCKS + 1, 80, 128), F32),
            pltpu.VMEM((SOURCES, 128), I32),
            pltpu.SMEM((SOURCES, 128), I32),
            pltpu.SMEM((LIST_CAP,), I32),
            pltpu.VMEM((4, 6, RADIAL, LINE), F32),
            pltpu.VMEM((3, 4, RADIAL, LINE), F32),
            pltpu.SemaphoreType.DMA,
        ],
    )
    from_y = lax.ppermute(flux_y, ALL, route)
    from_c = swap(flux_c, "c")
    fields, kept, sent = call(
        fluid_kernel,
        [
            ((OWN_BLOCKS, 64, 128), BF16),
            ((4, 2, RADIAL, LINE), F32),
            ((4, 2, RADIAL, LINE), F32),
        ],
        [u_star, porosity, planes, halo, from_y, from_c],
        scratch=[
            pltpu.VMEM((3, 10, RADIAL, LINE), F32),
            pltpu.VMEM((10, RADIAL, LINE), F32),
            pltpu.VMEM((4, 4, RADIAL, LINE), F32),
        ],
    )
    fields = lax.all_gather(over_y(fields), "c", axis=0)
    swapped = swap(sent, "c")
    mine = lax.axis_index("c") == lax.axis_index("z")
    out0, out1 = call(
        leave_kernel, [((5, MIG), F32), ((5, MIG), F32)], [fields, fpay, fpay_far]
    )
    arrive0 = lax.ppermute(out0, ALL, leave_route(-1))
    arrive1 = lax.ppermute(out1, ALL, leave_route(1))
    (parcel_next,) = call(
        move_kernel,
        [((3, PCAP), F32)],
        [fields, tile_block, cell, keep, parcel_vel, rate],
        smem=(1,),
    )
    fluid_next = jnp.where(mine, kept[:3], swapped[:3])
    pressure_next = jnp.where(mine, kept[3], swapped[3])
    return fluid_next, pressure_next, parcel_next, jnp.stack([arrive0, arrive1])


def solution(mesh):
    fine = Mesh(mesh.devices.reshape(N_BLK, N_Y, N_Z, N_C), ALL)
    placed = (
        P(None, ALL, None, None),
        P(ALL, None, None),
        P(None, ALL),
        P(ALL),
        P(ALL),
        P(ALL),
        P(ALL),
        P(ALL),
        P(None, ALL),
        P(None, ALL),
    )
    return jax.shard_map(
        per_device,
        mesh=fine,
        in_specs=placed,
        out_specs=(
            P(None, ALL, None, None),
            P(ALL, None, None),
            P(None, ALL),
            P(None, None, ALL),
        ),
        check_vma=False,
    )
```

```python
import jax
import jax.numpy as jnp
from jax import lax
from jax.experimental import pallas as pl
from jax.experimental.pallas import tpu as pltpu
from jax.sharding import Mesh, PartitionSpec as P

PCAP = 8192
TP = 256
TILES = PCAP // TP
ROWS = PCAP // 128
BLOCK = 2048
RADIAL = 16
LINE = 256
MIG = 256
N_BLK, N_Y, N_Z, N_C = 32, 4, 2, 2
Z_LO = 8
ALL = ("blk", "y", "z", "c")

DT = 0.2
NU = 0.5

PAY_ROWS = 6 * ROWS + 16
SCR_ROWS = 7 * ROWS
SOURCES = N_Y * N_Z
OWN_BLOCKS = 8
UNROLL = 4
LIST_CAP = SOURCES * TILES + UNROLL

PACK_LIMIT = 56 << 20

F32 = jnp.float32
BF16 = jnp.bfloat16
I32 = jnp.int32


def flat(blk, y, z, c):
    return ((blk * N_Y + y) * N_Z + z) * N_C + c


def every_place():
    for blk in range(N_BLK):
        for y in range(N_Y):
            for z in range(N_Z):
                for c in range(N_C):
                    yield blk, y, z, c


def halo_route():
    pairs = []
    for blk, y, z, c in every_place():
        if c == 1:
            here = flat(blk, y, z, 1)
            if y < N_Y - 1:
                there = flat(blk, y + 1, z, 0)
            else:
                crossing = blk % Z_LO == Z_LO - 1
                there = flat((blk + 1) % N_BLK, 0, 1 - z if crossing else z, 0)
            pairs += [(here, there), (there, here)]
    return pairs


def leave_route(step):
    edge = 0 if step < 0 else Z_LO - 1
    pairs = []
    for blk, y, z, c in every_place():
        sender = flat(blk, y, 1 - z if blk % Z_LO == edge else z, c)
        pairs.append((sender, flat((blk + step) % N_BLK, y, z, c)))
    return pairs


def swap(values, axis):
    return lax.ppermute(values, axis, [(0, 1), (1, 0)])


def call(kernel, outs, ins, scratch=(), smem=(), hbm=(), limit=16 << 20, flops=0):
    def space(i):
        return pltpu.SMEM if i in smem else pltpu.HBM if i in hbm else pltpu.VMEM

    specs = [pl.BlockSpec(memory_space=space(i)) for i in range(len(ins))]
    return pl.pallas_call(
        kernel,
        out_shape=[jax.ShapeDtypeStruct(shape, dtype) for shape, dtype in outs],
        in_specs=specs,
        out_specs=[pl.BlockSpec(memory_space=pltpu.VMEM) for _ in outs],
        scratch_shapes=list(scratch),
        compiler_params=pltpu.CompilerParams(vmem_limit_bytes=limit),
        cost_estimate=pl.CostEstimate(flops=flops, bytes_accessed=1 << 20, transcendentals=0),
    )(*ins)


def rows_iota(rows, lanes):
    return lax.broadcasted_iota(I32, (rows, lanes), 0)


def dot_nt(a, b):
    return lax.dot_general(a, b, (((1,), (1,)), ((), ())), preferred_element_type=F32)


def dot_nn(a, b):
    return lax.dot_general(a, b, (((1,), (0,)), ((), ())), preferred_element_type=F32)


def hi_of(cell):
    return ((cell >> 7) & 1) * 8 + (cell >> 8)


def pack_kernel(*refs):
    sources, (pay, fpay, keep), (vel, vol, rate, cell, tiles, count, lists, mig, vsc, tsc, sems) = (
        refs[:10],
        refs[10:13],
        refs[13:],
    )
    fluid, press = sources[8:]
    targets = [vel, vol, rate, cell, tiles, count, lists, mig]
    targets += [fpay.at[2 * k : 2 * k + 2] for k in range(3)] + [fpay.at[6:8]]
    origins = list(sources[:8]) + [fluid.at[k] for k in range(3)] + [press]
    copies = [
        pltpu.make_async_copy(origin, target, sems.at[i])
        for i, (origin, target) in enumerate(zip(origins, targets))
    ]
    for copy in copies:
        copy.start()
    for copy in copies:
        copy.wait()
    for r in range(ROWS):
        for k in range(3):
            vsc[k, r : r + 1, :] = vel[k : k + 1, r * 128 : (r + 1) * 128]
    slot = rows_iota(ROWS, 128) * 128 + lax.broadcasted_iota(I32, (ROWS, 128), 1)
    active = (slot < count[0]).astype(F32)
    drag = vol[...] * rate[...]
    pay[0:ROWS, :] = (vol[...] * active).astype(BF16)
    pay[ROWS : 2 * ROWS, :] = (drag * active).astype(BF16)
    for k in range(3):
        pay[(2 + k) * ROWS : (3 + k) * ROWS, :] = (drag * vsc[k] * active).astype(BF16)
    cells = cell[...]
    hi = hi_of(cells)
    code = ((cells & 127) + 128).astype(F32)
    for bit in range(4):
        code = code * jnp.where((hi >> bit) & 1 == 1, F32(2.0 ** (1 << bit)), F32(1.0))
    pay[5 * ROWS : 6 * ROWS, :] = code.astype(BF16)
    lane = lax.broadcasted_iota(I32, (1, TILES), 1)
    tsc[...] = jnp.zeros((16, 128), F32)
    tsc[0:1, 0:TILES] = tiles[...].astype(F32)
    raw_tiles = tsc[...].astype(BF16)
    tsc[0:1, 0:TILES] = jnp.where(lane * TP < count[0], tiles[...].astype(F32), 255.0)
    pay[6 * ROWS : 6 * ROWS + 16, :] = tsc[...].astype(BF16)
    slots = jnp.concatenate([lists[0:1, :], lists[1:2, :]], axis=1)
    lane512 = lax.broadcasted_iota(I32, (1, 2 * MIG), 1)
    ends = jnp.where(lane512 < MIG, mig[0:1, :], mig[1:2, :] + MIG)
    valid = jnp.where(lane512 < ends, F32(1.0), F32(0.0))
    low = (rows_iota(128, 2 * MIG) == (slots & 127)).astype(F32).astype(BF16)
    row_mask = rows_iota(ROWS, 2 * MIG) == (slots >> 7)
    counts = dot_nt(jnp.where(row_mask, valid, 0.0).astype(BF16), low)
    keep[...] = active * jnp.where(counts > 0.5, 0.0, 1.0)

    def picked(values, parts):
        total = None
        for _ in range(parts):
            piece = values.astype(BF16)
            values = values - piece.astype(F32)
            term = dot_nn(piece, low)
            total = term if total is None else total + term
        return jnp.sum(jnp.where(row_mask, total, 0.0), axis=0, keepdims=True)

    def put(row, values):
        fpay[8, row : row + 1, :] = values[:, :MIG]
        fpay[8, 8 + row : 9 + row, :] = values[:, MIG:]

    for k in range(3):
        put(k, picked(vsc[k], 3))
    put(3, picked(vol[...], 3))
    put(4, picked(rate[...], 3))
    tile_hot = (rows_iota(128, 2 * MIG) == (slots >> 8)).astype(F32).astype(BF16)
    block = dot_nn(raw_tiles, tile_hot)[0:1, :]
    cell_hi = picked((cells >> 7).astype(F32), 1)
    cell_lo = picked((cells & 127).astype(F32), 1)
    put(5, block * BLOCK + cell_hi * 128.0 + cell_lo)
    put(6, valid)
    put(7, jnp.zeros_like(valid))


def edge_kernel(own, far, edge, side):
    c = lax.axis_index("c")
    native = lax.axis_index("z") == c
    for k in range(4):
        edge[k] = jnp.where(native, own[2 * k + c], far[2 * k + c])
        for i in range(2):
            side[2 * k + i] = jnp.where(native, far[2 * k + i], own[2 * k + i])
    side[8] = jnp.where(native, own[7 - c], far[7 - c])


def at(values, axis, step):
    size = values.shape[axis]
    moved = pltpu.roll(values, (-step) % size, axis)
    place = lax.broadcasted_iota(I32, values.shape, axis)
    return jnp.where(place == (size - 1 if step > 0 else 0), 0.0, moved)


def rad_up(values):
    return at(values, values.ndim - 2, 1)


def rad_down(values):
    return at(values, values.ndim - 2, -1)


def axial_up(values):
    return at(values, values.ndim - 1, 1)


def axial_down(values):
    return at(values, values.ndim - 1, -1)


def add_deposits(pays, acc, scr, tile_v, tile_s, picks, sem):
    first = lax.axis_index("y") * 16 + lax.axis_index("c") * OWN_BLOCKS
    for s in range(SOURCES):
        tile_v[s : s + 1, :] = pays[s, 6 * ROWS : 6 * ROWS + 16, :].astype(F32)[0:1, :].astype(I32)
    copy = pltpu.make_async_copy(tile_v, tile_s, sem)
    copy.start()

    def widen(s, carry):
        base = pl.multiple_of(s * SCR_ROWS, 8)
        scr[pl.ds(base, 5 * ROWS), :] = pays[s, 0 : 5 * ROWS, :].astype(F32)
        code = pays[s, 5 * ROWS : 6 * ROWS, :].astype(F32)
        hi = jnp.zeros_like(code)
        for step in (8, 4, 2, 1):
            large = code >= 2.0 ** (7 + step)
            code = jnp.where(large, code * 2.0**-step, code)
            hi = hi + jnp.where(large, F32(step), 0.0)
        scr[pl.ds(base + 5 * ROWS, ROWS), :] = hi
        scr[pl.ds(base + 6 * ROWS, ROWS), :] = code - 128.0
        return carry

    lax.fori_loop(0, SOURCES, widen, 0)
    copy.wait()

    def choose(s, found):
        for t in range(TILES):
            block = tile_s[s, t] - first
            picks[found] = (s * SCR_ROWS + 2 * t) * 16 + block
            mine = jnp.logical_and(block >= 0, block < OWN_BLOCKS)
            found = found + mine.astype(I32)
        return found

    found = lax.fori_loop(0, SOURCES, choose, jnp.int32(0))
    for i in range(UNROLL):
        picks[found + i] = OWN_BLOCKS
    iota16 = lax.broadcasted_iota(I32, (16, 128), 0).astype(F32)
    iota128 = lax.broadcasted_iota(I32, (128, 128), 0).astype(F32)

    def one_tile(code):
        block = code & 15
        base = code >> 4
        left, right = [], []
        for h in range(2):
            hi = scr[pl.ds(base + 5 * ROWS + h, 1), :]
            lo = scr[pl.ds(base + 6 * ROWS + h, 1), :]
            mask = iota16 == hi
            parts = [
                jnp.where(mask, scr[pl.ds(base + k * ROWS + h, 1), :], 0.0).astype(BF16)
                for k in range(5)
            ]
            left.append(jnp.concatenate(parts, axis=0))
            right.append(jnp.where(iota128 == lo, F32(1.0), F32(0.0)).astype(BF16))
        sums = dot_nt(jnp.concatenate(left, axis=1), jnp.concatenate(right, axis=1))
        return block, sums

    def deposit(i, carry):
        done = [one_tile(picks[i * UNROLL + u]) for u in range(UNROLL)]
        for block, sums in done:
            acc[block] = acc[block] + sums
        return carry

    lax.fori_loop(0, (found + UNROLL - 1) // UNROLL, deposit, 0)


def first_deposit_kernel(pays, acc, *scratch):
    acc[...] = jnp.zeros_like(acc)
    add_deposits(pays, acc, *scratch)


def velocity_kernel(
    pays, before, own, far, side, edge, u_out, por_out, flux_y, flux_c, wide, flux, acc, *scratch
):
    c = lax.axis_index("c")
    native = lax.axis_index("z") == c
    acc[...] = before[...]
    add_deposits(pays, acc, *scratch)

    def amount(k):
        halves = []
        for b in range(OWN_BLOCKS):
            halves.append(
                jnp.concatenate([acc[b, k * 16 : k * 16 + 8, :], acc[b, k * 16 + 8 : k * 16 + 16, :]], axis=1)
            )
        return jnp.stack(
            [jnp.concatenate([halves[2 * i], halves[2 * i + 1]], axis=0) for i in range(4)]
        )

    for k in range(4):
        wide[k, 5 * c] = edge[k]
        for i in range(2):
            wide[k, 1 + 2 * c + i] = jnp.where(native, own[2 * k + i], far[2 * k + i])
            wide[k, 3 - 2 * c + i] = side[2 * k + i]
        wide[k, 5 * (1 - c)] = jnp.where(native, far[2 * k + c], own[2 * k + c])
    porosity = 1.0 / (1.0 + amount(0))
    por_out[...] = porosity
    below = 1.0 + DT * amount(1) / porosity
    centre = wide[3, 1:5]
    slopes = [
        0.5 * (wide[3, 2:6] - wide[3, 0:4]),
        0.5 * (rad_up(centre) - rad_down(centre)),
        0.5 * (axial_up(centre) - axial_down(centre)),
    ]
    for k in range(3):
        v = wide[k, 1:5]
        lap = (
            wide[k, 2:6] + wide[k, 0:4] + rad_up(v) + rad_down(v) + axial_up(v) + axial_down(v) - 6.0 * v
        )
        u = (v + DT * (NU * lap - slopes[k]) + DT * amount(2 + k) / porosity) / below
        u_out[k] = u
        flux[k] = porosity * u
    for i in range(3):
        for k in range(3):
            flux_y[3 * k + i] = flux[k, c + i]
            flux_c[3 * k + i] = flux[k, 1 - c + i]
        flux_y[9 + i] = wide[3, 1 + c + i]


def fluid_kernel(
    u_in, por_in, own, far, side, from_y, from_c, fields, kept, sent, flux, pres, out
):
    c = lax.axis_index("c")
    native = lax.axis_index("z") == c
    for k in range(3):
        flux[k, 3:7] = por_in[...] * u_in[k]
        for i in range(3):
            flux[k, 7 * c + i] = from_y[3 * k + i]
            flux[k, 7 * (1 - c) + i] = from_c[3 * k + i]
    for i in range(3):
        pres[7 * c + i] = from_y[9 + i]
    for i in range(2):
        pres[3 + 2 * c + i] = jnp.where(native, own[6 + i], far[6 + i])
        pres[5 - 2 * c + i] = side[6 + i]
        pres[7 - 6 * c + i] = jnp.where(native, far[6 + i], own[6 + i])
    pres[9 * (1 - c)] = side[8]
    f1 = flux[1, 1:9]
    f2 = flux[2, 1:9]
    source = 0.5 * (
        flux[0, 2:10] - flux[0, 0:8] + rad_up(f1) - rad_down(f1) + axial_up(f2) - axial_down(f2)
    )

    def sweep(p, s):
        centre = p[1:-1]
        return (
            p[2:]
            + p[:-2]
            + rad_up(centre)
            + rad_down(centre)
            + axial_up(centre)
            + axial_down(centre)
            - s / DT
        ) / 6.0

    p1 = sweep(pres[...], source)
    p2 = sweep(p1, source[1:-1])
    centre = p2[1:-1]
    slopes = [
        0.5 * (p2[2:] - p2[:-2]),
        0.5 * (rad_up(centre) - rad_down(centre)),
        0.5 * (axial_up(centre) - axial_down(centre)),
    ]
    for k in range(3):
        out[k] = u_in[k] - DT * slopes[k]
    out[3] = centre
    for k in range(4):
        for i in range(4):
            plane = out[k, i] if k < 3 else por_in[i]
            for h in range(2):
                half = plane[8 * h : 8 * h + 8]
                both = jnp.concatenate([half[:, :128], half[:, 128:]], axis=0)
                for copy in range(N_Y):
                    fields[copy, 2 * i + h, 16 * k : 16 * k + 16, :] = both.astype(BF16)
    for k in range(4):
        for i in range(2):
            kept[k, i] = out[k, 2 * c + i]
            sent[k, i] = out[k, 2 * (1 - c) + i]


def step_parcel(vel, rate, sampled):
    coupling = rate / (sampled[3] * sampled[3])
    pull = DT * coupling
    below = 1.0 + pull
    return [(vel[k] + pull * sampled[k]) / below for k in range(3)]


def leave_kernel(near, other, own, far, out0, out1):
    c = lax.axis_index("c")
    z_lo = lax.rem(lax.axis_index("blk"), Z_LO)
    list0 = jnp.where(z_lo == 0, far[8, 0:8, :], own[8, 0:8, :])
    list1 = jnp.where(z_lo == Z_LO - 1, far[8, 8:16, :], own[8, 8:16, :])
    both = jnp.concatenate([list0, list1], axis=1)
    place = both[5:6, :].astype(I32)
    block = place >> 11
    hi = hi_of(place & (BLOCK - 1))
    low = (rows_iota(128, 2 * MIG) == (place & 127)).astype(F32).astype(BF16)
    mask = rows_iota(16, 2 * MIG) == hi

    def gather(i, total):
        for u in range(OWN_BLOCKS):
            for half, core in ((near, c), (other, 1 - c)):
                picked = dot_nn(half[i, u], low)
                wanted = i * 16 + core * OWN_BLOCKS + u
                total = total + jnp.where(block == wanted, picked, 0.0)
        return total

    total = lax.fori_loop(0, N_Y, gather, jnp.zeros((64, 2 * MIG), F32))
    sampled = [
        jnp.sum(jnp.where(mask, total[16 * k : 16 * k + 16], 0.0), axis=0, keepdims=True)
        for k in range(4)
    ]
    sampled[3] = jnp.where(both[6:7, :] > 0.5, sampled[3], 1.0)
    vol, rate, valid = both[3:4, :], both[4:5, :], both[6:7, :]
    moved = step_parcel([both[k : k + 1, :] for k in range(3)], rate, sampled)
    for k, values in enumerate(moved + [vol, rate]):
        values = values * valid
        out0[k : k + 1, :] = values[:, :MIG]
        out1[k : k + 1, :] = values[:, MIG:]


def move_kernel(near, other, tiles_in, cell_in, keep, vel_in, rate_in, out, tiles, cell, vel, rate, sems):
    moves = ((tiles_in, tiles), (cell_in, cell), (vel_in, vel), (rate_in, rate))
    copies = [pltpu.make_async_copy(a, b, sems.at[i]) for i, (a, b) in enumerate(moves)]
    for copy in copies:
        copy.start()
    for copy in copies:
        copy.wait()
    c = lax.axis_index("c")
    iota16 = rows_iota(16, TP)
    iota128 = rows_iota(128, TP)

    def pair(ref, t):
        return jnp.concatenate([ref[pl.ds(2 * t, 1), :], ref[pl.ds(2 * t + 1, 1), :]], axis=1)

    def one_tile(t):
        block = tiles[t]
        row, col = block >> 4, block & 7
        here = jnp.where((block >> 3) & 1 == c, near[row, col], other[row, col])
        cells = pair(cell, t)
        low = jnp.where(iota128 == (cells & 127), F32(1.0), F32(0.0)).astype(BF16)
        picked = dot_nn(here, low)
        mask = iota16 == hi_of(cells)
        sampled = [
            jnp.sum(jnp.where(mask, picked[16 * k : 16 * k + 16], 0.0), axis=0, keepdims=True)
            for k in range(4)
        ]
        lanes = pl.ds(pl.multiple_of(t * TP, TP), TP)
        moved = step_parcel([vel[k : k + 1, lanes] for k in range(3)], pair(rate, t), sampled)
        stays = pair(keep, t)
        for k in range(3):
            out[k : k + 1, lanes] = moved[k] * stays

    def some(i, carry):
        for u in range(4):
            one_tile(i * 4 + u)
        return carry

    lax.fori_loop(0, TILES // 4, some, 0)


def over_y(values):
    copies = jnp.broadcast_to(values[None], (N_Y,) + values.shape)
    return lax.all_to_all(copies, "y", 0, 0, tiled=False)


def per_device(
    fluid_vel,
    pressure,
    parcel_vel,
    parcel_vol,
    parcel_rate,
    cell_local,
    tile_block,
    parcel_count,
    leave_lists,
    mig_counts,
):
    vol = parcel_vol.reshape(ROWS, 128)
    rate = parcel_rate.reshape(ROWS, 128)
    cell = cell_local.reshape(ROWS, 128)
    tiles = tile_block.reshape(1, TILES)
    plane = (RADIAL, LINE)
    pay, fpay, keep = call(
        pack_kernel,
        [((PAY_ROWS, 128), BF16), ((9,) + plane, F32), ((ROWS, 128), F32)],
        [parcel_vel, vol, rate, cell, tiles, parcel_count, leave_lists, mig_counts, fluid_vel, pressure],
        scratch=[
            pltpu.VMEM((3, PCAP), F32),
            pltpu.VMEM((ROWS, 128), F32),
            pltpu.VMEM((ROWS, 128), F32),
            pltpu.VMEM((ROWS, 128), I32),
            pltpu.VMEM((1, TILES), I32),
            pltpu.SMEM((1,), I32),
            pltpu.VMEM((2, MIG), I32),
            pltpu.VMEM((2, 1), I32),
            pltpu.VMEM((3, ROWS, 128), F32),
            pltpu.VMEM((16, 128), F32),
            pltpu.SemaphoreType.DMA((12,)),
        ],
        hbm=range(10),
        limit=PACK_LIMIT,
    )
    pay_far = swap(pay, "z")
    fpay_far = swap(fpay, "z")
    pays = over_y(jnp.concatenate([pay, pay_far]))
    pays, fpay_far = lax.optimization_barrier((pays, fpay_far))
    edge, side = call(
        edge_kernel, [((4,) + plane, F32), ((9,) + plane, F32)], [fpay, fpay_far]
    )
    route = halo_route()
    pays_c = swap(pays, "c")
    side = swap(side, "c")
    edge = lax.ppermute(edge, ALL, route)
    deposit_scratch = [
        pltpu.VMEM((SOURCES * SCR_ROWS, 128), F32),
        pltpu.VMEM((SOURCES, 128), I32),
        pltpu.SMEM((SOURCES, 128), I32),
        pltpu.SMEM((LIST_CAP,), I32),
        pltpu.SemaphoreType.DMA,
    ]
    sums_shape = (OWN_BLOCKS + 1, 80, 128)
    (sums,) = call(
        first_deposit_kernel,
        [(sums_shape, F32)],
        [pays.reshape(SOURCES, PAY_ROWS, 128)],
        scratch=deposit_scratch,
        flops=1 << 31,
    )
    u_star, porosity, flux_y, flux_c = call(
        velocity_kernel,
        [((3, 4) + plane, F32), ((4,) + plane, F32), ((12,) + plane, F32), ((9,) + plane, F32)],
        [pays_c.reshape(SOURCES, PAY_ROWS, 128), sums, fpay, fpay_far, side, edge],
        scratch=[
            pltpu.VMEM((4, 6) + plane, F32),
            pltpu.VMEM((3, 4) + plane, F32),
            pltpu.VMEM(sums_shape, F32),
        ]
        + deposit_scratch,
        flops=1 << 31,
    )
    from_y = lax.ppermute(flux_y, ALL, route)
    from_c = swap(flux_c, "c")
    fields, kept, sent = call(
        fluid_kernel,
        [((N_Y, OWN_BLOCKS, 64, 128), BF16), ((4, 2) + plane, F32), ((4, 2) + plane, F32)],
        [u_star, porosity, fpay, fpay_far, side, from_y, from_c],
        scratch=[
            pltpu.VMEM((3, 10) + plane, F32),
            pltpu.VMEM((10,) + plane, F32),
            pltpu.VMEM((4, 4) + plane, F32),
        ],
    )
    fields = lax.all_to_all(fields, "y", 0, 0)
    fields_c = swap(fields, "c")
    swapped = swap(sent, "c")
    mine = lax.axis_index("c") == lax.axis_index("z")
    out0, out1 = call(
        leave_kernel,
        [((5, MIG), F32), ((5, MIG), F32)],
        [fields, fields_c, fpay, fpay_far],
        flops=1 << 30,
    )
    arrive0 = lax.ppermute(out0, ALL, leave_route(-1))
    arrive1 = lax.ppermute(out1, ALL, leave_route(1))
    (parcel_next,) = call(
        move_kernel,
        [((3, PCAP), F32)],
        [fields, fields_c, tile_block, cell, keep, parcel_vel, rate],
        scratch=[
            pltpu.SMEM((TILES,), I32),
            pltpu.VMEM((ROWS, 128), I32),
            pltpu.VMEM((3, PCAP), F32),
            pltpu.VMEM((ROWS, 128), F32),
            pltpu.SemaphoreType.DMA((4,)),
        ],
        hbm=(2, 3, 5, 6),
        flops=1 << 31,
    )
    fluid_next = jnp.where(mine, kept[:3], swapped[:3])
    pressure_next = jnp.where(mine, kept[3], swapped[3])
    arrivals = jnp.stack([arrive0, arrive1], axis=1).transpose(1, 0, 2)
    return fluid_next, pressure_next, parcel_next, arrivals


def solution(mesh):
    fine = Mesh(mesh.devices.reshape(N_BLK, N_Y, N_Z, N_C), ALL)
    placed = (
        P(None, ALL, None, None),
        P(ALL, None, None),
        P(None, ALL),
        P(ALL),
        P(ALL),
        P(ALL),
        P(ALL),
        P(ALL),
        P(None, ALL),
        P(None, ALL),
    )
    return jax.shard_map(
        per_device,
        mesh=fine,
        in_specs=placed,
        out_specs=(
            P(None, ALL, None, None),
            P(ALL, None, None),
            P(None, ALL),
            P(None, None, ALL),
        ),
        check_vma=False,
    )
```

```python
import jax
import jax.numpy as jnp
from jax import lax
from jax.experimental import pallas as pl
from jax.experimental.pallas import tpu as pltpu
from jax.sharding import Mesh, PartitionSpec as P

PCAP = 8192
TP = 256
TILES = PCAP // TP
ROWS = PCAP // 128
BLOCK = 2048
RADIAL = 16
LINE = 256
MIG = 256
N_BLK, N_Y, N_Z, N_C = 32, 4, 2, 2
Z_LO = 8
ALL = ("blk", "y", "z", "c")

DT = 0.2
NU = 0.5

PAY_ROWS = 6 * ROWS + 16
SCR_ROWS = 7 * ROWS
SOURCES = N_Y * N_Z
OWN_BLOCKS = 8
UNROLL = 4
LIST_CAP = SOURCES * TILES + UNROLL

PACK_LIMIT = 56 << 20

F32 = jnp.float32
BF16 = jnp.bfloat16
I32 = jnp.int32


def flat(blk, y, z, c):
    return ((blk * N_Y + y) * N_Z + z) * N_C + c


def every_place():
    for blk in range(N_BLK):
        for y in range(N_Y):
            for z in range(N_Z):
                for c in range(N_C):
                    yield blk, y, z, c


def halo_route():
    pairs = []
    for blk, y, z, c in every_place():
        if c == 1:
            here = flat(blk, y, z, 1)
            if y < N_Y - 1:
                there = flat(blk, y + 1, z, 0)
            else:
                crossing = blk % Z_LO == Z_LO - 1
                there = flat((blk + 1) % N_BLK, 0, 1 - z if crossing else z, 0)
            pairs += [(here, there), (there, here)]
    return pairs


def leave_route(step):
    edge = 0 if step < 0 else Z_LO - 1
    pairs = []
    for blk, y, z, c in every_place():
        sender = flat(blk, y, 1 - z if blk % Z_LO == edge else z, c)
        pairs.append((sender, flat((blk + step) % N_BLK, y, z, c)))
    return pairs


def swap(values, axis):
    return lax.ppermute(values, axis, [(0, 1), (1, 0)])


def call(kernel, outs, ins, scratch=(), smem=(), hbm=(), limit=16 << 20, flops=0):
    def space(i):
        return pltpu.SMEM if i in smem else pltpu.HBM if i in hbm else pltpu.VMEM

    specs = [pl.BlockSpec(memory_space=space(i)) for i in range(len(ins))]
    return pl.pallas_call(
        kernel,
        out_shape=[jax.ShapeDtypeStruct(shape, dtype) for shape, dtype in outs],
        in_specs=specs,
        out_specs=[pl.BlockSpec(memory_space=pltpu.VMEM) for _ in outs],
        scratch_shapes=list(scratch),
        compiler_params=pltpu.CompilerParams(vmem_limit_bytes=limit),
        cost_estimate=pl.CostEstimate(flops=flops, bytes_accessed=1 << 20, transcendentals=0),
    )(*ins)


def rows_iota(rows, lanes):
    return lax.broadcasted_iota(I32, (rows, lanes), 0)


def dot_nt(a, b):
    return lax.dot_general(a, b, (((1,), (1,)), ((), ())), preferred_element_type=F32)


def dot_nn(a, b):
    return lax.dot_general(a, b, (((1,), (0,)), ((), ())), preferred_element_type=F32)


def hi_of(cell):
    return ((cell >> 7) & 1) * 8 + (cell >> 8)


def pack_kernel(*refs):
    sources, (pay, fpay, keep), (vel, vol, rate, cell, tiles, count, lists, mig, vsc, tsc, sems) = (
        refs[:10],
        refs[10:13],
        refs[13:],
    )
    fluid, press = sources[8:]
    targets = [vel, vol, rate, cell, tiles, count, lists, mig]
    targets += [fpay.at[2 * k : 2 * k + 2] for k in range(3)] + [fpay.at[6:8]]
    origins = list(sources[:8]) + [fluid.at[k] for k in range(3)] + [press]
    copies = [
        pltpu.make_async_copy(origin, target, sems.at[i])
        for i, (origin, target) in enumerate(zip(origins, targets))
    ]
    for copy in copies:
        copy.start()
    for copy in copies:
        copy.wait()
    for r in range(ROWS):
        for k in range(3):
            vsc[k, r : r + 1, :] = vel[k : k + 1, r * 128 : (r + 1) * 128]
    slot = rows_iota(ROWS, 128) * 128 + lax.broadcasted_iota(I32, (ROWS, 128), 1)
    active = (slot < count[0]).astype(F32)
    drag = vol[...] * rate[...]
    pay[0:ROWS, :] = (vol[...] * active).astype(BF16)
    pay[ROWS : 2 * ROWS, :] = (drag * active).astype(BF16)
    for k in range(3):
        pay[(2 + k) * ROWS : (3 + k) * ROWS, :] = (drag * vsc[k] * active).astype(BF16)
    cells = cell[...]
    hi = hi_of(cells)
    code = ((cells & 127) + 128).astype(F32)
    for bit in range(4):
        code = code * jnp.where((hi >> bit) & 1 == 1, F32(2.0 ** (1 << bit)), F32(1.0))
    pay[5 * ROWS : 6 * ROWS, :] = code.astype(BF16)
    lane = lax.broadcasted_iota(I32, (1, TILES), 1)
    tsc[...] = jnp.zeros((16, 128), F32)
    tsc[0:1, 0:TILES] = tiles[...].astype(F32)
    raw_tiles = tsc[...].astype(BF16)
    tsc[0:1, 0:TILES] = jnp.where(lane * TP < count[0], tiles[...].astype(F32), 255.0)
    pay[6 * ROWS : 6 * ROWS + 16, :] = tsc[...].astype(BF16)
    slots = jnp.concatenate([lists[0:1, :], lists[1:2, :]], axis=1)
    lane512 = lax.broadcasted_iota(I32, (1, 2 * MIG), 1)
    ends = jnp.where(lane512 < MIG, mig[:, 0:1], mig[:, 1:2] + MIG)
    valid = jnp.where(lane512 < ends, F32(1.0), F32(0.0))
    low = (rows_iota(128, 2 * MIG) == (slots & 127)).astype(F32).astype(BF16)
    row_mask = rows_iota(ROWS, 2 * MIG) == (slots >> 7)
    counts = dot_nt(jnp.where(row_mask, valid, 0.0).astype(BF16), low)
    keep[...] = active * jnp.where(counts > 0.5, 0.0, 1.0)

    def picked(values, parts):
        total = None
        for _ in range(parts):
            piece = values.astype(BF16)
            values = values - piece.astype(F32)
            term = dot_nn(piece, low)
            total = term if total is None else total + term
        return jnp.sum(jnp.where(row_mask, total, 0.0), axis=0, keepdims=True)

    def put(row, values):
        fpay[8, row : row + 1, :] = values[:, :MIG]
        fpay[8, 8 + row : 9 + row, :] = values[:, MIG:]

    for k in range(3):
        put(k, picked(vsc[k], 3))
    put(3, picked(vol[...], 3))
    put(4, picked(rate[...], 3))
    tile_hot = (rows_iota(128, 2 * MIG) == (slots >> 8)).astype(F32).astype(BF16)
    block = dot_nn(raw_tiles, tile_hot)[0:1, :]
    cell_hi = picked((cells >> 7).astype(F32), 1)
    cell_lo = picked((cells & 127).astype(F32), 1)
    put(5, block * BLOCK + cell_hi * 128.0 + cell_lo)
    put(6, valid)
    put(7, jnp.zeros_like(valid))


def edge_kernel(own, far, edge, side):
    c = lax.axis_index("c")
    native = lax.axis_index("z") == c
    for k in range(4):
        edge[k] = jnp.where(native, own[2 * k + c], far[2 * k + c])
        for i in range(2):
            side[2 * k + i] = jnp.where(native, far[2 * k + i], own[2 * k + i])
    side[8] = jnp.where(native, own[7 - c], far[7 - c])


def at(values, axis, step):
    size = values.shape[axis]
    moved = pltpu.roll(values, (-step) % size, axis)
    place = lax.broadcasted_iota(I32, values.shape, axis)
    return jnp.where(place == (size - 1 if step > 0 else 0), 0.0, moved)


def rad_up(values):
    return at(values, values.ndim - 2, 1)


def rad_down(values):
    return at(values, values.ndim - 2, -1)


def axial_up(values):
    return at(values, values.ndim - 1, 1)


def axial_down(values):
    return at(values, values.ndim - 1, -1)


def add_deposits(pays, acc, scr, tile_v, tile_s, picks, sem):
    first = lax.axis_index("y") * 16 + lax.axis_index("c") * OWN_BLOCKS
    for s in range(SOURCES):
        tile_v[s : s + 1, :] = pays[s, 6 * ROWS : 6 * ROWS + 16, :].astype(F32)[0:1, :].astype(I32)
    copy = pltpu.make_async_copy(tile_v, tile_s, sem)
    copy.start()

    def widen(s, carry):
        base = pl.multiple_of(s * SCR_ROWS, 8)
        scr[pl.ds(base, 5 * ROWS), :] = pays[s, 0 : 5 * ROWS, :].astype(F32)
        code = pays[s, 5 * ROWS : 6 * ROWS, :].astype(F32)
        hi = jnp.zeros_like(code)
        for step in (8, 4, 2, 1):
            large = code >= 2.0 ** (7 + step)
            code = jnp.where(large, code * 2.0**-step, code)
            hi = hi + jnp.where(large, F32(step), 0.0)
        scr[pl.ds(base + 5 * ROWS, ROWS), :] = hi
        scr[pl.ds(base + 6 * ROWS, ROWS), :] = code - 128.0
        return carry

    lax.fori_loop(0, SOURCES, widen, 0)
    copy.wait()

    def choose(s, found):
        for t in range(TILES):
            block = tile_s[s, t] - first
            picks[found] = (s * SCR_ROWS + 2 * t) * 16 + block
            mine = jnp.logical_and(block >= 0, block < OWN_BLOCKS)
            found = found + mine.astype(I32)
        return found

    found = lax.fori_loop(0, SOURCES, choose, jnp.int32(0))
    for i in range(UNROLL):
        picks[found + i] = OWN_BLOCKS
    iota16 = lax.broadcasted_iota(I32, (16, 128), 0).astype(F32)
    iota128 = lax.broadcasted_iota(I32, (128, 128), 0).astype(F32)

    def one_tile(code):
        block = code & 15
        base = code >> 4
        left, right = [], []
        for h in range(2):
            hi = scr[pl.ds(base + 5 * ROWS + h, 1), :]
            lo = scr[pl.ds(base + 6 * ROWS + h, 1), :]
            mask = iota16 == hi
            parts = [
                jnp.where(mask, scr[pl.ds(base + k * ROWS + h, 1), :], 0.0).astype(BF16)
                for k in range(5)
            ]
            left.append(jnp.concatenate(parts, axis=0))
            right.append(jnp.where(iota128 == lo, F32(1.0), F32(0.0)).astype(BF16))
        sums = dot_nt(jnp.concatenate(left, axis=1), jnp.concatenate(right, axis=1))
        return block, sums

    def deposit(i, carry):
        done = [one_tile(picks[i * UNROLL + u]) for u in range(UNROLL)]
        for block, sums in done:
            acc[block] = acc[block] + sums
        return carry

    lax.fori_loop(0, (found + UNROLL - 1) // UNROLL, deposit, 0)


def first_deposit_kernel(pays, acc, *scratch):
    acc[...] = jnp.zeros_like(acc)
    add_deposits(pays, acc, *scratch)


def second_deposit_kernel(pays, before, acc, *scratch):
    acc[...] = before[...]
    add_deposits(pays, acc, *scratch)


def velocity_kernel(acc, own, far, side, edge, u_out, por_out, flux_y, flux_c, wide, flux):
    c = lax.axis_index("c")
    native = lax.axis_index("z") == c

    def amount(k):
        halves = []
        for b in range(OWN_BLOCKS):
            halves.append(
                jnp.concatenate([acc[b, k * 16 : k * 16 + 8, :], acc[b, k * 16 + 8 : k * 16 + 16, :]], axis=1)
            )
        return jnp.stack(
            [jnp.concatenate([halves[2 * i], halves[2 * i + 1]], axis=0) for i in range(4)]
        )

    for k in range(4):
        wide[k, 5 * c] = edge[k]
        for i in range(2):
            wide[k, 1 + 2 * c + i] = jnp.where(native, own[2 * k + i], far[2 * k + i])
            wide[k, 3 - 2 * c + i] = side[2 * k + i]
        wide[k, 5 * (1 - c)] = jnp.where(native, far[2 * k + c], own[2 * k + c])
    porosity = 1.0 / (1.0 + amount(0))
    por_out[...] = porosity
    below = 1.0 + DT * amount(1) / porosity
    centre = wide[3, 1:5]
    slopes = [
        0.5 * (wide[3, 2:6] - wide[3, 0:4]),
        0.5 * (rad_up(centre) - rad_down(centre)),
        0.5 * (axial_up(centre) - axial_down(centre)),
    ]
    for k in range(3):
        v = wide[k, 1:5]
        lap = (
            wide[k, 2:6] + wide[k, 0:4] + rad_up(v) + rad_down(v) + axial_up(v) + axial_down(v) - 6.0 * v
        )
        u = (v + DT * (NU * lap - slopes[k]) + DT * amount(2 + k) / porosity) / below
        u_out[k] = u
        flux[k] = porosity * u
    for i in range(3):
        for k in range(3):
            flux_y[3 * k + i] = flux[k, c + i]
            flux_c[3 * k + i] = flux[k, 1 - c + i]
        flux_y[9 + i] = wide[3, 1 + c + i]


def fluid_kernel(
    u_in, por_in, own, far, side, from_y, from_c, fields, kept, sent, flux, pres, out
):
    c = lax.axis_index("c")
    native = lax.axis_index("z") == c
    for k in range(3):
        flux[k, 3:7] = por_in[...] * u_in[k]
        for i in range(3):
            flux[k, 7 * c + i] = from_y[3 * k + i]
            flux[k, 7 * (1 - c) + i] = from_c[1 - c, 3 * k + i]
    for i in range(3):
        pres[7 * c + i] = from_y[9 + i]
    for i in range(2):
        pres[3 + 2 * c + i] = jnp.where(native, own[6 + i], far[6 + i])
        pres[5 - 2 * c + i] = side[6 + i]
        pres[7 - 6 * c + i] = jnp.where(native, far[6 + i], own[6 + i])
    pres[9 * (1 - c)] = side[8]
    f1 = flux[1, 1:9]
    f2 = flux[2, 1:9]
    source = 0.5 * (
        flux[0, 2:10] - flux[0, 0:8] + rad_up(f1) - rad_down(f1) + axial_up(f2) - axial_down(f2)
    )

    def sweep(p, s):
        centre = p[1:-1]
        return (
            p[2:]
            + p[:-2]
            + rad_up(centre)
            + rad_down(centre)
            + axial_up(centre)
            + axial_down(centre)
            - s / DT
        ) / 6.0

    p1 = sweep(pres[...], source)
    p2 = sweep(p1, source[1:-1])
    centre = p2[1:-1]
    slopes = [
        0.5 * (p2[2:] - p2[:-2]),
        0.5 * (rad_up(centre) - rad_down(centre)),
        0.5 * (axial_up(centre) - axial_down(centre)),
    ]
    for k in range(3):
        out[k] = u_in[k] - DT * slopes[k]
    out[3] = centre
    for k in range(4):
        for i in range(4):
            plane = out[k, i] if k < 3 else por_in[i]
            for h in range(2):
                half = plane[8 * h : 8 * h + 8]
                both = jnp.concatenate([half[:, :128], half[:, 128:]], axis=0)
                for copy in range(N_Y):
                    fields[copy, 2 * i + h, 16 * k : 16 * k + 16, :] = both.astype(BF16)
    for k in range(4):
        for i in range(2):
            kept[k, i] = out[k, 2 * c + i]
            sent[k, i] = out[k, 2 * (1 - c) + i]


def step_parcel(vel, rate, sampled):
    coupling = rate / (sampled[3] * sampled[3])
    pull = DT * coupling
    below = 1.0 + pull
    return [(vel[k] + pull * sampled[k]) / below for k in range(3)]


def leave_kernel(near, other, own, far, out0, out1):
    c = lax.axis_index("c")
    z_lo = lax.rem(lax.axis_index("blk"), Z_LO)
    list0 = jnp.where(z_lo == 0, far[8, 0:8, :], own[8, 0:8, :])
    list1 = jnp.where(z_lo == Z_LO - 1, far[8, 8:16, :], own[8, 8:16, :])
    both = jnp.concatenate([list0, list1], axis=1)
    place = both[5:6, :].astype(I32)
    block = place >> 11
    hi = hi_of(place & (BLOCK - 1))
    low = (rows_iota(128, 2 * MIG) == (place & 127)).astype(F32).astype(BF16)
    mask = rows_iota(16, 2 * MIG) == hi

    def gather(i, total):
        for u in range(OWN_BLOCKS):
            for half, core in ((near, c), (other, 1 - c)):
                picked = dot_nn(half[i, u], low)
                wanted = i * 16 + core * OWN_BLOCKS + u
                total = total + jnp.where(block == wanted, picked, 0.0)
        return total

    total = lax.fori_loop(0, N_Y, gather, jnp.zeros((64, 2 * MIG), F32))
    sampled = [
        jnp.sum(jnp.where(mask, total[16 * k : 16 * k + 16], 0.0), axis=0, keepdims=True)
        for k in range(4)
    ]
    sampled[3] = jnp.where(both[6:7, :] > 0.5, sampled[3], 1.0)
    vol, rate, valid = both[3:4, :], both[4:5, :], both[6:7, :]
    moved = step_parcel([both[k : k + 1, :] for k in range(3)], rate, sampled)
    for k, values in enumerate(moved + [vol, rate]):
        values = values * valid
        out0[k : k + 1, :] = values[:, :MIG]
        out1[k : k + 1, :] = values[:, MIG:]


def move_kernel(near, other, tiles_in, cell_in, keep, vel_in, rate_in, out, tiles, cell, vel, rate, sems):
    moves = ((tiles_in, tiles), (cell_in, cell), (vel_in, vel), (rate_in, rate))
    copies = [pltpu.make_async_copy(a, b, sems.at[i]) for i, (a, b) in enumerate(moves)]
    for copy in copies:
        copy.start()
    for copy in copies:
        copy.wait()
    c = lax.axis_index("c")
    iota16 = rows_iota(16, TP)
    iota128 = rows_iota(128, TP)

    def pair(ref, t):
        return jnp.concatenate([ref[pl.ds(2 * t, 1), :], ref[pl.ds(2 * t + 1, 1), :]], axis=1)

    def one_tile(t):
        block = tiles[t]
        row, col = block >> 4, block & 7
        here = jnp.where((block >> 3) & 1 == c, near[row, col], other[row, col])
        cells = pair(cell, t)
        low = jnp.where(iota128 == (cells & 127), F32(1.0), F32(0.0)).astype(BF16)
        picked = dot_nn(here, low)
        mask = iota16 == hi_of(cells)
        sampled = [
            jnp.sum(jnp.where(mask, picked[16 * k : 16 * k + 16], 0.0), axis=0, keepdims=True)
            for k in range(4)
        ]
        lanes = pl.ds(pl.multiple_of(t * TP, TP), TP)
        moved = step_parcel([vel[k : k + 1, lanes] for k in range(3)], pair(rate, t), sampled)
        stays = pair(keep, t)
        for k in range(3):
            out[k : k + 1, lanes] = moved[k] * stays

    def some(i, carry):
        for u in range(4):
            one_tile(i * 4 + u)
        return carry

    lax.fori_loop(0, TILES // 4, some, 0)


def over_y(values):
    copies = jnp.broadcast_to(values[None], (N_Y,) + values.shape)
    return lax.all_to_all(copies, "y", 0, 0, tiled=False)


def per_device(
    fluid_vel,
    pressure,
    parcel_vel,
    parcel_vol,
    parcel_rate,
    cell_local,
    tile_block,
    parcel_count,
    leave_lists,
    mig_counts,
):
    vol = parcel_vol.reshape(ROWS, 128)
    rate = parcel_rate.reshape(ROWS, 128)
    cell = cell_local.reshape(ROWS, 128)
    tiles = tile_block.reshape(1, TILES)
    plane = (RADIAL, LINE)
    pay, fpay, keep = call(
        pack_kernel,
        [((PAY_ROWS, 128), BF16), ((9,) + plane, F32), ((ROWS, 128), F32)],
        [parcel_vel, vol, rate, cell, tiles, parcel_count, leave_lists, mig_counts.reshape(1, 2), fluid_vel, pressure],
        scratch=[
            pltpu.VMEM((3, PCAP), F32),
            pltpu.VMEM((ROWS, 128), F32),
            pltpu.VMEM((ROWS, 128), F32),
            pltpu.VMEM((ROWS, 128), I32),
            pltpu.VMEM((1, TILES), I32),
            pltpu.SMEM((1,), I32),
            pltpu.VMEM((2, MIG), I32),
            pltpu.VMEM((1, 2), I32),
            pltpu.VMEM((3, ROWS, 128), F32),
            pltpu.VMEM((16, 128), F32),
            pltpu.SemaphoreType.DMA((12,)),
        ],
        hbm=range(10),
        limit=PACK_LIMIT,
    )
    pay_far = swap(pay, "z")
    fpay_far = swap(fpay, "z")
    pays = over_y(jnp.concatenate([pay, pay_far]))
    deposit_scratch = [
        pltpu.VMEM((SOURCES * SCR_ROWS, 128), F32),
        pltpu.VMEM((SOURCES, 128), I32),
        pltpu.SMEM((SOURCES, 128), I32),
        pltpu.SMEM((LIST_CAP,), I32),
        pltpu.SemaphoreType.DMA,
    ]
    sums_shape = (OWN_BLOCKS + 1, 80, 128)
    (sums,) = call(
        first_deposit_kernel,
        [(sums_shape, F32)],
        [pays.reshape(SOURCES, PAY_ROWS, 128)],
        scratch=deposit_scratch,
    flops=1 << 36,
    )
    pays_c = swap(pays, "c")
    fpay_far, sums = lax.optimization_barrier((fpay_far, sums))
    edge, side = call(
        edge_kernel, [((4,) + plane, F32), ((9,) + plane, F32)], [fpay, fpay_far]
    )
    route = halo_route()
    side = swap(side, "c")
    edge = lax.ppermute(edge, ALL, route)
    (sums,) = call(
        second_deposit_kernel,
        [(sums_shape, F32)],
        [pays_c.reshape(SOURCES, PAY_ROWS, 128), sums],
        scratch=deposit_scratch,
        flops=1 << 36,
    )
    u_star, porosity, flux_y, flux_c = call(
        velocity_kernel,
        [((3, 4) + plane, F32), ((4,) + plane, F32), ((12,) + plane, F32), ((9,) + plane, F32)],
        [sums, fpay, fpay_far, side, edge],
        scratch=[pltpu.VMEM((4, 6) + plane, F32), pltpu.VMEM((3, 4) + plane, F32)],
    )
    from_y = lax.ppermute(flux_y, ALL, route)
    from_c = lax.all_gather(flux_c, "c", axis=0)
    fields, kept, sent = call(
        fluid_kernel,
        [((N_Y, OWN_BLOCKS, 64, 128), BF16), ((4, 2) + plane, F32), ((4, 2) + plane, F32)],
        [u_star, porosity, fpay, fpay_far, side, from_y, from_c],
        scratch=[
            pltpu.VMEM((3, 10) + plane, F32),
            pltpu.VMEM((10,) + plane, F32),
            pltpu.VMEM((4, 4) + plane, F32),
        ],
    )
    fields = lax.all_to_all(fields, "y", 0, 0)
    fields_c = swap(fields, "c")
    swapped = swap(sent, "c")
    mine = lax.axis_index("c") == lax.axis_index("z")
    out0, out1 = call(
        leave_kernel,
        [((5, MIG), F32), ((5, MIG), F32)],
        [fields, fields_c, fpay, fpay_far],
        flops=1 << 30,
    )
    arrive0 = lax.ppermute(out0, ALL, leave_route(-1))
    arrive1 = lax.ppermute(out1, ALL, leave_route(1))
    (parcel_next,) = call(
        move_kernel,
        [((3, PCAP), F32)],
        [fields, fields_c, tile_block, cell, keep, parcel_vel, rate],
        scratch=[
            pltpu.SMEM((TILES,), I32),
            pltpu.VMEM((ROWS, 128), I32),
            pltpu.VMEM((3, PCAP), F32),
            pltpu.VMEM((ROWS, 128), F32),
            pltpu.SemaphoreType.DMA((4,)),
        ],
        hbm=(2, 3, 5, 6),
        flops=1 << 31,
    )
    fluid_next = jnp.where(mine, kept[:3], swapped[:3])
    pressure_next = jnp.where(mine, kept[3], swapped[3])
    arrivals = jnp.stack([arrive0, arrive1], axis=1).transpose(1, 0, 2)
    return fluid_next, pressure_next, parcel_next, arrivals


def solution(mesh):
    fine = Mesh(mesh.devices.reshape(N_BLK, N_Y, N_Z, N_C), ALL)
    placed = (
        P(None, ALL, None, None),
        P(ALL, None, None),
        P(None, ALL),
        P(ALL),
        P(ALL),
        P(ALL),
        P(ALL),
        P(ALL),
        P(None, ALL),
        P(None, ALL),
    )
    return jax.shard_map(
        per_device,
        mesh=fine,
        in_specs=placed,
        out_specs=(
            P(None, ALL, None, None),
            P(ALL, None, None),
            P(None, ALL),
            P(None, None, ALL),
        ),
        check_vma=False,
    )
```

```python
import functools

import jax
import jax.numpy as jnp
from jax import lax
from jax.experimental import pallas as pl
from jax.experimental.pallas import tpu as pltpu
from jax.sharding import Mesh, PartitionSpec as P

PCAP = 8192
TP = 256
TILES = PCAP // TP
ROWS = PCAP // 128
BLOCK = 2048
RADIAL = 16
LINE = 256
MIG = 256
N_BLK, N_Y, N_Z, N_C = 32, 4, 2, 2
Z_LO = 8
ALL = ("blk", "y", "z", "c")

DT = 0.2
NU = 0.5

PAY_ROWS = 6 * ROWS + 16
SCR_ROWS = 7 * ROWS
SOURCES = N_Y * N_Z
OWN_BLOCKS = 8
UNROLL = 4
LIST_CAP = SOURCES * TILES + UNROLL

PACK_LIMIT = 56 << 20

F32 = jnp.float32
BF16 = jnp.bfloat16
I32 = jnp.int32


def flat(blk, y, z, c):
    return ((blk * N_Y + y) * N_Z + z) * N_C + c


def every_place():
    for blk in range(N_BLK):
        for y in range(N_Y):
            for z in range(N_Z):
                for c in range(N_C):
                    yield blk, y, z, c


def halo_route():
    pairs = []
    for blk, y, z, c in every_place():
        if c == 1:
            here = flat(blk, y, z, 1)
            if y < N_Y - 1:
                there = flat(blk, y + 1, z, 0)
            else:
                crossing = blk % Z_LO == Z_LO - 1
                there = flat((blk + 1) % N_BLK, 0, 1 - z if crossing else z, 0)
            pairs += [(here, there), (there, here)]
    return pairs


def leave_route(step):
    edge = 0 if step < 0 else Z_LO - 1
    pairs = []
    for blk, y, z, c in every_place():
        sender = flat(blk, y, 1 - z if blk % Z_LO == edge else z, c)
        pairs.append((sender, flat((blk + step) % N_BLK, y, z, c)))
    return pairs


def swap(values, axis):
    return lax.ppermute(values, axis, [(0, 1), (1, 0)])


def call(kernel, outs, ins, scratch=(), smem=(), hbm=(), limit=16 << 20, flops=0):
    def space(i):
        return pltpu.SMEM if i in smem else pltpu.HBM if i in hbm else pltpu.VMEM

    specs = [pl.BlockSpec(memory_space=space(i)) for i in range(len(ins))]
    return pl.pallas_call(
        kernel,
        out_shape=[jax.ShapeDtypeStruct(shape, dtype) for shape, dtype in outs],
        in_specs=specs,
        out_specs=[pl.BlockSpec(memory_space=pltpu.VMEM) for _ in outs],
        scratch_shapes=list(scratch),
        compiler_params=pltpu.CompilerParams(vmem_limit_bytes=limit),
        cost_estimate=pl.CostEstimate(flops=flops, bytes_accessed=1 << 20, transcendentals=0),
    )(*ins)


def rows_iota(rows, lanes):
    return lax.broadcasted_iota(I32, (rows, lanes), 0)


def dot_nt(a, b):
    return lax.dot_general(a, b, (((1,), (1,)), ((), ())), preferred_element_type=F32)


def dot_nn(a, b):
    return lax.dot_general(a, b, (((1,), (0,)), ((), ())), preferred_element_type=F32)


def hi_of(cell):
    return ((cell >> 7) & 1) * 8 + (cell >> 8)


def pack_kernel(*refs):
    sources, (pay, fpay, keep), (vel, vol, rate, cell, tiles, count, lists, mig, vsc, tsc, sems) = (
        refs[:10],
        refs[10:13],
        refs[13:],
    )
    fluid, press = sources[8:]
    targets = [vel, vol, rate, cell, tiles, count, lists, mig]
    targets += [fpay.at[2 * k : 2 * k + 2] for k in range(3)] + [fpay.at[6:8]]
    origins = list(sources[:8]) + [fluid.at[k] for k in range(3)] + [press]
    copies = [
        pltpu.make_async_copy(origin, target, sems.at[i])
        for i, (origin, target) in enumerate(zip(origins, targets))
    ]
    for copy in copies:
        copy.start()
    for copy in copies:
        copy.wait()
    for r in range(ROWS):
        for k in range(3):
            vsc[k, r : r + 1, :] = vel[k : k + 1, r * 128 : (r + 1) * 128]
    slot = rows_iota(ROWS, 128) * 128 + lax.broadcasted_iota(I32, (ROWS, 128), 1)
    active = (slot < count[0]).astype(F32)
    drag = vol[...] * rate[...]
    pay[0:ROWS, :] = (vol[...] * active).astype(BF16)
    pay[ROWS : 2 * ROWS, :] = (drag * active).astype(BF16)
    for k in range(3):
        pay[(2 + k) * ROWS : (3 + k) * ROWS, :] = (drag * vsc[k] * active).astype(BF16)
    cells = cell[...]
    hi = hi_of(cells)
    code = ((cells & 127) + 128).astype(F32)
    for bit in range(4):
        code = code * jnp.where((hi >> bit) & 1 == 1, F32(2.0 ** (1 << bit)), F32(1.0))
    pay[5 * ROWS : 6 * ROWS, :] = code.astype(BF16)
    lane = lax.broadcasted_iota(I32, (1, TILES), 1)
    tsc[...] = jnp.zeros((16, 128), F32)
    tsc[0:1, 0:TILES] = tiles[...].astype(F32)
    raw_tiles = tsc[...].astype(BF16)
    tsc[0:1, 0:TILES] = jnp.where(lane * TP < count[0], tiles[...].astype(F32), 255.0)
    pay[6 * ROWS : 6 * ROWS + 16, :] = tsc[...].astype(BF16)
    slots = jnp.concatenate([lists[0:1, :], lists[1:2, :]], axis=1)
    lane512 = lax.broadcasted_iota(I32, (1, 2 * MIG), 1)
    ends = jnp.where(lane512 < MIG, mig[:, 0:1], mig[:, 1:2] + MIG)
    valid = jnp.where(lane512 < ends, F32(1.0), F32(0.0))
    low = (rows_iota(128, 2 * MIG) == (slots & 127)).astype(F32).astype(BF16)
    row_mask = rows_iota(ROWS, 2 * MIG) == (slots >> 7)
    counts = dot_nt(jnp.where(row_mask, valid, 0.0).astype(BF16), low)
    keep[...] = active * jnp.where(counts > 0.5, 0.0, 1.0)

    def picked(values, parts):
        total = None
        for _ in range(parts):
            piece = values.astype(BF16)
            values = values - piece.astype(F32)
            term = dot_nn(piece, low)
            total = term if total is None else total + term
        return jnp.sum(jnp.where(row_mask, total, 0.0), axis=0, keepdims=True)

    def put(row, values):
        fpay[8, row : row + 1, :] = values[:, :MIG]
        fpay[8, 8 + row : 9 + row, :] = values[:, MIG:]

    for k in range(3):
        put(k, picked(vsc[k], 3))
    put(3, picked(vol[...], 3))
    put(4, picked(rate[...], 3))
    tile_hot = (rows_iota(128, 2 * MIG) == (slots >> 8)).astype(F32).astype(BF16)
    block = dot_nn(raw_tiles, tile_hot)[0:1, :]
    cell_hi = picked((cells >> 7).astype(F32), 1)
    cell_lo = picked((cells & 127).astype(F32), 1)
    put(5, block * BLOCK + cell_hi * 128.0 + cell_lo)
    put(6, valid)
    put(7, jnp.zeros_like(valid))


def edge_kernel(own, far, edge, side):
    c = lax.axis_index("c")
    native = lax.axis_index("z") == c
    for k in range(4):
        edge[k] = jnp.where(native, own[2 * k + c], far[2 * k + c])
        for i in range(2):
            side[2 * k + i] = jnp.where(native, far[2 * k + i], own[2 * k + i])
    side[8] = jnp.where(native, own[7 - c], far[7 - c])


def at(values, axis, step):
    size = values.shape[axis]
    moved = pltpu.roll(values, (-step) % size, axis)
    place = lax.broadcasted_iota(I32, values.shape, axis)
    return jnp.where(place == (size - 1 if step > 0 else 0), 0.0, moved)


def rad_up(values):
    return at(values, values.ndim - 2, 1)


def rad_down(values):
    return at(values, values.ndim - 2, -1)


def axial_up(values):
    return at(values, values.ndim - 1, 1)


def axial_down(values):
    return at(values, values.ndim - 1, -1)


def add_deposits(pays, acc, scr, tile_v, tile_s, picks, sem, skip_own=False):
    y = lax.axis_index("y")
    first = y * 16 + lax.axis_index("c") * OWN_BLOCKS
    sources = pays.shape[0]
    for s in range(sources):
        tile_v[s : s + 1, :] = pays[s, 6 * ROWS : 6 * ROWS + 16, :].astype(F32)[0:1, :].astype(I32)
    copy = pltpu.make_async_copy(tile_v, tile_s, sem)
    copy.start()

    def widen(s, carry):
        base = pl.multiple_of(s * SCR_ROWS, 8)
        scr[pl.ds(base, 5 * ROWS), :] = pays[s, 0 : 5 * ROWS, :].astype(F32)
        code = pays[s, 5 * ROWS : 6 * ROWS, :].astype(F32)
        hi = jnp.zeros_like(code)
        for step in (8, 4, 2, 1):
            large = code >= 2.0 ** (7 + step)
            code = jnp.where(large, code * 2.0**-step, code)
            hi = hi + jnp.where(large, F32(step), 0.0)
        scr[pl.ds(base + 5 * ROWS, ROWS), :] = hi
        scr[pl.ds(base + 6 * ROWS, ROWS), :] = code - 128.0
        return carry

    lax.fori_loop(0, sources, widen, 0)
    copy.wait()

    def choose(s, found):
        base = first + jnp.where(s // N_Z == y, 1024, 0) if skip_own else first
        for t in range(TILES):
            block = tile_s[s, t] - base
            picks[found] = (s * SCR_ROWS + 2 * t) * 16 + block
            mine = jnp.logical_and(block >= 0, block < OWN_BLOCKS)
            found = found + mine.astype(I32)
        return found

    found = lax.fori_loop(0, sources, choose, jnp.int32(0))
    for i in range(UNROLL):
        picks[found + i] = OWN_BLOCKS
    iota16 = lax.broadcasted_iota(I32, (16, 128), 0).astype(F32)
    iota128 = lax.broadcasted_iota(I32, (128, 128), 0).astype(F32)

    def one_tile(code):
        block = code & 15
        base = code >> 4
        left, right = [], []
        for h in range(2):
            hi = scr[pl.ds(base + 5 * ROWS + h, 1), :]
            lo = scr[pl.ds(base + 6 * ROWS + h, 1), :]
            mask = iota16 == hi
            parts = [
                jnp.where(mask, scr[pl.ds(base + k * ROWS + h, 1), :], 0.0).astype(BF16)
                for k in range(5)
            ]
            left.append(jnp.concatenate(parts, axis=0))
            right.append(jnp.where(iota128 == lo, F32(1.0), F32(0.0)).astype(BF16))
        sums = dot_nt(jnp.concatenate(left, axis=1), jnp.concatenate(right, axis=1))
        return block, sums

    def deposit(i, carry):
        done = [one_tile(picks[i * UNROLL + u]) for u in range(UNROLL)]
        for block, sums in done:
            acc[block] = acc[block] + sums
        return carry

    lax.fori_loop(0, (found + UNROLL - 1) // UNROLL, deposit, 0)


def first_deposit_kernel(pays, acc, *scratch):
    acc[...] = jnp.zeros_like(acc)
    add_deposits(pays, acc, *scratch)


def next_deposit_kernel(skip_own, pays, before, acc, *scratch):
    acc[...] = before[...]
    add_deposits(pays, acc, *scratch, skip_own=skip_own)


def spread_kernel(own, far, both, out):
    both[0] = own[...]
    both[1] = far[...]
    for y in range(N_Y):
        out[y, 0] = own[...]
        out[y, 1] = far[...]


def velocity_kernel(acc, own, far, side, edge, u_out, por_out, flux_y, flux_c, wide, flux):
    c = lax.axis_index("c")
    native = lax.axis_index("z") == c

    def amount(k):
        halves = []
        for b in range(OWN_BLOCKS):
            halves.append(
                jnp.concatenate([acc[b, k * 16 : k * 16 + 8, :], acc[b, k * 16 + 8 : k * 16 + 16, :]], axis=1)
            )
        return jnp.stack(
            [jnp.concatenate([halves[2 * i], halves[2 * i + 1]], axis=0) for i in range(4)]
        )

    for k in range(4):
        wide[k, 5 * c] = edge[k]
        for i in range(2):
            wide[k, 1 + 2 * c + i] = jnp.where(native, own[2 * k + i], far[2 * k + i])
            wide[k, 3 - 2 * c + i] = side[2 * k + i]
        wide[k, 5 * (1 - c)] = jnp.where(native, far[2 * k + c], own[2 * k + c])
    porosity = 1.0 / (1.0 + amount(0))
    por_out[...] = porosity
    below = 1.0 + DT * amount(1) / porosity
    centre = wide[3, 1:5]
    slopes = [
        0.5 * (wide[3, 2:6] - wide[3, 0:4]),
        0.5 * (rad_up(centre) - rad_down(centre)),
        0.5 * (axial_up(centre) - axial_down(centre)),
    ]
    for k in range(3):
        v = wide[k, 1:5]
        lap = (
            wide[k, 2:6] + wide[k, 0:4] + rad_up(v) + rad_down(v) + axial_up(v) + axial_down(v) - 6.0 * v
        )
        u = (v + DT * (NU * lap - slopes[k]) + DT * amount(2 + k) / porosity) / below
        u_out[k] = u
        flux[k] = porosity * u
    for i in range(3):
        for k in range(3):
            flux_y[3 * k + i] = flux[k, c + i]
            flux_c[3 * k + i] = flux[k, 1 - c + i]
        flux_y[9 + i] = wide[3, 1 + c + i]


def fluid_kernel(
    u_in, por_in, own, far, side, from_y, from_c, fields, kept, sent, flux, pres, out
):
    c = lax.axis_index("c")
    native = lax.axis_index("z") == c
    for k in range(3):
        flux[k, 3:7] = por_in[...] * u_in[k]
        for i in range(3):
            flux[k, 7 * c + i] = from_y[3 * k + i]
            flux[k, 7 * (1 - c) + i] = from_c[1 - c, 3 * k + i]
    for i in range(3):
        pres[7 * c + i] = from_y[9 + i]
    for i in range(2):
        pres[3 + 2 * c + i] = jnp.where(native, own[6 + i], far[6 + i])
        pres[5 - 2 * c + i] = side[6 + i]
        pres[7 - 6 * c + i] = jnp.where(native, far[6 + i], own[6 + i])
    pres[9 * (1 - c)] = side[8]
    f1 = flux[1, 1:9]
    f2 = flux[2, 1:9]
    source = 0.5 * (
        flux[0, 2:10] - flux[0, 0:8] + rad_up(f1) - rad_down(f1) + axial_up(f2) - axial_down(f2)
    )

    def sweep(p, s):
        centre = p[1:-1]
        return (
            p[2:]
            + p[:-2]
            + rad_up(centre)
            + rad_down(centre)
            + axial_up(centre)
            + axial_down(centre)
            - s / DT
        ) / 6.0

    p1 = sweep(pres[...], source)
    p2 = sweep(p1, source[1:-1])
    centre = p2[1:-1]
    slopes = [
        0.5 * (p2[2:] - p2[:-2]),
        0.5 * (rad_up(centre) - rad_down(centre)),
        0.5 * (axial_up(centre) - axial_down(centre)),
    ]
    for k in range(3):
        out[k] = u_in[k] - DT * slopes[k]
    out[3] = centre
    for k in range(4):
        for i in range(4):
            plane = out[k, i] if k < 3 else por_in[i]
            for h in range(2):
                half = plane[8 * h : 8 * h + 8]
                both = jnp.concatenate([half[:, :128], half[:, 128:]], axis=0)
                for copy in range(N_Y):
                    fields[copy, 2 * i + h, 16 * k : 16 * k + 16, :] = both.astype(BF16)
    for k in range(4):
        for i in range(2):
            kept[k, i] = out[k, 2 * c + i]
            sent[k, i] = out[k, 2 * (1 - c) + i]


def step_parcel(vel, rate, sampled):
    coupling = rate / (sampled[3] * sampled[3])
    pull = DT * coupling
    below = 1.0 + pull
    return [(vel[k] + pull * sampled[k]) / below for k in range(3)]


def leave_kernel(near, other, own, far, out0, out1):
    c = lax.axis_index("c")
    z_lo = lax.rem(lax.axis_index("blk"), Z_LO)
    list0 = jnp.where(z_lo == 0, far[8, 0:8, :], own[8, 0:8, :])
    list1 = jnp.where(z_lo == Z_LO - 1, far[8, 8:16, :], own[8, 8:16, :])
    both = jnp.concatenate([list0, list1], axis=1)
    place = both[5:6, :].astype(I32)
    block = place >> 11
    hi = hi_of(place & (BLOCK - 1))
    low = (rows_iota(128, 2 * MIG) == (place & 127)).astype(F32).astype(BF16)
    mask = rows_iota(16, 2 * MIG) == hi

    def gather(i, total):
        for u in range(OWN_BLOCKS):
            for half, core in ((near, c), (other, 1 - c)):
                picked = dot_nn(half[i, u], low)
                wanted = i * 16 + core * OWN_BLOCKS + u
                total = total + jnp.where(block == wanted, picked, 0.0)
        return total

    total = lax.fori_loop(0, N_Y, gather, jnp.zeros((64, 2 * MIG), F32))
    sampled = [
        jnp.sum(jnp.where(mask, total[16 * k : 16 * k + 16], 0.0), axis=0, keepdims=True)
        for k in range(4)
    ]
    sampled[3] = jnp.where(both[6:7, :] > 0.5, sampled[3], 1.0)
    vol, rate, valid = both[3:4, :], both[4:5, :], both[6:7, :]
    moved = step_parcel([both[k : k + 1, :] for k in range(3)], rate, sampled)
    for k, values in enumerate(moved + [vol, rate]):
        values = values * valid
        out0[k : k + 1, :] = values[:, :MIG]
        out1[k : k + 1, :] = values[:, MIG:]


def move_kernel(near, other, tiles_in, cell_in, keep, vel_in, rate_in, out, tiles, cell, vel, rate, sems):
    moves = ((tiles_in, tiles), (cell_in, cell), (vel_in, vel), (rate_in, rate))
    copies = [pltpu.make_async_copy(a, b, sems.at[i]) for i, (a, b) in enumerate(moves)]
    for copy in copies:
        copy.start()
    for copy in copies:
        copy.wait()
    c = lax.axis_index("c")
    iota16 = rows_iota(16, TP)
    iota128 = rows_iota(128, TP)

    def pair(ref, t):
        return jnp.concatenate([ref[pl.ds(2 * t, 1), :], ref[pl.ds(2 * t + 1, 1), :]], axis=1)

    def one_tile(t):
        block = tiles[t]
        row, col = block >> 4, block & 7
        here = jnp.where((block >> 3) & 1 == c, near[row, col], other[row, col])
        cells = pair(cell, t)
        low = jnp.where(iota128 == (cells & 127), F32(1.0), F32(0.0)).astype(BF16)
        picked = dot_nn(here, low)
        mask = iota16 == hi_of(cells)
        sampled = [
            jnp.sum(jnp.where(mask, picked[16 * k : 16 * k + 16], 0.0), axis=0, keepdims=True)
            for k in range(4)
        ]
        lanes = pl.ds(pl.multiple_of(t * TP, TP), TP)
        moved = step_parcel([vel[k : k + 1, lanes] for k in range(3)], pair(rate, t), sampled)
        stays = pair(keep, t)
        for k in range(3):
            out[k : k + 1, lanes] = moved[k] * stays

    def some(i, carry):
        for u in range(4):
            one_tile(i * 4 + u)
        return carry

    lax.fori_loop(0, TILES // 4, some, 0)


def per_device(
    fluid_vel,
    pressure,
    parcel_vel,
    parcel_vol,
    parcel_rate,
    cell_local,
    tile_block,
    parcel_count,
    leave_lists,
    mig_counts,
):
    vol = parcel_vol.reshape(ROWS, 128)
    rate = parcel_rate.reshape(ROWS, 128)
    cell = cell_local.reshape(ROWS, 128)
    tiles = tile_block.reshape(1, TILES)
    plane = (RADIAL, LINE)
    pay, fpay, keep = call(
        pack_kernel,
        [((PAY_ROWS, 128), BF16), ((9,) + plane, F32), ((ROWS, 128), F32)],
        [parcel_vel, vol, rate, cell, tiles, parcel_count, leave_lists, mig_counts.reshape(1, 2), fluid_vel, pressure],
        scratch=[
            pltpu.VMEM((3, PCAP), F32),
            pltpu.VMEM((ROWS, 128), F32),
            pltpu.VMEM((ROWS, 128), F32),
            pltpu.VMEM((ROWS, 128), I32),
            pltpu.VMEM((1, TILES), I32),
            pltpu.SMEM((1,), I32),
            pltpu.VMEM((2, MIG), I32),
            pltpu.VMEM((1, 2), I32),
            pltpu.VMEM((3, ROWS, 128), F32),
            pltpu.VMEM((16, 128), F32),
            pltpu.SemaphoreType.DMA((12,)),
        ],
        hbm=range(10),
        limit=PACK_LIMIT,
    )
    pay_far = swap(pay, "z")
    fpay_far = swap(fpay, "z")
    pay_pair, pays = call(
        spread_kernel,
        [((N_Z, PAY_ROWS, 128), BF16), ((N_Y, N_Z, PAY_ROWS, 128), BF16)],
        [pay, pay_far],
    )
    pays = lax.all_to_all(pays, "y", 0, 0)
    deposit_scratch = [
        pltpu.VMEM((SOURCES * SCR_ROWS, 128), F32),
        pltpu.VMEM((SOURCES, 128), I32),
        pltpu.SMEM((SOURCES, 128), I32),
        pltpu.SMEM((LIST_CAP,), I32),
        pltpu.SemaphoreType.DMA,
    ]
    sums_shape = (OWN_BLOCKS + 1, 80, 128)
    (sums,) = call(
        first_deposit_kernel,
        [(sums_shape, F32)],
        [pay_pair],
        scratch=deposit_scratch,
        flops=1 << 36,
    )
    (sums,) = call(
        functools.partial(next_deposit_kernel, True),
        [(sums_shape, F32)],
        [pays.reshape(SOURCES, PAY_ROWS, 128), sums],
        scratch=deposit_scratch,
        flops=1 << 36,
    )
    pays_c = swap(pays, "c")
    fpay_far, sums = lax.optimization_barrier((fpay_far, sums))
    edge, side = call(
        edge_kernel, [((4,) + plane, F32), ((9,) + plane, F32)], [fpay, fpay_far]
    )
    route = halo_route()
    side = swap(side, "c")
    edge = lax.ppermute(edge, ALL, route)
    (sums,) = call(
        functools.partial(next_deposit_kernel, False),
        [(sums_shape, F32)],
        [pays_c.reshape(SOURCES, PAY_ROWS, 128), sums],
        scratch=deposit_scratch,
        flops=1 << 36,
    )
    u_star, porosity, flux_y, flux_c = call(
        velocity_kernel,
        [((3, 4) + plane, F32), ((4,) + plane, F32), ((12,) + plane, F32), ((9,) + plane, F32)],
        [sums, fpay, fpay_far, side, edge],
        scratch=[pltpu.VMEM((4, 6) + plane, F32), pltpu.VMEM((3, 4) + plane, F32)],
    )
    from_y = lax.ppermute(flux_y, ALL, route)
    from_c = lax.all_gather(flux_c, "c", axis=0)
    fields, kept, sent = call(
        fluid_kernel,
        [((N_Y, OWN_BLOCKS, 64, 128), BF16), ((4, 2) + plane, F32), ((4, 2) + plane, F32)],
        [u_star, porosity, fpay, fpay_far, side, from_y, from_c],
        scratch=[
            pltpu.VMEM((3, 10) + plane, F32),
            pltpu.VMEM((10,) + plane, F32),
            pltpu.VMEM((4, 4) + plane, F32),
        ],
    )
    fields = lax.all_to_all(fields, "y", 0, 0)
    fields_c = swap(fields, "c")
    swapped = swap(sent, "c")
    mine = lax.axis_index("c") == lax.axis_index("z")
    out0, out1 = call(
        leave_kernel,
        [((5, MIG), F32), ((5, MIG), F32)],
        [fields, fields_c, fpay, fpay_far],
        flops=1 << 30,
    )
    arrive0 = lax.ppermute(out0, ALL, leave_route(-1))
    arrive1 = lax.ppermute(out1, ALL, leave_route(1))
    (parcel_next,) = call(
        move_kernel,
        [((3, PCAP), F32)],
        [fields, fields_c, tile_block, cell, keep, parcel_vel, rate],
        scratch=[
            pltpu.SMEM((TILES,), I32),
            pltpu.VMEM((ROWS, 128), I32),
            pltpu.VMEM((3, PCAP), F32),
            pltpu.VMEM((ROWS, 128), F32),
            pltpu.SemaphoreType.DMA((4,)),
        ],
        hbm=(2, 3, 5, 6),
        flops=1 << 31,
    )
    fluid_next = jnp.where(mine, kept[:3], swapped[:3])
    pressure_next = jnp.where(mine, kept[3], swapped[3])
    arrivals = jnp.stack([arrive0, arrive1], axis=1).transpose(1, 0, 2)
    return fluid_next, pressure_next, parcel_next, arrivals


def solution(mesh):
    fine = Mesh(mesh.devices.reshape(N_BLK, N_Y, N_Z, N_C), ALL)
    placed = (
        P(None, ALL, None, None),
        P(ALL, None, None),
        P(None, ALL),
        P(ALL),
        P(ALL),
        P(ALL),
        P(ALL),
        P(ALL),
        P(None, ALL),
        P(None, ALL),
    )
    return jax.shard_map(
        per_device,
        mesh=fine,
        in_specs=placed,
        out_specs=(
            P(None, ALL, None, None),
            P(ALL, None, None),
            P(None, ALL),
            P(None, None, ALL),
        ),
        check_vma=False,
    )
```

```python
import functools

import jax
import jax.numpy as jnp
from jax import lax
from jax.experimental import pallas as pl
from jax.experimental.pallas import tpu as pltpu
from jax.sharding import Mesh, PartitionSpec as P

PCAP = 8192
TP = 256
TILES = PCAP // TP
ROWS = PCAP // 128
BLOCK = 2048
RADIAL = 16
LINE = 256
MIG = 256
N_BLK, N_Y, N_Z, N_C = 32, 4, 2, 2
Z_LO = 8
ALL = ("blk", "y", "z", "c")

DT = 0.2
NU = 0.5

PAY_ROWS = 6 * ROWS + 16
SCR_ROWS = 7 * ROWS
SOURCES = N_Y * N_Z
OWN_BLOCKS = 8
UNROLL = 4
LIST_CAP = SOURCES * TILES + UNROLL

PACK_LIMIT = 56 << 20

F32 = jnp.float32
BF16 = jnp.bfloat16
I32 = jnp.int32


def flat(blk, y, z, c):
    return ((blk * N_Y + y) * N_Z + z) * N_C + c


def every_place():
    for blk in range(N_BLK):
        for y in range(N_Y):
            for z in range(N_Z):
                for c in range(N_C):
                    yield blk, y, z, c


def halo_route():
    pairs = []
    for blk, y, z, c in every_place():
        if c == 1:
            here = flat(blk, y, z, 1)
            if y < N_Y - 1:
                there = flat(blk, y + 1, z, 0)
            else:
                crossing = blk % Z_LO == Z_LO - 1
                there = flat((blk + 1) % N_BLK, 0, 1 - z if crossing else z, 0)
            pairs += [(here, there), (there, here)]
    return pairs


def leave_route(step):
    edge = 0 if step < 0 else Z_LO - 1
    pairs = []
    for blk, y, z, c in every_place():
        sender = flat(blk, y, 1 - z if blk % Z_LO == edge else z, c)
        pairs.append((sender, flat((blk + step) % N_BLK, y, z, c)))
    return pairs


def swap(values, axis):
    return lax.ppermute(values, axis, [(0, 1), (1, 0)])


def call(kernel, outs, ins, scratch=(), smem=(), hbm=(), limit=16 << 20, flops=0):
    def space(i):
        return pltpu.SMEM if i in smem else pltpu.HBM if i in hbm else pltpu.VMEM

    specs = [pl.BlockSpec(memory_space=space(i)) for i in range(len(ins))]
    return pl.pallas_call(
        kernel,
        out_shape=[jax.ShapeDtypeStruct(shape, dtype) for shape, dtype in outs],
        in_specs=specs,
        out_specs=[pl.BlockSpec(memory_space=pltpu.VMEM) for _ in outs],
        scratch_shapes=list(scratch),
        compiler_params=pltpu.CompilerParams(vmem_limit_bytes=limit),
        cost_estimate=pl.CostEstimate(flops=flops, bytes_accessed=1 << 20, transcendentals=0),
    )(*ins)


def rows_iota(rows, lanes):
    return lax.broadcasted_iota(I32, (rows, lanes), 0)


def dot_nt(a, b):
    return lax.dot_general(a, b, (((1,), (1,)), ((), ())), preferred_element_type=F32)


def dot_nn(a, b):
    return lax.dot_general(a, b, (((1,), (0,)), ((), ())), preferred_element_type=F32)


def hi_of(cell):
    return ((cell >> 7) & 1) * 8 + (cell >> 8)


def pack_kernel(*refs):
    sources, (pay, fpay, keep), (vel, vol, rate, cell, tiles, count, lists, mig, vsc, tsc, sems) = (
        refs[:10],
        refs[10:13],
        refs[13:],
    )
    fluid, press = sources[8:]
    targets = [vel, vol, rate, cell, tiles, count, lists, mig]
    targets += [fpay.at[2 * k : 2 * k + 2] for k in range(3)] + [fpay.at[6:8]]
    origins = list(sources[:8]) + [fluid.at[k] for k in range(3)] + [press]
    copies = [
        pltpu.make_async_copy(origin, target, sems.at[i])
        for i, (origin, target) in enumerate(zip(origins, targets))
    ]
    for copy in copies:
        copy.start()
    for copy in copies:
        copy.wait()
    for r in range(ROWS):
        for k in range(3):
            vsc[k, r : r + 1, :] = vel[k : k + 1, r * 128 : (r + 1) * 128]
    slot = rows_iota(ROWS, 128) * 128 + lax.broadcasted_iota(I32, (ROWS, 128), 1)
    active = (slot < count[0]).astype(F32)
    drag = vol[...] * rate[...]
    pay[0:ROWS, :] = (vol[...] * active).astype(BF16)
    pay[ROWS : 2 * ROWS, :] = (drag * active).astype(BF16)
    for k in range(3):
        pay[(2 + k) * ROWS : (3 + k) * ROWS, :] = (drag * vsc[k] * active).astype(BF16)
    cells = cell[...]
    hi = hi_of(cells)
    code = ((cells & 127) + 128).astype(F32)
    for bit in range(4):
        code = code * jnp.where((hi >> bit) & 1 == 1, F32(2.0 ** (1 << bit)), F32(1.0))
    pay[5 * ROWS : 6 * ROWS, :] = code.astype(BF16)
    lane = lax.broadcasted_iota(I32, (1, TILES), 1)
    tsc[...] = jnp.zeros((16, 128), F32)
    tsc[0:1, 0:TILES] = tiles[...].astype(F32)
    raw_tiles = tsc[...].astype(BF16)
    tsc[0:1, 0:TILES] = jnp.where(lane * TP < count[0], tiles[...].astype(F32), 255.0)
    pay[6 * ROWS : 6 * ROWS + 16, :] = tsc[...].astype(BF16)
    slots = jnp.concatenate([lists[0:1, :], lists[1:2, :]], axis=1)
    lane512 = lax.broadcasted_iota(I32, (1, 2 * MIG), 1)
    ends = jnp.where(lane512 < MIG, mig[:, 0:1], mig[:, 1:2] + MIG)
    valid = jnp.where(lane512 < ends, F32(1.0), F32(0.0))
    low = (rows_iota(128, 2 * MIG) == (slots & 127)).astype(F32).astype(BF16)
    row_mask = rows_iota(ROWS, 2 * MIG) == (slots >> 7)
    counts = dot_nt(jnp.where(row_mask, valid, 0.0).astype(BF16), low)
    keep[...] = active * jnp.where(counts > 0.5, 0.0, 1.0)

    def picked(values, parts):
        total = None
        for _ in range(parts):
            piece = values.astype(BF16)
            values = values - piece.astype(F32)
            term = dot_nn(piece, low)
            total = term if total is None else total + term
        return jnp.sum(jnp.where(row_mask, total, 0.0), axis=0, keepdims=True)

    def put(row, values):
        fpay[8, row : row + 1, :] = values[:, :MIG]
        fpay[8, 8 + row : 9 + row, :] = values[:, MIG:]

    for k in range(3):
        put(k, picked(vsc[k], 3))
    put(3, picked(vol[...], 3))
    put(4, picked(rate[...], 3))
    tile_hot = (rows_iota(128, 2 * MIG) == (slots >> 8)).astype(F32).astype(BF16)
    block = dot_nn(raw_tiles, tile_hot)[0:1, :]
    cell_hi = picked((cells >> 7).astype(F32), 1)
    cell_lo = picked((cells & 127).astype(F32), 1)
    put(5, block * BLOCK + cell_hi * 128.0 + cell_lo)
    put(6, valid)
    put(7, jnp.zeros_like(valid))


def edge_kernel(own, far, edge, side):
    c = lax.axis_index("c")
    native = lax.axis_index("z") == c
    for k in range(4):
        edge[k] = jnp.where(native, own[2 * k + c], far[2 * k + c])
        for i in range(2):
            side[2 * k + i] = jnp.where(native, far[2 * k + i], own[2 * k + i])
    side[8] = jnp.where(native, own[7 - c], far[7 - c])


def at(values, axis, step):
    size = values.shape[axis]
    moved = pltpu.roll(values, (-step) % size, axis)
    place = lax.broadcasted_iota(I32, values.shape, axis)
    return jnp.where(place == (size - 1 if step > 0 else 0), 0.0, moved)


def rad_up(values):
    return at(values, values.ndim - 2, 1)


def rad_down(values):
    return at(values, values.ndim - 2, -1)


def axial_up(values):
    return at(values, values.ndim - 1, 1)


def axial_down(values):
    return at(values, values.ndim - 1, -1)


def add_deposits(pays, acc, scr, tile_v, tile_s, picks, sem, skip_own=False):
    y = lax.axis_index("y")
    first = y * 16 + lax.axis_index("c") * OWN_BLOCKS
    sources = pays.shape[0]
    for s in range(sources):
        tile_v[s : s + 1, :] = pays[s, 6 * ROWS : 6 * ROWS + 16, :].astype(F32)[0:1, :].astype(I32)
    copy = pltpu.make_async_copy(tile_v, tile_s, sem)
    copy.start()

    def widen(s, carry):
        base = pl.multiple_of(s * SCR_ROWS, 8)
        scr[pl.ds(base, 5 * ROWS), :] = pays[s, 0 : 5 * ROWS, :].astype(F32)
        code = pays[s, 5 * ROWS : 6 * ROWS, :].astype(F32)
        hi = jnp.zeros_like(code)
        for step in (8, 4, 2, 1):
            large = code >= 2.0 ** (7 + step)
            code = jnp.where(large, code * 2.0**-step, code)
            hi = hi + jnp.where(large, F32(step), 0.0)
        scr[pl.ds(base + 5 * ROWS, ROWS), :] = hi
        scr[pl.ds(base + 6 * ROWS, ROWS), :] = code - 128.0
        return carry

    lax.fori_loop(0, sources, widen, 0)
    copy.wait()

    def choose(s, found):
        base = first + jnp.where(s // N_Z == y, 1024, 0) if skip_own else first
        for t in range(TILES):
            block = tile_s[s, t] - base
            picks[found] = (s * SCR_ROWS + 2 * t) * 16 + block
            mine = jnp.logical_and(block >= 0, block < OWN_BLOCKS)
            found = found + mine.astype(I32)
        return found

    found = lax.fori_loop(0, sources, choose, jnp.int32(0))
    for i in range(UNROLL):
        picks[found + i] = OWN_BLOCKS
    iota16 = lax.broadcasted_iota(I32, (16, 128), 0).astype(F32)
    iota128 = lax.broadcasted_iota(I32, (128, 128), 0).astype(F32)

    def one_tile(code):
        block = code & 15
        base = code >> 4
        left, right = [], []
        for h in range(2):
            hi = scr[pl.ds(base + 5 * ROWS + h, 1), :]
            lo = scr[pl.ds(base + 6 * ROWS + h, 1), :]
            mask = iota16 == hi
            parts = [
                jnp.where(mask, scr[pl.ds(base + k * ROWS + h, 1), :], 0.0).astype(BF16)
                for k in range(5)
            ]
            left.append(jnp.concatenate(parts, axis=0))
            right.append(jnp.where(iota128 == lo, F32(1.0), F32(0.0)).astype(BF16))
        sums = dot_nt(jnp.concatenate(left, axis=1), jnp.concatenate(right, axis=1))
        return block, sums

    def deposit(i, carry):
        done = [one_tile(picks[i * UNROLL + u]) for u in range(UNROLL)]
        for block, sums in done:
            acc[block] = acc[block] + sums
        return carry

    lax.fori_loop(0, (found + UNROLL - 1) // UNROLL, deposit, 0)


def first_deposit_kernel(pays, acc, *scratch):
    acc[...] = jnp.zeros_like(acc)
    add_deposits(pays, acc, *scratch)


def next_deposit_kernel(skip_own, pays, before, acc, *scratch):
    acc[...] = before[...]
    add_deposits(pays, acc, *scratch, skip_own=skip_own)


def spread_kernel(own, far, both, out):
    both[0] = own[...]
    both[1] = far[...]
    for y in range(N_Y):
        out[y, 0] = own[...]
        out[y, 1] = far[...]


def velocity_kernel(acc, own, far, side, edge, u_out, por_out, flux_y, flux_c, wide, flux):
    c = lax.axis_index("c")
    native = lax.axis_index("z") == c

    def amount(k):
        halves = []
        for b in range(OWN_BLOCKS):
            halves.append(
                jnp.concatenate([acc[b, k * 16 : k * 16 + 8, :], acc[b, k * 16 + 8 : k * 16 + 16, :]], axis=1)
            )
        return jnp.stack(
            [jnp.concatenate([halves[2 * i], halves[2 * i + 1]], axis=0) for i in range(4)]
        )

    for k in range(4):
        wide[k, 5 * c] = edge[k]
        for i in range(2):
            wide[k, 1 + 2 * c + i] = jnp.where(native, own[2 * k + i], far[2 * k + i])
            wide[k, 3 - 2 * c + i] = side[2 * k + i]
        wide[k, 5 * (1 - c)] = jnp.where(native, far[2 * k + c], own[2 * k + c])
    porosity = 1.0 / (1.0 + amount(0))
    por_out[...] = porosity
    below = 1.0 + DT * amount(1) / porosity
    centre = wide[3, 1:5]
    slopes = [
        0.5 * (wide[3, 2:6] - wide[3, 0:4]),
        0.5 * (rad_up(centre) - rad_down(centre)),
        0.5 * (axial_up(centre) - axial_down(centre)),
    ]
    for k in range(3):
        v = wide[k, 1:5]
        lap = (
            wide[k, 2:6] + wide[k, 0:4] + rad_up(v) + rad_down(v) + axial_up(v) + axial_down(v) - 6.0 * v
        )
        u = (v + DT * (NU * lap - slopes[k]) + DT * amount(2 + k) / porosity) / below
        u_out[k] = u
        flux[k] = porosity * u
    for i in range(3):
        for k in range(3):
            flux_y[3 * k + i] = flux[k, c + i]
            flux_c[3 * k + i] = flux[k, 1 - c + i]
        flux_y[9 + i] = wide[3, 1 + c + i]


def fluid_kernel(
    u_in, por_in, own, far, side, from_y, from_c, fields, kept, sent, flux, pres, out
):
    c = lax.axis_index("c")
    native = lax.axis_index("z") == c
    for k in range(3):
        flux[k, 3:7] = por_in[...] * u_in[k]
        for i in range(3):
            flux[k, 7 * c + i] = from_y[3 * k + i]
            flux[k, 7 * (1 - c) + i] = from_c[1 - c, 3 * k + i]
    for i in range(3):
        pres[7 * c + i] = from_y[9 + i]
    for i in range(2):
        pres[3 + 2 * c + i] = jnp.where(native, own[6 + i], far[6 + i])
        pres[5 - 2 * c + i] = side[6 + i]
        pres[7 - 6 * c + i] = jnp.where(native, far[6 + i], own[6 + i])
    pres[9 * (1 - c)] = side[8]
    f1 = flux[1, 1:9]
    f2 = flux[2, 1:9]
    source = 0.5 * (
        flux[0, 2:10] - flux[0, 0:8] + rad_up(f1) - rad_down(f1) + axial_up(f2) - axial_down(f2)
    )

    def sweep(p, s):
        centre = p[1:-1]
        return (
            p[2:]
            + p[:-2]
            + rad_up(centre)
            + rad_down(centre)
            + axial_up(centre)
            + axial_down(centre)
            - s / DT
        ) / 6.0

    p1 = sweep(pres[...], source)
    p2 = sweep(p1, source[1:-1])
    centre = p2[1:-1]
    slopes = [
        0.5 * (p2[2:] - p2[:-2]),
        0.5 * (rad_up(centre) - rad_down(centre)),
        0.5 * (axial_up(centre) - axial_down(centre)),
    ]
    for k in range(3):
        out[k] = u_in[k] - DT * slopes[k]
    out[3] = centre
    for k in range(4):
        for i in range(4):
            plane = out[k, i] if k < 3 else por_in[i]
            for h in range(2):
                half = plane[8 * h : 8 * h + 8]
                both = jnp.concatenate([half[:, :128], half[:, 128:]], axis=0)
                for copy in range(N_Y):
                    fields[copy, 2 * i + h, 16 * k : 16 * k + 16, :] = both.astype(BF16)
    for k in range(4):
        for i in range(2):
            kept[k, i] = out[k, 2 * c + i]
            sent[k, i] = out[k, 2 * (1 - c) + i]


def step_parcel(vel, rate, sampled):
    coupling = rate / (sampled[3] * sampled[3])
    pull = DT * coupling
    below = 1.0 + pull
    return [(vel[k] + pull * sampled[k]) / below for k in range(3)]


def leave_lists_of(own, far):
    z_lo = lax.rem(lax.axis_index("blk"), Z_LO)
    list0 = jnp.where(z_lo == 0, far[8, 0:8, :], own[8, 0:8, :])
    list1 = jnp.where(z_lo == Z_LO - 1, far[8, 8:16, :], own[8, 8:16, :])
    return jnp.concatenate([list0, list1], axis=1)


def sample_lists(fields, core, both, total):
    place = both[5:6, :].astype(I32)
    block = place >> 11
    low = (rows_iota(128, 2 * MIG) == (place & 127)).astype(F32).astype(BF16)

    def gather(i, total):
        for u in range(OWN_BLOCKS):
            picked = dot_nn(fields[i, u], low)
            total = total + jnp.where(block == i * 16 + core * OWN_BLOCKS + u, picked, 0.0)
        return total

    return lax.fori_loop(0, N_Y, gather, total)


def first_leave_kernel(near, own, far, out):
    start = jnp.zeros((64, 2 * MIG), F32)
    out[...] = sample_lists(near, lax.axis_index("c"), leave_lists_of(own, far), start)


def last_leave_kernel(other, own, far, half, out0, out1):
    both = leave_lists_of(own, far)
    total = sample_lists(other, 1 - lax.axis_index("c"), both, half[...])
    mask = rows_iota(16, 2 * MIG) == hi_of(both[5:6, :].astype(I32) & (BLOCK - 1))
    sampled = [
        jnp.sum(jnp.where(mask, total[16 * k : 16 * k + 16], 0.0), axis=0, keepdims=True)
        for k in range(4)
    ]
    sampled[3] = jnp.where(both[6:7, :] > 0.5, sampled[3], 1.0)
    vol, rate, valid = both[3:4, :], both[4:5, :], both[6:7, :]
    moved = step_parcel([both[k : k + 1, :] for k in range(3)], rate, sampled)
    for k, values in enumerate(moved + [vol, rate]):
        values = values * valid
        out0[k : k + 1, :] = values[:, :MIG]
        out1[k : k + 1, :] = values[:, MIG:]


def move_kernel(near, other, tiles_in, cell_in, keep, vel_in, rate_in, out, tiles, cell, vel, rate, sems):
    moves = ((tiles_in, tiles), (cell_in, cell), (vel_in, vel), (rate_in, rate))
    copies = [pltpu.make_async_copy(a, b, sems.at[i]) for i, (a, b) in enumerate(moves)]
    for copy in copies:
        copy.start()
    for copy in copies:
        copy.wait()
    c = lax.axis_index("c")
    iota16 = rows_iota(16, TP)
    iota128 = rows_iota(128, TP)

    def pair(ref, t):
        return jnp.concatenate([ref[pl.ds(2 * t, 1), :], ref[pl.ds(2 * t + 1, 1), :]], axis=1)

    def one_tile(t):
        block = tiles[t]
        row, col = block >> 4, block & 7
        here = jnp.where((block >> 3) & 1 == c, near[row, col], other[row, col])
        cells = pair(cell, t)
        low = jnp.where(iota128 == (cells & 127), F32(1.0), F32(0.0)).astype(BF16)
        picked = dot_nn(here, low)
        mask = iota16 == hi_of(cells)
        sampled = [
            jnp.sum(jnp.where(mask, picked[16 * k : 16 * k + 16], 0.0), axis=0, keepdims=True)
            for k in range(4)
        ]
        lanes = pl.ds(pl.multiple_of(t * TP, TP), TP)
        moved = step_parcel([vel[k : k + 1, lanes] for k in range(3)], pair(rate, t), sampled)
        stays = pair(keep, t)
        for k in range(3):
            out[k : k + 1, lanes] = moved[k] * stays

    def some(i, carry):
        for u in range(4):
            one_tile(i * 4 + u)
        return carry

    lax.fori_loop(0, TILES // 4, some, 0)


def per_device(
    fluid_vel,
    pressure,
    parcel_vel,
    parcel_vol,
    parcel_rate,
    cell_local,
    tile_block,
    parcel_count,
    leave_lists,
    mig_counts,
):
    vol = parcel_vol.reshape(ROWS, 128)
    rate = parcel_rate.reshape(ROWS, 128)
    cell = cell_local.reshape(ROWS, 128)
    tiles = tile_block.reshape(1, TILES)
    plane = (RADIAL, LINE)
    pay, fpay, keep = call(
        pack_kernel,
        [((PAY_ROWS, 128), BF16), ((9,) + plane, F32), ((ROWS, 128), F32)],
        [parcel_vel, vol, rate, cell, tiles, parcel_count, leave_lists, mig_counts.reshape(1, 2), fluid_vel, pressure],
        scratch=[
            pltpu.VMEM((3, PCAP), F32),
            pltpu.VMEM((ROWS, 128), F32),
            pltpu.VMEM((ROWS, 128), F32),
            pltpu.VMEM((ROWS, 128), I32),
            pltpu.VMEM((1, TILES), I32),
            pltpu.SMEM((1,), I32),
            pltpu.VMEM((2, MIG), I32),
            pltpu.VMEM((1, 2), I32),
            pltpu.VMEM((3, ROWS, 128), F32),
            pltpu.VMEM((16, 128), F32),
            pltpu.SemaphoreType.DMA((12,)),
        ],
        hbm=range(10),
        limit=PACK_LIMIT,
    )
    pay_far = swap(pay, "z")
    fpay_far = swap(fpay, "z")
    pay_pair, pays = call(
        spread_kernel,
        [((N_Z, PAY_ROWS, 128), BF16), ((N_Y, N_Z, PAY_ROWS, 128), BF16)],
        [pay, pay_far],
    )
    pays = lax.all_to_all(pays, "y", 0, 0)
    deposit_scratch = [
        pltpu.VMEM((SOURCES * SCR_ROWS, 128), F32),
        pltpu.VMEM((SOURCES, 128), I32),
        pltpu.SMEM((SOURCES, 128), I32),
        pltpu.SMEM((LIST_CAP,), I32),
        pltpu.SemaphoreType.DMA,
    ]
    sums_shape = (OWN_BLOCKS + 1, 80, 128)
    (sums,) = call(
        first_deposit_kernel,
        [(sums_shape, F32)],
        [pay_pair],
        scratch=deposit_scratch,
        flops=1 << 36,
    )
    (sums,) = call(
        functools.partial(next_deposit_kernel, True),
        [(sums_shape, F32)],
        [pays.reshape(SOURCES, PAY_ROWS, 128), sums],
        scratch=deposit_scratch,
        flops=1 << 36,
    )
    pays_c = swap(pays, "c")
    edge, side = call(
        edge_kernel, [((4,) + plane, F32), ((9,) + plane, F32)], [fpay, fpay_far]
    )
    route = halo_route()
    side = swap(side, "c")
    edge = lax.ppermute(edge, ALL, route)
    (sums,) = call(
        functools.partial(next_deposit_kernel, False),
        [(sums_shape, F32)],
        [pays_c.reshape(SOURCES, PAY_ROWS, 128), sums],
        scratch=deposit_scratch,
        flops=1 << 36,
    )
    u_star, porosity, flux_y, flux_c = call(
        velocity_kernel,
        [((3, 4) + plane, F32), ((4,) + plane, F32), ((12,) + plane, F32), ((9,) + plane, F32)],
        [sums, fpay, fpay_far, side, edge],
        scratch=[pltpu.VMEM((4, 6) + plane, F32), pltpu.VMEM((3, 4) + plane, F32)],
    )
    from_y = lax.ppermute(flux_y, ALL, route)
    from_c = lax.all_gather(flux_c, "c", axis=0)
    fields, kept, sent = call(
        fluid_kernel,
        [((N_Y, OWN_BLOCKS, 64, 128), BF16), ((4, 2) + plane, F32), ((4, 2) + plane, F32)],
        [u_star, porosity, fpay, fpay_far, side, from_y, from_c],
        scratch=[
            pltpu.VMEM((3, 10) + plane, F32),
            pltpu.VMEM((10,) + plane, F32),
            pltpu.VMEM((4, 4) + plane, F32),
        ],
    )
    fields = lax.all_to_all(fields, "y", 0, 0)
    fields_c = swap(fields, "c")
    swapped = swap(sent, "c")
    mine = lax.axis_index("c") == lax.axis_index("z")
    (half,) = call(
        first_leave_kernel,
        [((64, 2 * MIG), F32)],
        [fields, fpay, fpay_far],
        flops=1 << 36,
    )
    out0, out1 = call(
        last_leave_kernel,
        [((5, MIG), F32), ((5, MIG), F32)],
        [fields_c, fpay, fpay_far, half],
    )
    arrive0 = lax.ppermute(out0, ALL, leave_route(-1))
    arrive1 = lax.ppermute(out1, ALL, leave_route(1))
    (parcel_next,) = call(
        move_kernel,
        [((3, PCAP), F32)],
        [fields, fields_c, tile_block, cell, keep, parcel_vel, rate],
        scratch=[
            pltpu.SMEM((TILES,), I32),
            pltpu.VMEM((ROWS, 128), I32),
            pltpu.VMEM((3, PCAP), F32),
            pltpu.VMEM((ROWS, 128), F32),
            pltpu.SemaphoreType.DMA((4,)),
        ],
        hbm=(2, 3, 5, 6),
        flops=1 << 31,
    )
    kept, swapped, parcel_next = lax.optimization_barrier((kept, swapped, parcel_next))
    fluid_next = jnp.where(mine, kept[:3], swapped[:3])
    pressure_next = jnp.where(mine, kept[3], swapped[3])
    arrivals = jnp.stack([arrive0, arrive1], axis=1).transpose(1, 0, 2)
    return fluid_next, pressure_next, parcel_next, arrivals


def solution(mesh):
    fine = Mesh(mesh.devices.reshape(N_BLK, N_Y, N_Z, N_C), ALL)
    placed = (
        P(None, ALL, None, None),
        P(ALL, None, None),
        P(None, ALL),
        P(ALL),
        P(ALL),
        P(ALL),
        P(ALL),
        P(ALL),
        P(None, ALL),
        P(None, ALL),
    )
    return jax.shard_map(
        per_device,
        mesh=fine,
        in_specs=placed,
        out_specs=(
            P(None, ALL, None, None),
            P(ALL, None, None),
            P(None, ALL),
            P(None, None, ALL),
        ),
        check_vma=False,
    )
```

```python
import functools

import jax
import jax.numpy as jnp
from jax import lax
from jax.experimental import pallas as pl
from jax.experimental.pallas import tpu as pltpu
from jax.sharding import Mesh, PartitionSpec as P

PCAP = 8192
TP = 256
TILES = PCAP // TP
ROWS = PCAP // 128
BLOCK = 2048
RADIAL = 16
LINE = 256
MIG = 256
N_BLK, N_Y, N_Z, N_C = 32, 4, 2, 2
Z_LO = 8
ALL = ("blk", "y", "z", "c")

DT = 0.2
NU = 0.5

PAY_ROWS = 6 * ROWS + 16
SCR_ROWS = 7 * ROWS
SOURCES = N_Y * N_Z
OWN_BLOCKS = 8
UNROLL = 8
LIST_CAP = SOURCES * TILES + UNROLL

PACK_LIMIT = 56 << 20

F32 = jnp.float32
BF16 = jnp.bfloat16
I32 = jnp.int32


def flat(blk, y, z, c):
    return ((blk * N_Y + y) * N_Z + z) * N_C + c


def every_place():
    for blk in range(N_BLK):
        for y in range(N_Y):
            for z in range(N_Z):
                for c in range(N_C):
                    yield blk, y, z, c


def halo_route():
    pairs = []
    for blk, y, z, c in every_place():
        if c == 1:
            here = flat(blk, y, z, 1)
            if y < N_Y - 1:
                there = flat(blk, y + 1, z, 0)
            else:
                crossing = blk % Z_LO == Z_LO - 1
                there = flat((blk + 1) % N_BLK, 0, 1 - z if crossing else z, 0)
            pairs += [(here, there), (there, here)]
    return pairs


def leave_route(step):
    edge = 0 if step < 0 else Z_LO - 1
    pairs = []
    for blk, y, z, c in every_place():
        sender = flat(blk, y, 1 - z if blk % Z_LO == edge else z, c)
        pairs.append((sender, flat((blk + step) % N_BLK, y, z, c)))
    return pairs


def swap(values, axis):
    return lax.ppermute(values, axis, [(0, 1), (1, 0)])


def call(kernel, outs, ins, scratch=(), smem=(), hbm=(), limit=16 << 20, flops=0):
    def space(i):
        return pltpu.SMEM if i in smem else pltpu.HBM if i in hbm else pltpu.VMEM

    specs = [pl.BlockSpec(memory_space=space(i)) for i in range(len(ins))]
    return pl.pallas_call(
        kernel,
        out_shape=[jax.ShapeDtypeStruct(shape, dtype) for shape, dtype in outs],
        in_specs=specs,
        out_specs=[pl.BlockSpec(memory_space=pltpu.VMEM) for _ in outs],
        scratch_shapes=list(scratch),
        compiler_params=pltpu.CompilerParams(vmem_limit_bytes=limit),
        cost_estimate=pl.CostEstimate(flops=flops, bytes_accessed=1 << 20, transcendentals=0),
    )(*ins)


def rows_iota(rows, lanes):
    return lax.broadcasted_iota(I32, (rows, lanes), 0)


def dot_nt(a, b):
    return lax.dot_general(a, b, (((1,), (1,)), ((), ())), preferred_element_type=F32)


def dot_nn(a, b):
    return lax.dot_general(a, b, (((1,), (0,)), ((), ())), preferred_element_type=F32)


def hi_of(cell):
    return ((cell >> 7) & 1) * 8 + (cell >> 8)


def load_all(pairs, sems):
    copies = [pltpu.make_async_copy(a, b, sems.at[i]) for i, (a, b) in enumerate(pairs)]
    for copy in copies:
        copy.start()
    for copy in copies:
        copy.wait()


def fold_rows(vel, vsc):
    for r in range(ROWS):
        for k in range(3):
            vsc[k, r : r + 1, :] = vel[k : k + 1, r * 128 : (r + 1) * 128]


def active_slots(count):
    slot = rows_iota(ROWS, 128) * 128 + lax.broadcasted_iota(I32, (ROWS, 128), 1)
    return (slot < count[0]).astype(F32)


def pack_kernel(*refs):
    sources, pay, held, (vsc, tsc, sems) = refs[:6], refs[6], refs[7:13], refs[13:]
    vel, vol, rate, cell, tiles, count = held
    load_all(list(zip(sources, held)), sems)
    fold_rows(vel, vsc)
    active = active_slots(count)
    drag = vol[...] * rate[...]
    pay[0:ROWS, :] = (vol[...] * active).astype(BF16)
    pay[ROWS : 2 * ROWS, :] = (drag * active).astype(BF16)
    for k in range(3):
        pay[(2 + k) * ROWS : (3 + k) * ROWS, :] = (drag * vsc[k] * active).astype(BF16)
    cells = cell[...]
    hi = hi_of(cells)
    code = ((cells & 127) + 128).astype(F32)
    for bit in range(4):
        code = code * jnp.where((hi >> bit) & 1 == 1, F32(2.0 ** (1 << bit)), F32(1.0))
    pay[5 * ROWS : 6 * ROWS, :] = code.astype(BF16)
    lane = lax.broadcasted_iota(I32, (1, TILES), 1)
    tsc[...] = jnp.zeros((16, 128), F32)
    tsc[0:1, 0:TILES] = jnp.where(lane * TP < count[0], tiles[...].astype(F32), 255.0)
    pay[6 * ROWS : 6 * ROWS + 16, :] = tsc[...].astype(BF16)


def leaver_kernel(*refs):
    sources, (fpay, keep), held, (vsc, tsc, sems) = refs[:10], refs[10:12], refs[12:20], refs[20:]
    vel, vol, rate, cell, tiles, count, lists, mig = held
    fluid, press = sources[8:]
    pairs = list(zip(sources[:8], held))
    pairs += [(fluid.at[k], fpay.at[2 * k : 2 * k + 2]) for k in range(3)] + [(press, fpay.at[6:8])]
    load_all(pairs, sems)
    fold_rows(vel, vsc)
    cells = cell[...]
    tsc[...] = jnp.zeros((16, 128), F32)
    tsc[0:1, 0:TILES] = tiles[...].astype(F32)
    raw_tiles = tsc[...].astype(BF16)
    slots = jnp.concatenate([lists[0:1, :], lists[1:2, :]], axis=1)
    lane512 = lax.broadcasted_iota(I32, (1, 2 * MIG), 1)
    ends = jnp.where(lane512 < MIG, mig[:, 0:1], mig[:, 1:2] + MIG)
    valid = jnp.where(lane512 < ends, F32(1.0), F32(0.0))
    low = (rows_iota(128, 2 * MIG) == (slots & 127)).astype(F32).astype(BF16)
    row_mask = rows_iota(ROWS, 2 * MIG) == (slots >> 7)
    counts = dot_nt(jnp.where(row_mask, valid, 0.0).astype(BF16), low)
    keep[...] = active_slots(count) * jnp.where(counts > 0.5, 0.0, 1.0)

    def picked(values, parts):
        total = None
        for _ in range(parts):
            piece = values.astype(BF16)
            values = values - piece.astype(F32)
            term = dot_nn(piece, low)
            total = term if total is None else total + term
        return jnp.sum(jnp.where(row_mask, total, 0.0), axis=0, keepdims=True)

    def put(row, values):
        fpay[8, row : row + 1, :] = values[:, :MIG]
        fpay[8, 8 + row : 9 + row, :] = values[:, MIG:]

    for k in range(3):
        put(k, picked(vsc[k], 3))
    put(3, picked(vol[...], 3))
    put(4, picked(rate[...], 3))
    tile_hot = (rows_iota(128, 2 * MIG) == (slots >> 8)).astype(F32).astype(BF16)
    block = dot_nn(raw_tiles, tile_hot)[0:1, :]
    cell_hi = picked((cells >> 7).astype(F32), 1)
    cell_lo = picked((cells & 127).astype(F32), 1)
    put(5, block * BLOCK + cell_hi * 128.0 + cell_lo)
    put(6, valid)
    put(7, jnp.zeros_like(valid))


def edge_kernel(own, far, edge, side):
    c = lax.axis_index("c")
    native = lax.axis_index("z") == c
    for k in range(4):
        edge[k] = jnp.where(native, own[2 * k + c], far[2 * k + c])
        for i in range(2):
            side[2 * k + i] = jnp.where(native, far[2 * k + i], own[2 * k + i])
    side[8] = jnp.where(native, own[7 - c], far[7 - c])


def at(values, axis, step):
    size = values.shape[axis]
    moved = pltpu.roll(values, (-step) % size, axis)
    place = lax.broadcasted_iota(I32, values.shape, axis)
    return jnp.where(place == (size - 1 if step > 0 else 0), 0.0, moved)


def rad_up(values):
    return at(values, values.ndim - 2, 1)


def rad_down(values):
    return at(values, values.ndim - 2, -1)


def axial_up(values):
    return at(values, values.ndim - 1, 1)


def axial_down(values):
    return at(values, values.ndim - 1, -1)


def add_deposits(pays, acc, scr, tile_v, tile_s, picks, sem, skip_own=False):
    y = lax.axis_index("y")
    first = y * 16 + lax.axis_index("c") * OWN_BLOCKS
    sources = pays.shape[0]
    for s in range(sources):
        tile_v[s : s + 1, :] = pays[s, 6 * ROWS : 6 * ROWS + 16, :].astype(F32)[0:1, :].astype(I32)
    copy = pltpu.make_async_copy(tile_v, tile_s, sem)
    copy.start()

    def widen(s, carry):
        base = pl.multiple_of(s * SCR_ROWS, 8)
        scr[pl.ds(base, 5 * ROWS), :] = pays[s, 0 : 5 * ROWS, :].astype(F32)
        code = pays[s, 5 * ROWS : 6 * ROWS, :].astype(F32)
        hi = jnp.zeros_like(code)
        for step in (8, 4, 2, 1):
            large = code >= 2.0 ** (7 + step)
            code = jnp.where(large, code * 2.0**-step, code)
            hi = hi + jnp.where(large, F32(step), 0.0)
        scr[pl.ds(base + 5 * ROWS, ROWS), :] = hi
        scr[pl.ds(base + 6 * ROWS, ROWS), :] = code - 128.0
        return carry

    lax.fori_loop(0, sources, widen, 0)
    copy.wait()

    def choose(s, found):
        base = first + jnp.where(s // N_Z == y, 1024, 0) if skip_own else first
        for t in range(TILES):
            block = tile_s[s, t] - base
            picks[found] = (s * SCR_ROWS + 2 * t) * 16 + block
            mine = jnp.logical_and(block >= 0, block < OWN_BLOCKS)
            found = found + mine.astype(I32)
        return found

    found = lax.fori_loop(0, sources, choose, jnp.int32(0))
    for i in range(UNROLL):
        picks[found + i] = OWN_BLOCKS
    iota16 = lax.broadcasted_iota(I32, (16, 128), 0).astype(F32)
    iota128 = lax.broadcasted_iota(I32, (128, 128), 0).astype(F32)

    def one_tile(code):
        block = code & 15
        base = code >> 4
        left, right = [], []
        for h in range(2):
            hi = scr[pl.ds(base + 5 * ROWS + h, 1), :]
            lo = scr[pl.ds(base + 6 * ROWS + h, 1), :]
            mask = iota16 == hi
            parts = [
                jnp.where(mask, scr[pl.ds(base + k * ROWS + h, 1), :], 0.0).astype(BF16)
                for k in range(5)
            ]
            left.append(jnp.concatenate(parts, axis=0))
            right.append(jnp.where(iota128 == lo, F32(1.0), F32(0.0)).astype(BF16))
        sums = dot_nt(jnp.concatenate(left, axis=1), jnp.concatenate(right, axis=1))
        return block, sums

    def deposit(i, carry):
        done = [one_tile(picks[i * UNROLL + u]) for u in range(UNROLL)]
        for block, sums in done:
            acc[block] = acc[block] + sums
        return carry

    lax.fori_loop(0, (found + UNROLL - 1) // UNROLL, deposit, 0)


def first_deposit_kernel(pays, acc, *scratch):
    acc[...] = jnp.zeros_like(acc)
    add_deposits(pays, acc, *scratch)


def next_deposit_kernel(skip_own, pays, before, acc, *scratch):
    acc[...] = before[...]
    add_deposits(pays, acc, *scratch, skip_own=skip_own)


def spread_kernel(own, far, both, out):
    both[0] = own[...]
    both[1] = far[...]
    for y in range(N_Y):
        out[y, 0] = own[...]
        out[y, 1] = far[...]


def velocity_kernel(acc, own, far, side, edge, u_out, por_out, flux_y, flux_c, wide, flux):
    c = lax.axis_index("c")
    native = lax.axis_index("z") == c

    def amount(k):
        halves = []
        for b in range(OWN_BLOCKS):
            halves.append(
                jnp.concatenate([acc[b, k * 16 : k * 16 + 8, :], acc[b, k * 16 + 8 : k * 16 + 16, :]], axis=1)
            )
        return jnp.stack(
            [jnp.concatenate([halves[2 * i], halves[2 * i + 1]], axis=0) for i in range(4)]
        )

    for k in range(4):
        wide[k, 5 * c] = edge[k]
        for i in range(2):
            wide[k, 1 + 2 * c + i] = jnp.where(native, own[2 * k + i], far[2 * k + i])
            wide[k, 3 - 2 * c + i] = side[2 * k + i]
        wide[k, 5 * (1 - c)] = jnp.where(native, far[2 * k + c], own[2 * k + c])
    porosity = 1.0 / (1.0 + amount(0))
    por_out[...] = porosity
    below = 1.0 + DT * amount(1) / porosity
    centre = wide[3, 1:5]
    slopes = [
        0.5 * (wide[3, 2:6] - wide[3, 0:4]),
        0.5 * (rad_up(centre) - rad_down(centre)),
        0.5 * (axial_up(centre) - axial_down(centre)),
    ]
    for k in range(3):
        v = wide[k, 1:5]
        lap = (
            wide[k, 2:6] + wide[k, 0:4] + rad_up(v) + rad_down(v) + axial_up(v) + axial_down(v) - 6.0 * v
        )
        u = (v + DT * (NU * lap - slopes[k]) + DT * amount(2 + k) / porosity) / below
        u_out[k] = u
        flux[k] = porosity * u
    for i in range(3):
        for k in range(3):
            flux_y[3 * k + i] = flux[k, c + i]
            flux_c[3 * k + i] = flux[k, 1 - c + i]
        flux_y[9 + i] = wide[3, 1 + c + i]


def fluid_kernel(
    u_in, por_in, own, far, side, from_y, from_c, fields, kept, sent, flux, pres, out
):
    c = lax.axis_index("c")
    native = lax.axis_index("z") == c
    for k in range(3):
        flux[k, 3:7] = por_in[...] * u_in[k]
        for i in range(3):
            flux[k, 7 * c + i] = from_y[3 * k + i]
            flux[k, 7 * (1 - c) + i] = from_c[1 - c, 3 * k + i]
    for i in range(3):
        pres[7 * c + i] = from_y[9 + i]
    for i in range(2):
        pres[3 + 2 * c + i] = jnp.where(native, own[6 + i], far[6 + i])
        pres[5 - 2 * c + i] = side[6 + i]
        pres[7 - 6 * c + i] = jnp.where(native, far[6 + i], own[6 + i])
    pres[9 * (1 - c)] = side[8]
    f1 = flux[1, 1:9]
    f2 = flux[2, 1:9]
    source = 0.5 * (
        flux[0, 2:10] - flux[0, 0:8] + rad_up(f1) - rad_down(f1) + axial_up(f2) - axial_down(f2)
    )

    def sweep(p, s):
        centre = p[1:-1]
        return (
            p[2:]
            + p[:-2]
            + rad_up(centre)
            + rad_down(centre)
            + axial_up(centre)
            + axial_down(centre)
            - s / DT
        ) / 6.0

    p1 = sweep(pres[...], source)
    p2 = sweep(p1, source[1:-1])
    centre = p2[1:-1]
    slopes = [
        0.5 * (p2[2:] - p2[:-2]),
        0.5 * (rad_up(centre) - rad_down(centre)),
        0.5 * (axial_up(centre) - axial_down(centre)),
    ]
    for k in range(3):
        out[k] = u_in[k] - DT * slopes[k]
    out[3] = centre
    for k in range(4):
        for i in range(4):
            plane = out[k, i] if k < 3 else por_in[i]
            for h in range(2):
                half = plane[8 * h : 8 * h + 8]
                both = jnp.concatenate([half[:, :128], half[:, 128:]], axis=0)
                for copy in range(N_Y):
                    fields[copy, 2 * i + h, 16 * k : 16 * k + 16, :] = both.astype(BF16)
    for k in range(4):
        for i in range(2):
            kept[k, i] = out[k, 2 * c + i]
            sent[k, i] = out[k, 2 * (1 - c) + i]


def step_parcel(vel, rate, sampled):
    coupling = rate / (sampled[3] * sampled[3])
    pull = DT * coupling
    below = 1.0 + pull
    return [(vel[k] + pull * sampled[k]) / below for k in range(3)]


def leave_lists_of(own, far):
    z_lo = lax.rem(lax.axis_index("blk"), Z_LO)
    list0 = jnp.where(z_lo == 0, far[8, 0:8, :], own[8, 0:8, :])
    list1 = jnp.where(z_lo == Z_LO - 1, far[8, 8:16, :], own[8, 8:16, :])
    return jnp.concatenate([list0, list1], axis=1)


def sample_lists(fields, core, both, total):
    place = both[5:6, :].astype(I32)
    block = place >> 11
    low = (rows_iota(128, 2 * MIG) == (place & 127)).astype(F32).astype(BF16)

    def gather(i, total):
        for u in range(OWN_BLOCKS):
            picked = dot_nn(fields[i, u], low)
            total = total + jnp.where(block == i * 16 + core * OWN_BLOCKS + u, picked, 0.0)
        return total

    return lax.fori_loop(0, N_Y, gather, total)


def first_leave_kernel(near, own, far, out):
    start = jnp.zeros((64, 2 * MIG), F32)
    out[...] = sample_lists(near, lax.axis_index("c"), leave_lists_of(own, far), start)


def last_leave_kernel(other, own, far, half, out0, out1):
    both = leave_lists_of(own, far)
    total = sample_lists(other, 1 - lax.axis_index("c"), both, half[...])
    mask = rows_iota(16, 2 * MIG) == hi_of(both[5:6, :].astype(I32) & (BLOCK - 1))
    sampled = [
        jnp.sum(jnp.where(mask, total[16 * k : 16 * k + 16], 0.0), axis=0, keepdims=True)
        for k in range(4)
    ]
    sampled[3] = jnp.where(both[6:7, :] > 0.5, sampled[3], 1.0)
    vol, rate, valid = both[3:4, :], both[4:5, :], both[6:7, :]
    moved = step_parcel([both[k : k + 1, :] for k in range(3)], rate, sampled)
    for k, values in enumerate(moved + [vol, rate]):
        values = values * valid
        out0[k : k + 1, :] = values[:, :MIG]
        out1[k : k + 1, :] = values[:, MIG:]


def move_kernel(
    near, other, tiles_in, cell_in, keep, vel_in, rate_in, kept, swapped, out, fluid, press, *scratch
):
    tiles, cell, vel, rate, sems = scratch
    load_all([(tiles_in, tiles), (cell_in, cell), (vel_in, vel), (rate_in, rate)], sems)
    c = lax.axis_index("c")
    iota16 = rows_iota(16, TP)
    iota128 = rows_iota(128, TP)

    def pair(ref, t):
        return jnp.concatenate([ref[pl.ds(2 * t, 1), :], ref[pl.ds(2 * t + 1, 1), :]], axis=1)

    def one_tile(t):
        block = tiles[t]
        row, col = block >> 4, block & 7
        here = jnp.where((block >> 3) & 1 == c, near[row, col], other[row, col])
        cells = pair(cell, t)
        low = jnp.where(iota128 == (cells & 127), F32(1.0), F32(0.0)).astype(BF16)
        picked = dot_nn(here, low)
        mask = iota16 == hi_of(cells)
        sampled = [
            jnp.sum(jnp.where(mask, picked[16 * k : 16 * k + 16], 0.0), axis=0, keepdims=True)
            for k in range(4)
        ]
        lanes = pl.ds(pl.multiple_of(t * TP, TP), TP)
        moved = step_parcel([vel[k : k + 1, lanes] for k in range(3)], pair(rate, t), sampled)
        stays = pair(keep, t)
        for k in range(3):
            out[k : k + 1, lanes] = moved[k] * stays

    def some(i, carry):
        for u in range(4):
            one_tile(i * 4 + u)
        return carry

    lax.fori_loop(0, TILES // 4, some, 0)
    mine = lax.axis_index("z") == c
    for k in range(3):
        fluid[k] = jnp.where(mine, kept[k], swapped[k])
    press[...] = jnp.where(mine, kept[3], swapped[3])


def per_device(
    fluid_vel,
    pressure,
    parcel_vel,
    parcel_vol,
    parcel_rate,
    cell_local,
    tile_block,
    parcel_count,
    leave_lists,
    mig_counts,
):
    vol = parcel_vol.reshape(ROWS, 128)
    rate = parcel_rate.reshape(ROWS, 128)
    cell = cell_local.reshape(ROWS, 128)
    tiles = tile_block.reshape(1, TILES)
    plane = (RADIAL, LINE)
    parcels = [parcel_vel, vol, rate, cell, tiles, parcel_count]
    held = [
        pltpu.VMEM((3, PCAP), F32),
        pltpu.VMEM((ROWS, 128), F32),
        pltpu.VMEM((ROWS, 128), F32),
        pltpu.VMEM((ROWS, 128), I32),
        pltpu.VMEM((1, TILES), I32),
        pltpu.SMEM((1,), I32),
    ]
    folded = [pltpu.VMEM((3, ROWS, 128), F32), pltpu.VMEM((16, 128), F32)]
    (pay,) = call(
        pack_kernel,
        [((PAY_ROWS, 128), BF16)],
        parcels,
        scratch=held + folded + [pltpu.SemaphoreType.DMA((6,))],
        hbm=range(6),
        limit=PACK_LIMIT,
    )
    fpay, keep = call(
        leaver_kernel,
        [((9,) + plane, F32), ((ROWS, 128), F32)],
        parcels + [leave_lists, mig_counts.reshape(1, 2), fluid_vel, pressure],
        scratch=held
        + [pltpu.VMEM((2, MIG), I32), pltpu.VMEM((1, 2), I32)]
        + folded
        + [pltpu.SemaphoreType.DMA((12,))],
        hbm=range(10),
        limit=PACK_LIMIT,
    )
    pay_far = swap(pay, "z")
    fpay_far = swap(fpay, "z")
    pay_pair, pays = call(
        spread_kernel,
        [((N_Z, PAY_ROWS, 128), BF16), ((N_Y, N_Z, PAY_ROWS, 128), BF16)],
        [pay, pay_far],
    )
    pays = lax.all_to_all(pays, "y", 0, 0)
    deposit_scratch = [
        pltpu.VMEM((SOURCES * SCR_ROWS, 128), F32),
        pltpu.VMEM((SOURCES, 128), I32),
        pltpu.SMEM((SOURCES, 128), I32),
        pltpu.SMEM((LIST_CAP,), I32),
        pltpu.SemaphoreType.DMA,
    ]
    sums_shape = (OWN_BLOCKS + 1, 80, 128)
    (sums,) = call(
        first_deposit_kernel,
        [(sums_shape, F32)],
        [pay_pair],
        scratch=deposit_scratch,
        flops=1 << 36,
    )
    (sums,) = call(
        functools.partial(next_deposit_kernel, True),
        [(sums_shape, F32)],
        [pays.reshape(SOURCES, PAY_ROWS, 128), sums],
        scratch=deposit_scratch,
        flops=1 << 36,
    )
    pays_c = swap(pays, "c")
    edge, side = call(
        edge_kernel, [((4,) + plane, F32), ((9,) + plane, F32)], [fpay, fpay_far]
    )
    route = halo_route()
    side = swap(side, "c")
    edge = lax.ppermute(edge, ALL, route)
    (sums,) = call(
        functools.partial(next_deposit_kernel, False),
        [(sums_shape, F32)],
        [pays_c.reshape(SOURCES, PAY_ROWS, 128), sums],
        scratch=deposit_scratch,
        flops=1 << 36,
    )
    u_star, porosity, flux_y, flux_c = call(
        velocity_kernel,
        [((3, 4) + plane, F32), ((4,) + plane, F32), ((12,) + plane, F32), ((9,) + plane, F32)],
        [sums, fpay, fpay_far, side, edge],
        scratch=[pltpu.VMEM((4, 6) + plane, F32), pltpu.VMEM((3, 4) + plane, F32)],
    )
    from_y = lax.ppermute(flux_y, ALL, route)
    from_c = lax.all_gather(flux_c, "c", axis=0)
    fields, kept, sent = call(
        fluid_kernel,
        [((N_Y, OWN_BLOCKS, 64, 128), BF16), ((4, 2) + plane, F32), ((4, 2) + plane, F32)],
        [u_star, porosity, fpay, fpay_far, side, from_y, from_c],
        scratch=[
            pltpu.VMEM((3, 10) + plane, F32),
            pltpu.VMEM((10,) + plane, F32),
            pltpu.VMEM((4, 4) + plane, F32),
        ],
    )
    fields = lax.all_to_all(fields, "y", 0, 0)
    fields_c = swap(fields, "c")
    swapped = swap(sent, "c")
    (half,) = call(
        first_leave_kernel,
        [((64, 2 * MIG), F32)],
        [fields, fpay, fpay_far],
        flops=1 << 36,
    )
    out0, out1 = call(
        last_leave_kernel,
        [((5, MIG), F32), ((5, MIG), F32)],
        [fields_c, fpay, fpay_far, half],
    )
    arrive0 = lax.ppermute(out0, ALL, leave_route(-1))
    arrive1 = lax.ppermute(out1, ALL, leave_route(1))
    parcel_next, fluid_next, pressure_next = call(
        move_kernel,
        [((3, PCAP), F32), ((3, 2) + plane, F32), ((2,) + plane, F32)],
        [fields, fields_c, tile_block, cell, keep, parcel_vel, rate, kept, swapped],
        scratch=[
            pltpu.SMEM((TILES,), I32),
            pltpu.VMEM((ROWS, 128), I32),
            pltpu.VMEM((3, PCAP), F32),
            pltpu.VMEM((ROWS, 128), F32),
            pltpu.SemaphoreType.DMA((4,)),
        ],
        hbm=(2, 3, 5, 6),
        flops=1 << 31,
    )
    arrivals = jnp.stack([arrive0, arrive1], axis=1).transpose(1, 0, 2)
    return fluid_next, pressure_next, parcel_next, arrivals


def solution(mesh):
    fine = Mesh(mesh.devices.reshape(N_BLK, N_Y, N_Z, N_C), ALL)
    placed = (
        P(None, ALL, None, None),
        P(ALL, None, None),
        P(None, ALL),
        P(ALL),
        P(ALL),
        P(ALL),
        P(ALL),
        P(ALL),
        P(None, ALL),
        P(None, ALL),
    )
    return jax.shard_map(
        per_device,
        mesh=fine,
        in_specs=placed,
        out_specs=(
            P(None, ALL, None, None),
            P(ALL, None, None),
            P(None, ALL),
            P(None, None, ALL),
        ),
        check_vma=False,
    )
```

```python
import functools

import jax
import jax.numpy as jnp
from jax import lax
from jax.experimental import pallas as pl
from jax.experimental.pallas import tpu as pltpu
from jax.sharding import Mesh, PartitionSpec as P

PCAP = 8192
TP = 256
TILES = PCAP // TP
ROWS = PCAP // 128
BLOCK = 2048
RADIAL = 16
LINE = 256
MIG = 256
N_BLK, N_Y, N_Z, N_C = 32, 4, 2, 2
Z_LO = 8
ALL = ("blk", "y", "z", "c")

DT = 0.2
NU = 0.5

PAY_ROWS = 6 * ROWS + 16
SCR_ROWS = 7 * ROWS
SOURCES = N_Y * N_Z
OWN_BLOCKS = 8
UNROLL = 8
LIST_CAP = SOURCES * TILES + UNROLL

PACK_LIMIT = 56 << 20

F32 = jnp.float32
BF16 = jnp.bfloat16
I32 = jnp.int32


def flat(blk, y, z, c):
    return ((blk * N_Y + y) * N_Z + z) * N_C + c


def every_place():
    for blk in range(N_BLK):
        for y in range(N_Y):
            for z in range(N_Z):
                for c in range(N_C):
                    yield blk, y, z, c


def halo_route():
    pairs = []
    for blk, y, z, c in every_place():
        if c == 1:
            here = flat(blk, y, z, 1)
            if y < N_Y - 1:
                there = flat(blk, y + 1, z, 0)
            else:
                crossing = blk % Z_LO == Z_LO - 1
                there = flat((blk + 1) % N_BLK, 0, 1 - z if crossing else z, 0)
            pairs += [(here, there), (there, here)]
    return pairs


def leave_route(step):
    edge = 0 if step < 0 else Z_LO - 1
    pairs = []
    for blk, y, z, c in every_place():
        sender = flat(blk, y, 1 - z if blk % Z_LO == edge else z, c)
        pairs.append((sender, flat((blk + step) % N_BLK, y, z, c)))
    return pairs


def swap(values, axis):
    return lax.ppermute(values, axis, [(0, 1), (1, 0)])


def call(kernel, outs, ins, scratch=(), smem=(), hbm=(), limit=16 << 20, flops=0):
    def space(i):
        return pltpu.SMEM if i in smem else pltpu.HBM if i in hbm else pltpu.VMEM

    specs = [pl.BlockSpec(memory_space=space(i)) for i in range(len(ins))]
    return pl.pallas_call(
        kernel,
        out_shape=[jax.ShapeDtypeStruct(shape, dtype) for shape, dtype in outs],
        in_specs=specs,
        out_specs=[pl.BlockSpec(memory_space=pltpu.VMEM) for _ in outs],
        scratch_shapes=list(scratch),
        compiler_params=pltpu.CompilerParams(vmem_limit_bytes=limit),
        cost_estimate=pl.CostEstimate(flops=flops, bytes_accessed=1 << 20, transcendentals=0),
    )(*ins)


def rows_iota(rows, lanes):
    return lax.broadcasted_iota(I32, (rows, lanes), 0)


def dot_nt(a, b):
    return lax.dot_general(a, b, (((1,), (1,)), ((), ())), preferred_element_type=F32)


def dot_nn(a, b):
    return lax.dot_general(a, b, (((1,), (0,)), ((), ())), preferred_element_type=F32)


def hi_of(cell):
    return ((cell >> 7) & 1) * 8 + (cell >> 8)


def load_all(pairs, sems):
    copies = [pltpu.make_async_copy(a, b, sems.at[i]) for i, (a, b) in enumerate(pairs)]
    for copy in copies:
        copy.start()
    for copy in copies:
        copy.wait()


def fold_rows(vel, vsc):
    for r in range(ROWS):
        for k in range(3):
            vsc[k, r : r + 1, :] = vel[k : k + 1, r * 128 : (r + 1) * 128]


def active_slots(count):
    slot = rows_iota(ROWS, 128) * 128 + lax.broadcasted_iota(I32, (ROWS, 128), 1)
    return (slot < count[...]).astype(F32)


def pack_kernel(*refs):
    sources, pay, held, (vsc, tsc, sems) = refs[:6], refs[6], refs[7:13], refs[13:]
    vel, vol, rate, cell, tiles, count = held
    load_all(list(zip(sources, held)), sems)
    fold_rows(vel, vsc)
    active = active_slots(count)
    drag = vol[...] * rate[...]
    pay[0:ROWS, :] = (vol[...] * active).astype(BF16)
    pay[ROWS : 2 * ROWS, :] = (drag * active).astype(BF16)
    for k in range(3):
        pay[(2 + k) * ROWS : (3 + k) * ROWS, :] = (drag * vsc[k] * active).astype(BF16)
    cells = cell[...]
    hi = hi_of(cells)
    code = ((cells & 127) + 128).astype(F32)
    for bit in range(4):
        code = code * jnp.where((hi >> bit) & 1 == 1, F32(2.0 ** (1 << bit)), F32(1.0))
    pay[5 * ROWS : 6 * ROWS, :] = code.astype(BF16)
    lane = lax.broadcasted_iota(I32, (1, TILES), 1)
    tsc[...] = jnp.zeros((16, 128), F32)
    tsc[0:1, 0:TILES] = jnp.where(lane * TP < count[...], tiles[...].astype(F32), 255.0)
    pay[6 * ROWS : 6 * ROWS + 16, :] = tsc[...].astype(BF16)


def place_rows():
    return rows_iota(RADIAL, LINE) % 8 == 5


def fixed_point(values, places=False):
    scale = jnp.where(place_rows(), F32(1.0), F32(2.0**20)) if places else F32(2.0**20)
    return jnp.floor(values * scale + 0.5).astype(I32)


def from_fixed_point(code, places=False):
    scale = jnp.where(place_rows(), F32(1.0), F32(2.0**-20)) if places else F32(2.0**-20)
    return code.astype(F32) * scale


def leaver_kernel(*refs):
    sources, (fpay, keep, coded), held, (vsc, tsc, sems) = refs[:10], refs[10:13], refs[13:21], refs[21:]
    vel, vol, rate, cell, tiles, count, lists, mig = held
    fluid, press = sources[8:]
    pairs = list(zip(sources[:8], held))
    pairs += [(fluid.at[k], fpay.at[2 * k : 2 * k + 2]) for k in range(3)] + [(press, fpay.at[6:8])]
    load_all(pairs, sems)
    fold_rows(vel, vsc)
    cells = cell[...]
    tsc[...] = jnp.zeros((16, 128), F32)
    tsc[0:1, 0:TILES] = tiles[...].astype(F32)
    raw_tiles = tsc[...].astype(BF16)
    slots = jnp.concatenate([lists[0:1, :], lists[1:2, :]], axis=1)
    lane512 = lax.broadcasted_iota(I32, (1, 2 * MIG), 1)
    ends = jnp.where(lane512 < MIG, mig[:, 0:1], mig[:, 1:2] + MIG)
    valid = jnp.where(lane512 < ends, F32(1.0), F32(0.0))
    low = (rows_iota(128, 2 * MIG) == (slots & 127)).astype(F32).astype(BF16)
    row_mask = rows_iota(ROWS, 2 * MIG) == (slots >> 7)
    counts = dot_nt(jnp.where(row_mask, valid, 0.0).astype(BF16), low)
    keep[...] = active_slots(count) * jnp.where(counts > 0.5, 0.0, 1.0)

    def picked(values, parts):
        total = None
        for _ in range(parts):
            piece = values.astype(BF16)
            values = values - piece.astype(F32)
            term = dot_nn(piece, low)
            total = term if total is None else total + term
        return jnp.sum(jnp.where(row_mask, total, 0.0), axis=0, keepdims=True)

    def put(row, values):
        fpay[8, row : row + 1, :] = values[:, :MIG]
        fpay[8, 8 + row : 9 + row, :] = values[:, MIG:]

    for k in range(3):
        put(k, picked(vsc[k], 3))
    put(3, picked(vol[...], 3))
    put(4, picked(rate[...], 3))
    tile_hot = (rows_iota(128, 2 * MIG) == (slots >> 8)).astype(F32).astype(BF16)
    block = dot_nn(raw_tiles, tile_hot)[0:1, :]
    cell_hi = picked((cells >> 7).astype(F32), 1)
    cell_lo = picked((cells & 127).astype(F32), 1)
    put(5, block * BLOCK + cell_hi * 128.0 + cell_lo)
    put(6, valid)
    put(7, jnp.zeros_like(valid))
    codes = [fixed_point(fpay[p], places=p == 8) for p in range(9)]
    for p in range(9):
        coded[p] = (codes[p] >> 8).astype(jnp.int16)
    for j in range(5):
        shared = codes[2 * j] & 255
        if j < 4:
            shared = shared + (codes[2 * j + 1] & 255) * 256
        coded[9 + j] = (shared - 32768).astype(jnp.int16)


def edge_kernel(own, coded, edge, side, far):
    for p in range(9):
        shared = coded[9 + p // 2].astype(I32) + 32768
        low = shared >> 8 if p % 2 else shared & 255
        far[p] = from_fixed_point(coded[p].astype(I32) * 256 + low, places=p == 8)
    c = lax.axis_index("c")
    native = lax.axis_index("z") == c
    for k in range(4):
        edge[k] = jnp.where(native, own[2 * k + c], far[2 * k + c])
        for i in range(2):
            side[2 * k + i] = jnp.where(native, far[2 * k + i], own[2 * k + i])
    side[8] = jnp.where(native, own[7 - c], far[7 - c])


def at(values, axis, step):
    size = values.shape[axis]
    moved = pltpu.roll(values, (-step) % size, axis)
    place = lax.broadcasted_iota(I32, values.shape, axis)
    return jnp.where(place == (size - 1 if step > 0 else 0), 0.0, moved)


def rad_up(values):
    return at(values, values.ndim - 2, 1)


def rad_down(values):
    return at(values, values.ndim - 2, -1)


def axial_up(values):
    return at(values, values.ndim - 1, 1)


def axial_down(values):
    return at(values, values.ndim - 1, -1)


def add_deposits(pays, acc, scr, tile_v, tile_s, picks, sem, skip_own=False):
    y = lax.axis_index("y")
    first = y * 16 + lax.axis_index("c") * OWN_BLOCKS
    sources = pays.shape[0]
    for s in range(sources):
        tile_v[s : s + 1, :] = pays[s, 6 * ROWS : 6 * ROWS + 16, :].astype(F32)[0:1, :].astype(I32)
    copy = pltpu.make_async_copy(tile_v, tile_s, sem)
    copy.start()

    def widen(s, carry):
        base = pl.multiple_of(s * SCR_ROWS, 8)
        scr[pl.ds(base, 5 * ROWS), :] = pays[s, 0 : 5 * ROWS, :].astype(F32)
        code = pays[s, 5 * ROWS : 6 * ROWS, :].astype(F32)
        hi = jnp.zeros_like(code)
        for step in (8, 4, 2, 1):
            large = code >= 2.0 ** (7 + step)
            code = jnp.where(large, code * 2.0**-step, code)
            hi = hi + jnp.where(large, F32(step), 0.0)
        scr[pl.ds(base + 5 * ROWS, ROWS), :] = hi
        scr[pl.ds(base + 6 * ROWS, ROWS), :] = code - 128.0
        return carry

    lax.fori_loop(0, sources, widen, 0)
    copy.wait()

    def choose(s, found):
        base = first + jnp.where(s // N_Z == y, 1024, 0) if skip_own else first
        for t in range(TILES):
            block = tile_s[s, t] - base
            picks[found] = (s * SCR_ROWS + 2 * t) * 16 + block
            mine = jnp.logical_and(block >= 0, block < OWN_BLOCKS)
            found = found + mine.astype(I32)
        return found

    found = lax.fori_loop(0, sources, choose, jnp.int32(0))
    for i in range(UNROLL):
        picks[found + i] = OWN_BLOCKS
    iota16 = lax.broadcasted_iota(I32, (16, 128), 0).astype(F32)
    iota128 = lax.broadcasted_iota(I32, (128, 128), 0).astype(F32)

    def one_tile(code):
        block = code & 15
        base = code >> 4
        left, right = [], []
        for h in range(2):
            hi = scr[pl.ds(base + 5 * ROWS + h, 1), :]
            lo = scr[pl.ds(base + 6 * ROWS + h, 1), :]
            mask = iota16 == hi
            parts = [
                jnp.where(mask, scr[pl.ds(base + k * ROWS + h, 1), :], 0.0).astype(BF16)
                for k in range(5)
            ]
            left.append(jnp.concatenate(parts, axis=0))
            right.append(jnp.where(iota128 == lo, F32(1.0), F32(0.0)).astype(BF16))
        sums = dot_nt(jnp.concatenate(left, axis=1), jnp.concatenate(right, axis=1))
        return block, sums

    def deposit(i, carry):
        done = [one_tile(picks[i * UNROLL + u]) for u in range(UNROLL)]
        for block, sums in done:
            acc[block] = acc[block] + sums
        return carry

    lax.fori_loop(0, (found + UNROLL - 1) // UNROLL, deposit, 0)


def first_deposit_kernel(pays, *refs):
    given, (acc, *kept), scratch = refs[:5], refs[5:11], refs[11:]
    for source, target in zip(given, kept):
        target[...] = source[...]
    acc[...] = jnp.zeros_like(acc)
    add_deposits(pays, acc, *scratch)


def next_deposit_kernel(skip_own, pays, before, acc, *scratch):
    acc[...] = before[...]
    add_deposits(pays, acc, *scratch, skip_own=skip_own)


def spread_kernel(own, far, both, out):
    both[0] = own[...]
    both[1] = far[...]
    for y in range(N_Y):
        out[y, 0] = own[...]
        out[y, 1] = far[...]


def velocity_kernel(acc, own, far, side, edge, u_out, por_out, flux_y, flux_c, wide, flux):
    c = lax.axis_index("c")
    native = lax.axis_index("z") == c

    def amount(k):
        halves = []
        for b in range(OWN_BLOCKS):
            halves.append(
                jnp.concatenate([acc[b, k * 16 : k * 16 + 8, :], acc[b, k * 16 + 8 : k * 16 + 16, :]], axis=1)
            )
        return jnp.stack(
            [jnp.concatenate([halves[2 * i], halves[2 * i + 1]], axis=0) for i in range(4)]
        )

    for k in range(4):
        wide[k, 5 * c] = edge[k]
        for i in range(2):
            wide[k, 1 + 2 * c + i] = jnp.where(native, own[2 * k + i], far[2 * k + i])
            wide[k, 3 - 2 * c + i] = side[2 * k + i]
        wide[k, 5 * (1 - c)] = jnp.where(native, far[2 * k + c], own[2 * k + c])
    porosity = 1.0 / (1.0 + amount(0))
    por_out[...] = porosity
    below = 1.0 + DT * amount(1) / porosity
    centre = wide[3, 1:5]
    slopes = [
        0.5 * (wide[3, 2:6] - wide[3, 0:4]),
        0.5 * (rad_up(centre) - rad_down(centre)),
        0.5 * (axial_up(centre) - axial_down(centre)),
    ]
    for k in range(3):
        v = wide[k, 1:5]
        lap = (
            wide[k, 2:6] + wide[k, 0:4] + rad_up(v) + rad_down(v) + axial_up(v) + axial_down(v) - 6.0 * v
        )
        u = (v + DT * (NU * lap - slopes[k]) + DT * amount(2 + k) / porosity) / below
        u_out[k] = u
        flux[k] = porosity * u
    for i in range(3):
        for k in range(3):
            flux_y[3 * k + i] = flux[k, c + i]
            flux_c[3 * k + i] = flux[k, 1 - c + i]
        flux_y[9 + i] = wide[3, 1 + c + i]


def fluid_kernel(
    u_in, por_in, own, far, side, from_y, from_c, fields, kept, sent, flux, pres, out
):
    c = lax.axis_index("c")
    native = lax.axis_index("z") == c
    for k in range(3):
        flux[k, 3:7] = por_in[...] * u_in[k]
        for i in range(3):
            flux[k, 7 * c + i] = from_y[3 * k + i]
            flux[k, 7 * (1 - c) + i] = from_c[1 - c, 3 * k + i]
    for i in range(3):
        pres[7 * c + i] = from_y[9 + i]
    for i in range(2):
        pres[3 + 2 * c + i] = jnp.where(native, own[6 + i], far[6 + i])
        pres[5 - 2 * c + i] = side[6 + i]
        pres[7 - 6 * c + i] = jnp.where(native, far[6 + i], own[6 + i])
    pres[9 * (1 - c)] = side[8]
    f1 = flux[1, 1:9]
    f2 = flux[2, 1:9]
    source = 0.5 * (
        flux[0, 2:10] - flux[0, 0:8] + rad_up(f1) - rad_down(f1) + axial_up(f2) - axial_down(f2)
    )

    def sweep(p, s):
        centre = p[1:-1]
        return (
            p[2:]
            + p[:-2]
            + rad_up(centre)
            + rad_down(centre)
            + axial_up(centre)
            + axial_down(centre)
            - s / DT
        ) / 6.0

    p1 = sweep(pres[...], source)
    p2 = sweep(p1, source[1:-1])
    centre = p2[1:-1]
    slopes = [
        0.5 * (p2[2:] - p2[:-2]),
        0.5 * (rad_up(centre) - rad_down(centre)),
        0.5 * (axial_up(centre) - axial_down(centre)),
    ]
    for k in range(3):
        out[k] = u_in[k] - DT * slopes[k]
    out[3] = centre
    for k in range(4):
        for i in range(4):
            plane = out[k, i] if k < 3 else por_in[i]
            for h in range(2):
                half = plane[8 * h : 8 * h + 8]
                both = jnp.concatenate([half[:, :128], half[:, 128:]], axis=0)
                for copy in range(N_Y):
                    fields[copy, 2 * i + h, 16 * k : 16 * k + 16, :] = both.astype(BF16)
    for k in range(4):
        for i in range(2):
            kept[k, i] = out[k, 2 * c + i]
            sent[k, i] = out[k, 2 * (1 - c) + i]


def step_parcel(vel, rate, sampled):
    coupling = rate / (sampled[3] * sampled[3])
    pull = DT * coupling
    below = 1.0 + pull
    return [(vel[k] + pull * sampled[k]) / below for k in range(3)]


def leave_lists_of(own, far):
    z_lo = lax.rem(lax.axis_index("blk"), Z_LO)
    list0 = jnp.where(z_lo == 0, far[8, 0:8, :], own[8, 0:8, :])
    list1 = jnp.where(z_lo == Z_LO - 1, far[8, 8:16, :], own[8, 8:16, :])
    return jnp.concatenate([list0, list1], axis=1)


def sample_lists(fields, core, both, total):
    place = both[5:6, :].astype(I32)
    block = place >> 11
    low = (rows_iota(128, 2 * MIG) == (place & 127)).astype(F32).astype(BF16)

    def gather(i, total):
        for u in range(OWN_BLOCKS):
            picked = dot_nn(fields[i, u], low)
            total = total + jnp.where(block == i * 16 + core * OWN_BLOCKS + u, picked, 0.0)
        return total

    return lax.fori_loop(0, N_Y, gather, total)


def first_leave_kernel(near, own, far, out):
    start = jnp.zeros((64, 2 * MIG), F32)
    out[...] = sample_lists(near, lax.axis_index("c"), leave_lists_of(own, far), start)


def last_leave_kernel(other, own, far, half, out0, out1):
    both = leave_lists_of(own, far)
    total = sample_lists(other, 1 - lax.axis_index("c"), both, half[...])
    mask = rows_iota(16, 2 * MIG) == hi_of(both[5:6, :].astype(I32) & (BLOCK - 1))
    sampled = [
        jnp.sum(jnp.where(mask, total[16 * k : 16 * k + 16], 0.0), axis=0, keepdims=True)
        for k in range(4)
    ]
    sampled[3] = jnp.where(both[6:7, :] > 0.5, sampled[3], 1.0)
    vol, rate, valid = both[3:4, :], both[4:5, :], both[6:7, :]
    moved = step_parcel([both[k : k + 1, :] for k in range(3)], rate, sampled)
    for k, values in enumerate(moved + [vol, rate]):
        values = values * valid
        out0[k : k + 1, :] = values[:, :MIG]
        out1[k : k + 1, :] = values[:, MIG:]


def move_kernel(
    near, other, tiles_in, cell, keep, vel, rate, kept, swapped, out, fluid, press, *scratch
):
    tiles, sems = scratch
    load_all([(tiles_in, tiles)], sems)
    c = lax.axis_index("c")
    iota16 = rows_iota(16, TP)
    iota128 = rows_iota(128, TP)

    def pair(ref, t):
        return jnp.concatenate([ref[pl.ds(2 * t, 1), :], ref[pl.ds(2 * t + 1, 1), :]], axis=1)

    def one_tile(t):
        block = tiles[0, t]
        row, col = block >> 4, block & 7
        here = jnp.where((block >> 3) & 1 == c, near[row, col], other[row, col])
        cells = pair(cell, t)
        low = jnp.where(iota128 == (cells & 127), F32(1.0), F32(0.0)).astype(BF16)
        picked = dot_nn(here, low)
        mask = iota16 == hi_of(cells)
        sampled = [
            jnp.sum(jnp.where(mask, picked[16 * k : 16 * k + 16], 0.0), axis=0, keepdims=True)
            for k in range(4)
        ]
        lanes = pl.ds(pl.multiple_of(t * TP, TP), TP)
        moved = step_parcel([vel[k : k + 1, lanes] for k in range(3)], pair(rate, t), sampled)
        stays = pair(keep, t)
        for k in range(3):
            out[k : k + 1, lanes] = moved[k] * stays

    def some(i, carry):
        for u in range(4):
            one_tile(i * 4 + u)
        return carry

    lax.fori_loop(0, TILES // 4, some, 0)
    mine = lax.axis_index("z") == c
    for k in range(3):
        fluid[k] = jnp.where(mine, kept[k], swapped[k])
    press[...] = jnp.where(mine, kept[3], swapped[3])


def per_device(
    fluid_vel,
    pressure,
    parcel_vel,
    parcel_vol,
    parcel_rate,
    cell_local,
    tile_block,
    parcel_count,
    leave_lists,
    mig_counts,
):
    vol = parcel_vol.reshape(ROWS, 128)
    rate = parcel_rate.reshape(ROWS, 128)
    cell = cell_local.reshape(ROWS, 128)
    tiles = tile_block.reshape(1, TILES)
    plane = (RADIAL, LINE)
    parcels = [parcel_vel, vol, rate, cell, tiles, parcel_count.reshape(1, 1)]
    held = [
        pltpu.VMEM((3, PCAP), F32),
        pltpu.VMEM((ROWS, 128), F32),
        pltpu.VMEM((ROWS, 128), F32),
        pltpu.VMEM((ROWS, 128), I32),
        pltpu.VMEM((1, TILES), I32),
        pltpu.VMEM((1, 1), I32),
    ]
    folded = [pltpu.VMEM((3, ROWS, 128), F32), pltpu.VMEM((16, 128), F32)]
    (pay,) = call(
        pack_kernel,
        [((PAY_ROWS, 128), BF16)],
        parcels,
        scratch=held + folded + [pltpu.SemaphoreType.DMA((6,))],
        hbm=range(6),
        limit=PACK_LIMIT,
    )
    fpay, keep, coded = call(
        leaver_kernel,
        [((9,) + plane, F32), ((ROWS, 128), F32), ((14,) + plane, jnp.int16)],
        parcels + [leave_lists, mig_counts.reshape(1, 2), fluid_vel, pressure],
        scratch=held
        + [pltpu.VMEM((2, MIG), I32), pltpu.VMEM((1, 2), I32)]
        + folded
        + [pltpu.SemaphoreType.DMA((12,))],
        hbm=range(10),
        limit=PACK_LIMIT,
    )
    pay_far = swap(pay, "z")
    coded_far = swap(coded, "z")
    pay_pair, pays = call(
        spread_kernel,
        [((N_Z, PAY_ROWS, 128), BF16), ((N_Y, N_Z, PAY_ROWS, 128), BF16)],
        [pay, pay_far],
    )
    pays = lax.all_to_all(pays, "y", 0, 0)
    deposit_scratch = [
        pltpu.VMEM((SOURCES * SCR_ROWS, 128), F32),
        pltpu.VMEM((SOURCES, 128), I32),
        pltpu.SMEM((SOURCES, 128), I32),
        pltpu.SMEM((LIST_CAP,), I32),
        pltpu.SemaphoreType.DMA,
    ]
    sums_shape = (OWN_BLOCKS + 1, 80, 128)
    sums, keep, vel_held, rate_held, cell_held, tiles_held = call(
        first_deposit_kernel,
        [
            (sums_shape, F32),
            ((ROWS, 128), F32),
            ((3, PCAP), F32),
            ((ROWS, 128), F32),
            ((ROWS, 128), I32),
            ((1, TILES), I32),
        ],
        [pay_pair, keep, parcel_vel, rate, cell, tiles],
        scratch=deposit_scratch,
        flops=1 << 36,
    )
    (sums,) = call(
        functools.partial(next_deposit_kernel, True),
        [(sums_shape, F32)],
        [pays.reshape(SOURCES, PAY_ROWS, 128), sums],
        scratch=deposit_scratch,
        flops=1 << 36,
    )
    pays_c = swap(pays, "c")
    edge, side, fpay_far = call(
        edge_kernel,
        [((4,) + plane, F32), ((9,) + plane, F32), ((9,) + plane, F32)],
        [fpay, coded_far],
    )
    route = halo_route()
    side = swap(side, "c")
    edge = lax.ppermute(edge, ALL, route)
    (sums,) = call(
        functools.partial(next_deposit_kernel, False),
        [(sums_shape, F32)],
        [pays_c.reshape(SOURCES, PAY_ROWS, 128), sums],
        scratch=deposit_scratch,
        flops=1 << 36,
    )
    u_star, porosity, flux_y, flux_c = call(
        velocity_kernel,
        [((3, 4) + plane, F32), ((4,) + plane, F32), ((12,) + plane, F32), ((9,) + plane, F32)],
        [sums, fpay, fpay_far, side, edge],
        scratch=[pltpu.VMEM((4, 6) + plane, F32), pltpu.VMEM((3, 4) + plane, F32)],
    )
    from_y = lax.ppermute(flux_y, ALL, route)
    from_c = lax.all_gather(flux_c, "c", axis=0)
    fields, kept, sent = call(
        fluid_kernel,
        [((N_Y, OWN_BLOCKS, 64, 128), BF16), ((4, 2) + plane, F32), ((4, 2) + plane, F32)],
        [u_star, porosity, fpay, fpay_far, side, from_y, from_c],
        scratch=[
            pltpu.VMEM((3, 10) + plane, F32),
            pltpu.VMEM((10,) + plane, F32),
            pltpu.VMEM((4, 4) + plane, F32),
        ],
    )
    fields = lax.all_to_all(fields, "y", 0, 0)
    fields_c = swap(fields, "c")
    swapped = swap(sent, "c")
    (half,) = call(
        first_leave_kernel,
        [((64, 2 * MIG), F32)],
        [fields, fpay, fpay_far],
        flops=1 << 36,
    )
    out0, out1 = call(
        last_leave_kernel,
        [((5, MIG), F32), ((5, MIG), F32)],
        [fields_c, fpay, fpay_far, half],
    )
    arrive0 = lax.ppermute(out0, ALL, leave_route(-1))
    arrive1 = lax.ppermute(out1, ALL, leave_route(1))
    parcel_next, fluid_next, pressure_next = call(
        move_kernel,
        [((3, PCAP), F32), ((3, 2) + plane, F32), ((2,) + plane, F32)],
        [fields, fields_c, tiles_held, cell_held, keep, vel_held, rate_held, kept, swapped],
        scratch=[pltpu.SMEM((1, TILES), I32), pltpu.SemaphoreType.DMA((1,))],
        flops=1 << 31,
    )
    arrivals = jnp.stack([arrive0, arrive1], axis=1).transpose(1, 0, 2)
    return fluid_next, pressure_next, parcel_next, arrivals


def solution(mesh):
    fine = Mesh(mesh.devices.reshape(N_BLK, N_Y, N_Z, N_C), ALL)
    placed = (
        P(None, ALL, None, None),
        P(ALL, None, None),
        P(None, ALL),
        P(ALL),
        P(ALL),
        P(ALL),
        P(ALL),
        P(ALL),
        P(None, ALL),
        P(None, ALL),
    )
    return jax.shard_map(
        per_device,
        mesh=fine,
        in_specs=placed,
        out_specs=(
            P(None, ALL, None, None),
            P(ALL, None, None),
            P(None, ALL),
            P(None, None, ALL),
        ),
        check_vma=False,
    )
```

```python
import functools

import jax
import jax.numpy as jnp
from jax import lax
from jax.experimental import pallas as pl
from jax.experimental.pallas import tpu as pltpu
from jax.sharding import Mesh, PartitionSpec as P

PCAP = 8192
TP = 256
TILES = PCAP // TP
ROWS = PCAP // 128
BLOCK = 2048
RADIAL = 16
LINE = 256
MIG = 256
N_BLK, N_Y, N_Z, N_C = 32, 4, 2, 2
Z_LO = 8
ALL = ("blk", "y", "z", "c")

DT = 0.2
NU = 0.5

PAY_ROWS = 6 * ROWS + 16
SCR_ROWS = 7 * ROWS
SOURCES = N_Y * N_Z
OWN_BLOCKS = 8
UNROLL = 8
LIST_CAP = SOURCES * TILES + UNROLL

PACK_LIMIT = 56 << 20

F32 = jnp.float32
BF16 = jnp.bfloat16
I32 = jnp.int32


def flat(blk, y, z, c):
    return ((blk * N_Y + y) * N_Z + z) * N_C + c


def every_place():
    for blk in range(N_BLK):
        for y in range(N_Y):
            for z in range(N_Z):
                for c in range(N_C):
                    yield blk, y, z, c


def halo_route():
    pairs = []
    for blk, y, z, c in every_place():
        if c == 1:
            here = flat(blk, y, z, 1)
            if y < N_Y - 1:
                there = flat(blk, y + 1, z, 0)
            else:
                crossing = blk % Z_LO == Z_LO - 1
                there = flat((blk + 1) % N_BLK, 0, 1 - z if crossing else z, 0)
            pairs += [(here, there), (there, here)]
    return pairs


def leave_route(step):
    edge = 0 if step < 0 else Z_LO - 1
    pairs = []
    for blk, y, z, c in every_place():
        sender = flat(blk, y, 1 - z if blk % Z_LO == edge else z, c)
        pairs.append((sender, flat((blk + step) % N_BLK, y, z, c)))
    return pairs


def swap(values, axis):
    return lax.ppermute(values, axis, [(0, 1), (1, 0)])


def call(kernel, outs, ins, scratch=(), smem=(), hbm=(), limit=16 << 20, flops=0):
    def space(i):
        return pltpu.SMEM if i in smem else pltpu.HBM if i in hbm else pltpu.VMEM

    specs = [pl.BlockSpec(memory_space=space(i)) for i in range(len(ins))]
    return pl.pallas_call(
        kernel,
        out_shape=[jax.ShapeDtypeStruct(shape, dtype) for shape, dtype in outs],
        in_specs=specs,
        out_specs=[pl.BlockSpec(memory_space=pltpu.VMEM) for _ in outs],
        scratch_shapes=list(scratch),
        compiler_params=pltpu.CompilerParams(vmem_limit_bytes=limit),
        cost_estimate=pl.CostEstimate(flops=flops, bytes_accessed=1 << 20, transcendentals=0),
    )(*ins)


def rows_iota(rows, lanes):
    return lax.broadcasted_iota(I32, (rows, lanes), 0)


def dot_nt(a, b):
    return lax.dot_general(a, b, (((1,), (1,)), ((), ())), preferred_element_type=F32)


def dot_nn(a, b):
    return lax.dot_general(a, b, (((1,), (0,)), ((), ())), preferred_element_type=F32)


def hi_of(cell):
    return ((cell >> 7) & 1) * 8 + (cell >> 8)


def load_all(pairs, sems):
    copies = [pltpu.make_async_copy(a, b, sems.at[i]) for i, (a, b) in enumerate(pairs)]
    for copy in copies:
        copy.start()
    for copy in copies:
        copy.wait()


def fold_rows(vel, vsc):
    for r in range(ROWS):
        for k in range(3):
            vsc[k, r : r + 1, :] = vel[k : k + 1, r * 128 : (r + 1) * 128]


def active_slots(count):
    slot = rows_iota(ROWS, 128) * 128 + lax.broadcasted_iota(I32, (ROWS, 128), 1)
    return (slot < count[...]).astype(F32)


def pack_kernel(*refs):
    sources, pay, held, (vsc, tsc, sems) = refs[:6], refs[6], refs[7:13], refs[13:]
    vel, vol, rate, cell, tiles, count = held
    load_all(list(zip(sources, held)), sems)
    fold_rows(vel, vsc)
    active = active_slots(count)
    drag = vol[...] * rate[...]
    pay[0:ROWS, :] = (vol[...] * active).astype(BF16)
    pay[ROWS : 2 * ROWS, :] = (drag * active).astype(BF16)
    for k in range(3):
        pay[(2 + k) * ROWS : (3 + k) * ROWS, :] = (drag * vsc[k] * active).astype(BF16)
    cells = cell[...]
    hi = hi_of(cells)
    code = ((cells & 127) + 128).astype(F32)
    for bit in range(4):
        code = code * jnp.where((hi >> bit) & 1 == 1, F32(2.0 ** (1 << bit)), F32(1.0))
    pay[5 * ROWS : 6 * ROWS, :] = code.astype(BF16)
    lane = lax.broadcasted_iota(I32, (1, TILES), 1)
    tsc[...] = jnp.zeros((16, 128), F32)
    tsc[0:1, 0:TILES] = jnp.where(lane * TP < count[...], tiles[...].astype(F32), 255.0)
    pay[6 * ROWS : 6 * ROWS + 16, :] = tsc[...].astype(BF16)


def place_rows():
    return rows_iota(RADIAL, LINE) % 8 == 5


def fixed_point(values, places=False):
    scale = jnp.where(place_rows(), F32(1.0), F32(2.0**20)) if places else F32(2.0**20)
    return jnp.floor(values * scale + 0.5).astype(I32)


def from_fixed_point(code, places=False):
    scale = jnp.where(place_rows(), F32(1.0), F32(2.0**-20)) if places else F32(2.0**-20)
    return code.astype(F32) * scale


def leaver_kernel(*refs):
    sources, (fpay, keep, coded), held, (vsc, tsc, sems) = refs[:10], refs[10:13], refs[13:21], refs[21:]
    vel, vol, rate, cell, tiles, count, lists, mig = held
    fluid, press = sources[8:]
    pairs = list(zip(sources[:8], held))
    pairs += [(fluid.at[k], fpay.at[2 * k : 2 * k + 2]) for k in range(3)] + [(press, fpay.at[6:8])]
    load_all(pairs, sems)
    fold_rows(vel, vsc)
    cells = cell[...]
    tsc[...] = jnp.zeros((16, 128), F32)
    tsc[0:1, 0:TILES] = tiles[...].astype(F32)
    raw_tiles = tsc[...].astype(BF16)
    slots = jnp.concatenate([lists[0:1, :], lists[1:2, :]], axis=1)
    lane512 = lax.broadcasted_iota(I32, (1, 2 * MIG), 1)
    ends = jnp.where(lane512 < MIG, mig[:, 0:1], mig[:, 1:2] + MIG)
    valid = jnp.where(lane512 < ends, F32(1.0), F32(0.0))
    low = (rows_iota(128, 2 * MIG) == (slots & 127)).astype(F32).astype(BF16)
    row_mask = rows_iota(ROWS, 2 * MIG) == (slots >> 7)
    counts = dot_nt(jnp.where(row_mask, valid, 0.0).astype(BF16), low)
    keep[...] = active_slots(count) * jnp.where(counts > 0.5, 0.0, 1.0)

    def picked(values, parts):
        total = None
        for _ in range(parts):
            piece = values.astype(BF16)
            values = values - piece.astype(F32)
            term = dot_nn(piece, low)
            total = term if total is None else total + term
        return jnp.sum(jnp.where(row_mask, total, 0.0), axis=0, keepdims=True)

    def put(row, values):
        fpay[8, row : row + 1, :] = values[:, :MIG]
        fpay[8, 8 + row : 9 + row, :] = values[:, MIG:]

    for k in range(3):
        put(k, picked(vsc[k], 3))
    put(3, picked(vol[...], 3))
    put(4, picked(rate[...], 3))
    tile_hot = (rows_iota(128, 2 * MIG) == (slots >> 8)).astype(F32).astype(BF16)
    block = dot_nn(raw_tiles, tile_hot)[0:1, :]
    cell_hi = picked((cells >> 7).astype(F32), 1)
    cell_lo = picked((cells & 127).astype(F32), 1)
    put(5, block * BLOCK + cell_hi * 128.0 + cell_lo)
    put(6, valid)
    put(7, jnp.zeros_like(valid))
    codes = [fixed_point(fpay[p], places=p == 8) for p in range(9)]
    for p in range(9):
        coded[p] = (codes[p] >> 8).astype(jnp.int16)
    for j in range(5):
        shared = codes[2 * j] & 255
        if j < 4:
            shared = shared + (codes[2 * j + 1] & 255) * 256
        coded[9 + j] = (shared - 32768).astype(jnp.int16)


def edge_kernel(own, coded, edge, side, far):
    for p in range(9):
        shared = coded[9 + p // 2].astype(I32) + 32768
        low = shared >> 8 if p % 2 else shared & 255
        far[p] = from_fixed_point(coded[p].astype(I32) * 256 + low, places=p == 8)
    c = lax.axis_index("c")
    native = lax.axis_index("z") == c
    for k in range(4):
        edge[k] = jnp.where(native, own[2 * k + c], far[2 * k + c])
        for i in range(2):
            side[2 * k + i] = jnp.where(native, far[2 * k + i], own[2 * k + i])
    side[8] = jnp.where(native, own[7 - c], far[7 - c])


def at(values, axis, step):
    size = values.shape[axis]
    moved = pltpu.roll(values, (-step) % size, axis)
    place = lax.broadcasted_iota(I32, values.shape, axis)
    return jnp.where(place == (size - 1 if step > 0 else 0), 0.0, moved)


def rad_up(values):
    return at(values, values.ndim - 2, 1)


def rad_down(values):
    return at(values, values.ndim - 2, -1)


def axial_up(values):
    return at(values, values.ndim - 1, 1)


def axial_down(values):
    return at(values, values.ndim - 1, -1)


def add_deposits(pays, acc, scr, tile_v, tile_s, picks, sem, skip_own=False):
    y = lax.axis_index("y")
    first = y * 16 + lax.axis_index("c") * OWN_BLOCKS
    sources = pays.shape[0]
    for s in range(sources):
        tile_v[s : s + 1, :] = pays[s, 6 * ROWS : 6 * ROWS + 16, :].astype(F32)[0:1, :].astype(I32)
    copy = pltpu.make_async_copy(tile_v, tile_s, sem)
    copy.start()

    def widen(s, carry):
        base = pl.multiple_of(s * SCR_ROWS, 8)
        scr[pl.ds(base, 5 * ROWS), :] = pays[s, 0 : 5 * ROWS, :].astype(F32)
        code = pays[s, 5 * ROWS : 6 * ROWS, :].astype(F32)
        hi = jnp.zeros_like(code)
        for step in (8, 4, 2, 1):
            large = code >= 2.0 ** (7 + step)
            code = jnp.where(large, code * 2.0**-step, code)
            hi = hi + jnp.where(large, F32(step), 0.0)
        scr[pl.ds(base + 5 * ROWS, ROWS), :] = hi
        scr[pl.ds(base + 6 * ROWS, ROWS), :] = code - 128.0
        return carry

    lax.fori_loop(0, sources, widen, 0)
    copy.wait()

    def choose(s, found):
        base = first + jnp.where(s // N_Z == y, 1024, 0) if skip_own else first
        for t in range(TILES):
            block = tile_s[s, t] - base
            picks[found] = (s * SCR_ROWS + 2 * t) * 16 + block
            mine = jnp.logical_and(block >= 0, block < OWN_BLOCKS)
            found = found + mine.astype(I32)
        return found

    found = lax.fori_loop(0, sources, choose, jnp.int32(0))
    for i in range(UNROLL):
        picks[found + i] = OWN_BLOCKS
    iota16 = lax.broadcasted_iota(I32, (16, 128), 0).astype(F32)
    iota128 = lax.broadcasted_iota(I32, (128, 128), 0).astype(F32)

    def one_tile(code):
        block = code & 15
        base = code >> 4
        left, right = [], []
        for h in range(2):
            hi = scr[pl.ds(base + 5 * ROWS + h, 1), :]
            lo = scr[pl.ds(base + 6 * ROWS + h, 1), :]
            mask = iota16 == hi
            parts = [
                jnp.where(mask, scr[pl.ds(base + k * ROWS + h, 1), :], 0.0).astype(BF16)
                for k in range(5)
            ]
            left.append(jnp.concatenate(parts, axis=0))
            right.append(jnp.where(iota128 == lo, F32(1.0), F32(0.0)).astype(BF16))
        sums = dot_nt(jnp.concatenate(left, axis=1), jnp.concatenate(right, axis=1))
        return block, sums

    def deposit(i, carry):
        done = [one_tile(picks[i * UNROLL + u]) for u in range(UNROLL)]
        for block, sums in done:
            acc[block] = acc[block] + sums
        return carry

    lax.fori_loop(0, (found + UNROLL - 1) // UNROLL, deposit, 0)


def first_deposit_kernel(own, away, *refs):
    given, (acc, *kept), (pays, *scratch) = refs[:5], refs[5:11], refs[11:]
    pays[0] = own[...]
    pays[1] = away[...]
    for source, target in zip(given, kept):
        target[...] = source[...]
    acc[...] = jnp.zeros_like(acc)
    add_deposits(pays, acc, *scratch)


def next_deposit_kernel(skip_own, pays, before, acc, *scratch):
    acc[...] = before[...]
    add_deposits(pays, acc, *scratch, skip_own=skip_own)


def spread_kernel(own, far, out):
    for y in range(N_Y):
        out[y, 0] = own[...]
        out[y, 1] = far[...]


def velocity_kernel(acc, own, far, side, edge, u_out, por_out, flux_y, flux_c, wide, flux):
    c = lax.axis_index("c")
    native = lax.axis_index("z") == c

    def amount(k):
        halves = []
        for b in range(OWN_BLOCKS):
            halves.append(
                jnp.concatenate([acc[b, k * 16 : k * 16 + 8, :], acc[b, k * 16 + 8 : k * 16 + 16, :]], axis=1)
            )
        return jnp.stack(
            [jnp.concatenate([halves[2 * i], halves[2 * i + 1]], axis=0) for i in range(4)]
        )

    for k in range(4):
        wide[k, 5 * c] = edge[k]
        for i in range(2):
            wide[k, 1 + 2 * c + i] = jnp.where(native, own[2 * k + i], far[2 * k + i])
            wide[k, 3 - 2 * c + i] = side[2 * k + i]
        wide[k, 5 * (1 - c)] = jnp.where(native, far[2 * k + c], own[2 * k + c])
    porosity = 1.0 / (1.0 + amount(0))
    por_out[...] = porosity
    below = 1.0 + DT * amount(1) / porosity
    centre = wide[3, 1:5]
    slopes = [
        0.5 * (wide[3, 2:6] - wide[3, 0:4]),
        0.5 * (rad_up(centre) - rad_down(centre)),
        0.5 * (axial_up(centre) - axial_down(centre)),
    ]
    for k in range(3):
        v = wide[k, 1:5]
        lap = (
            wide[k, 2:6] + wide[k, 0:4] + rad_up(v) + rad_down(v) + axial_up(v) + axial_down(v) - 6.0 * v
        )
        u = (v + DT * (NU * lap - slopes[k]) + DT * amount(2 + k) / porosity) / below
        u_out[k] = u
        flux[k] = porosity * u
    for i in range(3):
        for k in range(3):
            flux_y[3 * k + i] = flux[k, c + i]
            flux_c[3 * k + i] = flux[k, 1 - c + i]
        flux_y[9 + i] = wide[3, 1 + c + i]


def fluid_kernel(
    u_in, por_in, own, far, side, from_y, from_c, fields, kept, sent, flux, pres, out
):
    c = lax.axis_index("c")
    native = lax.axis_index("z") == c
    for k in range(3):
        flux[k, 3:7] = por_in[...] * u_in[k]
        for i in range(3):
            flux[k, 7 * c + i] = from_y[3 * k + i]
            flux[k, 7 * (1 - c) + i] = from_c[1 - c, 3 * k + i]
    for i in range(3):
        pres[7 * c + i] = from_y[9 + i]
    for i in range(2):
        pres[3 + 2 * c + i] = jnp.where(native, own[6 + i], far[6 + i])
        pres[5 - 2 * c + i] = side[6 + i]
        pres[7 - 6 * c + i] = jnp.where(native, far[6 + i], own[6 + i])
    pres[9 * (1 - c)] = side[8]
    f1 = flux[1, 1:9]
    f2 = flux[2, 1:9]
    source = 0.5 * (
        flux[0, 2:10] - flux[0, 0:8] + rad_up(f1) - rad_down(f1) + axial_up(f2) - axial_down(f2)
    )

    def sweep(p, s):
        centre = p[1:-1]
        return (
            p[2:]
            + p[:-2]
            + rad_up(centre)
            + rad_down(centre)
            + axial_up(centre)
            + axial_down(centre)
            - s / DT
        ) / 6.0

    p1 = sweep(pres[...], source)
    p2 = sweep(p1, source[1:-1])
    centre = p2[1:-1]
    slopes = [
        0.5 * (p2[2:] - p2[:-2]),
        0.5 * (rad_up(centre) - rad_down(centre)),
        0.5 * (axial_up(centre) - axial_down(centre)),
    ]
    for k in range(3):
        out[k] = u_in[k] - DT * slopes[k]
    out[3] = centre
    for k in range(4):
        for i in range(4):
            plane = out[k, i] if k < 3 else por_in[i]
            for h in range(2):
                half = plane[8 * h : 8 * h + 8]
                both = jnp.concatenate([half[:, :128], half[:, 128:]], axis=0)
                for copy in range(N_Y):
                    fields[copy, 2 * i + h, 16 * k : 16 * k + 16, :] = both.astype(BF16)
    for k in range(4):
        for i in range(2):
            kept[k, i] = out[k, 2 * c + i]
            sent[k, i] = out[k, 2 * (1 - c) + i]


def step_parcel(vel, rate, sampled):
    coupling = rate / (sampled[3] * sampled[3])
    pull = DT * coupling
    below = 1.0 + pull
    return [(vel[k] + pull * sampled[k]) / below for k in range(3)]


def leave_lists_of(own, far):
    z_lo = lax.rem(lax.axis_index("blk"), Z_LO)
    list0 = jnp.where(z_lo == 0, far[8, 0:8, :], own[8, 0:8, :])
    list1 = jnp.where(z_lo == Z_LO - 1, far[8, 8:16, :], own[8, 8:16, :])
    return jnp.concatenate([list0, list1], axis=1)


def sample_lists(fields, core, both, total):
    place = both[5:6, :].astype(I32)
    block = place >> 11
    low = (rows_iota(128, 2 * MIG) == (place & 127)).astype(F32).astype(BF16)

    def gather(i, total):
        for u in range(OWN_BLOCKS):
            picked = dot_nn(fields[i, u], low)
            total = total + jnp.where(block == i * 16 + core * OWN_BLOCKS + u, picked, 0.0)
        return total

    return lax.fori_loop(0, N_Y, gather, total)


def first_leave_kernel(near, own, far, out):
    start = jnp.zeros((64, 2 * MIG), F32)
    out[...] = sample_lists(near, lax.axis_index("c"), leave_lists_of(own, far), start)


def last_leave_kernel(other, own, far, half, out0, out1):
    both = leave_lists_of(own, far)
    total = sample_lists(other, 1 - lax.axis_index("c"), both, half[...])
    mask = rows_iota(16, 2 * MIG) == hi_of(both[5:6, :].astype(I32) & (BLOCK - 1))
    sampled = [
        jnp.sum(jnp.where(mask, total[16 * k : 16 * k + 16], 0.0), axis=0, keepdims=True)
        for k in range(4)
    ]
    sampled[3] = jnp.where(both[6:7, :] > 0.5, sampled[3], 1.0)
    vol, rate, valid = both[3:4, :], both[4:5, :], both[6:7, :]
    moved = step_parcel([both[k : k + 1, :] for k in range(3)], rate, sampled)
    for k, values in enumerate(moved + [vol, rate]):
        values = values * valid
        out0[k : k + 1, :] = values[:, :MIG]
        out1[k : k + 1, :] = values[:, MIG:]


def move_kernel(
    near, other, tiles_in, cell, keep, vel, rate, kept, swapped, out, fluid, press, *scratch
):
    tiles, sems = scratch
    load_all([(tiles_in, tiles)], sems)
    c = lax.axis_index("c")
    iota16 = rows_iota(16, TP)
    iota128 = rows_iota(128, TP)

    def pair(ref, t):
        return jnp.concatenate([ref[pl.ds(2 * t, 1), :], ref[pl.ds(2 * t + 1, 1), :]], axis=1)

    def one_tile(t):
        block = tiles[0, t]
        row, col = block >> 4, block & 7
        here = jnp.where((block >> 3) & 1 == c, near[row, col], other[row, col])
        cells = pair(cell, t)
        low = jnp.where(iota128 == (cells & 127), F32(1.0), F32(0.0)).astype(BF16)
        picked = dot_nn(here, low)
        mask = iota16 == hi_of(cells)
        sampled = [
            jnp.sum(jnp.where(mask, picked[16 * k : 16 * k + 16], 0.0), axis=0, keepdims=True)
            for k in range(4)
        ]
        lanes = pl.ds(pl.multiple_of(t * TP, TP), TP)
        moved = step_parcel([vel[k : k + 1, lanes] for k in range(3)], pair(rate, t), sampled)
        stays = pair(keep, t)
        for k in range(3):
            out[k : k + 1, lanes] = moved[k] * stays

    def some(i, carry):
        for u in range(4):
            one_tile(i * 4 + u)
        return carry

    lax.fori_loop(0, TILES // 4, some, 0)
    mine = lax.axis_index("z") == c
    for k in range(3):
        fluid[k] = jnp.where(mine, kept[k], swapped[k])
    press[...] = jnp.where(mine, kept[3], swapped[3])


def join_kernel(first, second, out):
    for k in range(5):
        out[k, 0:1, :] = first[k : k + 1, :]
        out[k, 1:2, :] = second[k : k + 1, :]


def per_device(
    fluid_vel,
    pressure,
    parcel_vel,
    parcel_vol,
    parcel_rate,
    cell_local,
    tile_block,
    parcel_count,
    leave_lists,
    mig_counts,
):
    vol = parcel_vol.reshape(ROWS, 128)
    rate = parcel_rate.reshape(ROWS, 128)
    cell = cell_local.reshape(ROWS, 128)
    tiles = tile_block.reshape(1, TILES)
    plane = (RADIAL, LINE)
    parcels = [parcel_vel, vol, rate, cell, tiles, parcel_count.reshape(1, 1)]
    held = [
        pltpu.VMEM((3, PCAP), F32),
        pltpu.VMEM((ROWS, 128), F32),
        pltpu.VMEM((ROWS, 128), F32),
        pltpu.VMEM((ROWS, 128), I32),
        pltpu.VMEM((1, TILES), I32),
        pltpu.VMEM((1, 1), I32),
    ]
    folded = [pltpu.VMEM((3, ROWS, 128), F32), pltpu.VMEM((16, 128), F32)]
    (pay,) = call(
        pack_kernel,
        [((PAY_ROWS, 128), BF16)],
        parcels,
        scratch=held + folded + [pltpu.SemaphoreType.DMA((6,))],
        hbm=range(6),
        limit=PACK_LIMIT,
    )
    fpay, keep, coded = call(
        leaver_kernel,
        [((9,) + plane, F32), ((ROWS, 128), F32), ((14,) + plane, jnp.int16)],
        parcels + [leave_lists, mig_counts.reshape(1, 2), fluid_vel, pressure],
        scratch=held
        + [pltpu.VMEM((2, MIG), I32), pltpu.VMEM((1, 2), I32)]
        + folded
        + [pltpu.SemaphoreType.DMA((12,))],
        hbm=range(10),
        limit=PACK_LIMIT,
    )
    pay_far = swap(pay, "z")
    coded_far = swap(coded, "z")
    (pays,) = call(
        spread_kernel,
        [((N_Y, N_Z, PAY_ROWS, 128), BF16)],
        [pay, pay_far],
    )
    pays = lax.all_to_all(pays, "y", 0, 0)
    deposit_scratch = [
        pltpu.VMEM((SOURCES * SCR_ROWS, 128), F32),
        pltpu.VMEM((SOURCES, 128), I32),
        pltpu.SMEM((SOURCES, 128), I32),
        pltpu.SMEM((LIST_CAP,), I32),
        pltpu.SemaphoreType.DMA,
    ]
    sums_shape = (OWN_BLOCKS + 1, 80, 128)
    sums, keep, vel_held, rate_held, cell_held, tiles_held = call(
        first_deposit_kernel,
        [
            (sums_shape, F32),
            ((ROWS, 128), F32),
            ((3, PCAP), F32),
            ((ROWS, 128), F32),
            ((ROWS, 128), I32),
            ((1, TILES), I32),
        ],
        [pay, pay_far, keep, parcel_vel, rate, cell, tiles],
        scratch=[pltpu.VMEM((N_Z, PAY_ROWS, 128), BF16)] + deposit_scratch,
        flops=1 << 36,
    )
    (sums,) = call(
        functools.partial(next_deposit_kernel, True),
        [(sums_shape, F32)],
        [pays.reshape(SOURCES, PAY_ROWS, 128), sums],
        scratch=deposit_scratch,
        flops=1 << 36,
    )
    pays_c = swap(pays, "c")
    edge, side, fpay_far = call(
        edge_kernel,
        [((4,) + plane, F32), ((9,) + plane, F32), ((9,) + plane, F32)],
        [fpay, coded_far],
    )
    route = halo_route()
    side = swap(side, "c")
    edge = lax.ppermute(edge, ALL, route)
    (sums,) = call(
        functools.partial(next_deposit_kernel, False),
        [(sums_shape, F32)],
        [pays_c.reshape(SOURCES, PAY_ROWS, 128), sums],
        scratch=deposit_scratch,
        flops=1 << 36,
    )
    u_star, porosity, flux_y, flux_c = call(
        velocity_kernel,
        [((3, 4) + plane, F32), ((4,) + plane, F32), ((12,) + plane, F32), ((9,) + plane, F32)],
        [sums, fpay, fpay_far, side, edge],
        scratch=[pltpu.VMEM((4, 6) + plane, F32), pltpu.VMEM((3, 4) + plane, F32)],
    )
    from_y = lax.ppermute(flux_y, ALL, route)
    from_c = lax.all_gather(flux_c, "c", axis=0)
    fields, kept, sent = call(
        fluid_kernel,
        [((N_Y, OWN_BLOCKS, 64, 128), BF16), ((4, 2) + plane, F32), ((4, 2) + plane, F32)],
        [u_star, porosity, fpay, fpay_far, side, from_y, from_c],
        scratch=[
            pltpu.VMEM((3, 10) + plane, F32),
            pltpu.VMEM((10,) + plane, F32),
            pltpu.VMEM((4, 4) + plane, F32),
        ],
    )
    fields = lax.all_to_all(fields, "y", 0, 0)
    fields_c = swap(fields, "c")
    swapped = swap(sent, "c")
    (half,) = call(
        first_leave_kernel,
        [((64, 2 * MIG), F32)],
        [fields, fpay, fpay_far],
        flops=1 << 36,
    )
    out0, out1 = call(
        last_leave_kernel,
        [((5, MIG), F32), ((5, MIG), F32)],
        [fields_c, fpay, fpay_far, half],
    )
    arrive0 = lax.ppermute(out0, ALL, leave_route(-1))
    arrive1 = lax.ppermute(out1, ALL, leave_route(1))
    parcel_next, fluid_next, pressure_next = call(
        move_kernel,
        [((3, PCAP), F32), ((3, 2) + plane, F32), ((2,) + plane, F32)],
        [fields, fields_c, tiles_held, cell_held, keep, vel_held, rate_held, kept, swapped],
        scratch=[pltpu.SMEM((1, TILES), I32), pltpu.SemaphoreType.DMA((1,))],
        flops=1 << 31,
    )
    (arrivals,) = call(join_kernel, [((5, 2, MIG), F32)], [arrive0, arrive1])
    return fluid_next, pressure_next, parcel_next, arrivals.transpose(1, 0, 2)


def solution(mesh):
    fine = Mesh(mesh.devices.reshape(N_BLK, N_Y, N_Z, N_C), ALL)
    placed = (
        P(None, ALL, None, None),
        P(ALL, None, None),
        P(None, ALL),
        P(ALL),
        P(ALL),
        P(ALL),
        P(ALL),
        P(ALL),
        P(None, ALL),
        P(None, ALL),
    )
    return jax.shard_map(
        per_device,
        mesh=fine,
        in_specs=placed,
        out_specs=(
            P(None, ALL, None, None),
            P(ALL, None, None),
            P(None, ALL),
            P(None, None, ALL),
        ),
        check_vma=False,
    )
```
